256 devices in a mesh: dp: 8 (over x_lo, y), tm: 32 (over x_hi, z, core).
Axes of the slice: x: 4 (x_hi: 2, x_lo: 2; x = x_hi * 2 + x_lo), y: 4, z: 8, core: 2. Of those that a mesh axis runs over, the one named last changes fastest.
Arguments:
- video_clips: bfloat16 [8, 128, 4, 24, 1024], P('dp', 'tm'), may hold values from -6 to 6
- kernel: bfloat16 [3, 3, 3, 1024, 1024], P(None, None, None, 'tm', 'dp'), may hold values from -0.0390625 to 0.0390625
- conv_bias: float32 [1024], P('dp'), may hold values from -3 to 3
- cotangent: bfloat16 [8, 64, 2, 12, 1024], P(None, 'tm', None, None, 'dp'), may hold values from -6 to 6
Outputs:
- sampled: bfloat16 [8, 64, 2, 12, 1024], P(None, 'tm', None, None, 'dp')
- clip_grad: bfloat16 [8, 128, 4, 24, 1024], P('dp', 'tm')
- kernel_grad: float32 [3, 3, 3, 1024, 1024], P(None, None, None, 'tm', 'dp')
- bias_grad: float32 [1024], P('dp')
The draws below stay inside these ranges and needn't reach their ends.
All inputs are finite; a program needn't handle non-finite values.
Results may differ from the reference program's by a relative error of at most 0.019.
Values may be sent and summed in bfloat16 or wider, within the bound.
A program may use at most 192 MiB of HBM per device.

```python
import math
import jax
import jax.numpy as jnp
from jax import lax

C = 1024
ROWS = 4
COLS = 24
VIDEOS = 8
FRAMES = 128
N_DP = 8
N_TM = 32


def with_spikes(array, own_key, source, target, shards_of, factor):
    def block_of(dim):
        return (jnp.arange(array.shape[dim]) // (array.shape[dim] // shards_of)).reshape((-1,) + (1,) * (array.ndim - 1 - dim))

    near = jax.random.permutation(own_key, shards_of)[block_of(target)]
    other_side = (block_of(target) + shards_of // 2) % shards_of
    return jnp.where((block_of(source) == near) | (block_of(source) == other_side), factor * array, array)


def block_scale(key, dims, split, least, high):
    gain, own = 1.0, jax.random.fold_in(key, 6)
    for dim, parts in split:
        steps = jnp.exp(jax.random.uniform(jax.random.fold_in(own, dim), (parts,), jnp.float32, least / len(split), high / len(split)))
        gain = gain * jnp.repeat(steps, dims[dim] // parts).reshape([-1 if axis == dim else 1 for axis in range(len(dims))])
    return gain


def normal_values(rng, shape, deviation, limit, pieces=(), held_as=jnp.bfloat16):
    values = deviation * jax.random.normal(rng, shape, jnp.float32)
    if pieces:
        values = values * block_scale(rng, shape, pieces, -0.22, 0.18)
    return jnp.clip(values, -limit, limit).astype(held_as)


def gaussian_with(stream_key, extent, deviation, limit, pieces, heavy, dtype=jnp.bfloat16):
    array = deviation * jax.random.normal(stream_key, extent, jnp.float32)
    if pieces:
        array = array * block_scale(stream_key, extent, pieces, -0.22, 0.18)
    return jnp.clip(with_spikes(array, jax.random.fold_in(stream_key, 3), *heavy), -limit, limit).astype(dtype)


def setup_inputs(seed: int = 0) -> dict:
    key_list = jax.random.split(jax.random.key(seed), 5)
    video_clips = gaussian_with(key_list[0], (VIDEOS, FRAMES, ROWS, COLS, C), 1.0, 6.0, ((0, 8), (1, 32)), (1, 4, 32, 2.75))
    kernel = normal_values(key_list[1], (3, 3, 3, C, C), (27 * C) ** -0.5, 0.0390625, ((3, 32), (4, 8)))
    conv_bias = normal_values(key_list[2], (C,), 0.5, 3.0, ((0, 8),), jnp.float32)
    cotangent = normal_values(key_list[3], (VIDEOS, FRAMES // 2, ROWS // 2, COLS // 2, C), 1.0, 6.0, ((1, 32), (4, 8)))
    return {"video_clips": video_clips, "kernel": kernel, "conv_bias": conv_bias, "cotangent": cotangent}


tap_list = [(t_tap, h_tap, w_tap) for t_tap in range(3) for h_tap in range(3) for w_tap in range(3)]

def choose_line(values_in, tap_index, dim_index):
    length = values_in.shape[dim_index]
    even_part = lax.slice_in_dim(values_in, 0, length, 2, dim_index)
    odd_part = lax.slice_in_dim(values_in, 1, length, 2, dim_index)
    if tap_index == 1:
        return even_part
    if tap_index == 2:
        return odd_part
    leading = lax.slice_in_dim(odd_part, 0, odd_part.shape[dim_index] - 1, 1, dim_index)
    zero_line = jnp.zeros_like(lax.slice_in_dim(odd_part, 0, 1, 1, dim_index))
    return jnp.concatenate([zero_line, leading], axis=dim_index)

def tap_view(frames, rim_frame, t_tap, h_tap, w_tap):
    if t_tap == 1:
        picked = frames[:, 0::2]
    elif t_tap == 2:
        picked = frames[:, 1::2]
    else:
        picked = jnp.concatenate([rim_frame, frames[:, 1::2][:, :-1]], axis=1)
    return choose_line(choose_line(picked, h_tap, 2), w_tap, 3)

def conv_forward(frames, rim_frame, weights):
    channels = frames.shape[-1]
    result = None
    for t_tap, h_tap, w_tap in tap_list:
        tap_rows = tap_view(frames, rim_frame, t_tap, h_tap, w_tap)
        product = jnp.dot(tap_rows.reshape(-1, channels), weights[t_tap, h_tap, w_tap], preferred_element_type=jnp.float32)
        result = product if result is None else result + product
    return result.reshape(tap_rows.shape[:-1] + (weights.shape[-1],))

def lift(values_in, dim_index):
    length = values_in.shape[dim_index]
    rest_part = lax.slice_in_dim(values_in, 1, length, 1, dim_index)
    zero_line = jnp.zeros_like(lax.slice_in_dim(values_in, 0, 1, 1, dim_index))
    return jnp.concatenate([rest_part, zero_line], axis=dim_index)

def spread_back(grad_bf, weights, t_tap):
    leading_dims = grad_bf.shape[:-1]
    rows_in = grad_bf.reshape(-1, grad_bf.shape[-1])
    pieces_map = {}
    for h_tap in range(3):
        for w_tap in range(3):
            product = lax.dot_general(rows_in, weights[t_tap, h_tap, w_tap], (((1,), (1,)), ((), ())), preferred_element_type=jnp.float32)
            pieces_map[h_tap, w_tap] = product.reshape(leading_dims + (weights.shape[3],))
    even_even = pieces_map[1, 1]
    even_odd = pieces_map[1, 2] + lift(pieces_map[1, 0], 3)
    odd_even = pieces_map[2, 1] + lift(pieces_map[0, 1], 2)
    odd_odd = pieces_map[2, 2] + lift(pieces_map[2, 0], 3) + lift(pieces_map[0, 2], 2) + lift(lift(pieces_map[0, 0], 2), 3)
    even_rows = jnp.stack([even_even, even_odd], axis=4)
    odd_rows = jnp.stack([odd_even, odd_odd], axis=4)
    joined = jnp.stack([even_rows, odd_rows], axis=3)
    dims_out = joined.shape
    return joined.reshape(dims_out[0], dims_out[1], dims_out[2] * 2, dims_out[4] * 2, dims_out[6])

def spread_frames(grad_bf, weights):
    start_part = spread_back(grad_bf, weights, 0)
    even_frames = spread_back(grad_bf, weights, 1)
    odd_frames = spread_back(grad_bf, weights, 2) + lift(start_part, 1)
    woven = jnp.stack([even_frames, odd_frames], axis=2)
    dims_out = woven.shape
    woven = woven.reshape((dims_out[0], dims_out[1] * 2) + dims_out[3:])
    return jnp.concatenate([woven, start_part[:, :1]], axis=1)

def reference(video_clips, kernel, conv_bias, cotangent):
    videos, frames_all, rows_all, cols_all, channels = video_clips.shape
    blocks = N_TM
    per_block = frames_all // blocks
    blocked = video_clips.reshape(videos, blocks, per_block, rows_all, cols_all, channels)
    last_frames = blocked[:, :, per_block - 1:]
    rim_frames = jnp.concatenate([jnp.zeros_like(last_frames[:, :1]), last_frames[:, :-1]], axis=1)
    flat_frames = blocked.reshape(videos * blocks, per_block, rows_all, cols_all, channels)
    flat_rims = rim_frames.reshape(videos * blocks, 1, rows_all, cols_all, channels)
    pre_act = conv_forward(flat_frames, flat_rims, kernel) + conv_bias
    sigmoid_val = jax.nn.sigmoid(pre_act)
    out_dims = (videos, frames_all // 2, rows_all // 2, cols_all // 2, channels)
    sampled = (pre_act * sigmoid_val).astype(jnp.bfloat16).reshape(out_dims)
    slope_grad = cotangent.astype(jnp.float32).reshape(pre_act.shape) * sigmoid_val * (1.0 + pre_act * (1.0 - sigmoid_val))
    grad_bf = slope_grad.astype(jnp.bfloat16)
    positions = videos * (frames_all // 2) * (rows_all // 2) * (cols_all // 2)
    inv_scale = 1.0 / math.sqrt(positions)
    bias_grad = lax.optimization_barrier(jnp.sum(slope_grad, axis=(0, 1, 2, 3))) * inv_scale
    share_width = channels // N_DP
    summed = None
    for column in range(N_DP):
        lower = column * share_width
        term_value = spread_frames(grad_bf[..., lower:lower + share_width], kernel[..., lower:lower + share_width])
        rounded = lax.optimization_barrier(term_value.astype(jnp.bfloat16)).astype(jnp.float32)
        summed = rounded if summed is None else summed + rounded
    summed = summed.reshape(videos, blocks, per_block + 1, rows_all, cols_all, channels)
    main_part = summed[:, :, :per_block]
    head_part = summed[:, :, per_block:]
    carried = jnp.concatenate([head_part[:, 1:], jnp.zeros_like(head_part[:, :1])], axis=1)
    main_part = jnp.concatenate([main_part[:, :, :per_block - 1], main_part[:, :, per_block - 1:] + carried], axis=2)
    clip_grad = main_part.reshape(video_clips.shape).astype(jnp.bfloat16)
    right_rows = grad_bf.reshape(videos, blocks, -1, channels).astype(jnp.float32)
    scaled_terms = []
    for t_tap, h_tap, w_tap in tap_list:
        tap_rows = tap_view(flat_frames, flat_rims, t_tap, h_tap, w_tap)
        left_rows = tap_rows.reshape(videos, blocks, -1, channels).astype(jnp.float32)
        block_sums = jnp.einsum('vtmc,vtmd->tcd', left_rows, right_rows, precision=lax.Precision.HIGHEST) * inv_scale
        rounded = lax.optimization_barrier(block_sums.astype(jnp.bfloat16)).astype(jnp.float32)
        scaled_terms.append(lax.optimization_barrier(jnp.sum(rounded, axis=0)))
    kernel_grad = jnp.stack(scaled_terms).reshape(3, 3, 3, channels, channels)
    return (sampled, clip_grad, kernel_grad, bias_grad)
```

```python
import math

import jax
import jax.numpy as jnp
import numpy as np
from jax import lax
from jax.experimental import pallas as pl
from jax.experimental.pallas import tpu as pltpu
from jax.sharding import PartitionSpec as P

MESH = pl.DeviceIdType.MESH
F32 = jnp.float32
BF16 = jnp.bfloat16
POSITIONS = 12288


def tap_gather():
    table = np.zeros((224, 96), np.float32)
    for h in range(3):
        for w in range(3):
            for r in range(2):
                for q in range(12):
                    row, col = 2 * r + h - 1, 2 * q + w - 1
                    if 0 <= row < 4 and 0 <= col < 24:
                        table[(h * 3 + w) * 24 + r * 12 + q, row * 24 + col] = 1.0
    return table


def kernel(
    x_ref, w_ref, cot_ref, bias_ref, gat_ref, sca_ref,
    samp_out, dx_out, dw_out, db_out,
    land, halo, wg, cotl, biasl, im_e, im_o, pacc, part, rsl, sbuf, sland, gbuf, ghalo, bz, bs, bl,
    d_e, d_o, dxb, dxp, dxs, dxl, dwb, dws, dwr, dwl, kout, dbo,
    x_send, x_recv, f_send, h_sem, w_send, w_recv, c_send, c_recv, b_send, b_recv, rs_send, rs_recv,
    s_send, s_recv, ag_send, ag_recv, bz_send, bz_recv, gh_sem, bs_send, bs_recv, dxp_send, dxp_recv,
    dx_send, dx_recv, k1_send, k1_recv, k2_send, k2_recv, o_sem,
):
    dp, tm = lax.axis_index("dp"), lax.axis_index("tm")
    xl, y = lax.div(dp, 4), lax.rem(dp, 4)
    xh, z, c = lax.div(tm, 16), lax.rem(lax.div(tm, 2), 8), lax.rem(tm, 2)
    primary = c == xl
    inv = 1.0 / math.sqrt(POSITIONS)

    def dev(xl_, y_, xh_, z_, c_):
        return (xl_ * 4 + y_, (xh_ * 8 + z_) * 2 + c_)

    def remote(src, dst, send, recv, device):
        return pltpu.make_async_remote_copy(
            src_ref=src, dst_ref=dst, send_sem=send, recv_sem=recv, device_id=device, device_id_type=MESH
        )

    def landed(dst, sem):
        pltpu.make_async_copy(dst, dst, sem).wait()

    def plus(a, by, n):
        return lax.rem(a + by, n)

    partner = dev(1 - xl, y, xh, z, c)
    sibling = dev(xl, y, xh, z, 1 - c)
    across = dev(xl, y, 1 - xh, z, c)

    barrier = pltpu.get_barrier_semaphore()
    peers = [partner]
    for dz in range(8):
        for dc in range(2):
            if dz or dc:
                peers.append(dev(xl, y, xh, plus(z, dz, 8), plus(c, dc, 2)))
    for dy in range(4):
        for dh in range(2):
            for dc in range(2):
                if dy or dh:
                    peers.append(dev(xl, plus(y, dy, 4), plus(xh, dh, 2), z, plus(c, dc, 2)))
    for peer in peers:
        pl.semaphore_signal(barrier, inc=1, device_id=peer, device_id_type=MESH)
    pl.semaphore_wait(barrier, len(peers))

    ends = []

    me_k = 2 * z + c
    for n, dz in enumerate((1, 7, 2, 6, 3, 5, 4)):
        zt = plus(z, dz, 8)
        copy = remote(x_ref.at[zt], land.at[me_k], x_send.at[n], x_recv.at[me_k], dev(xl, y, xh, zt, xl))
        copy.start()
        ends.append(copy.wait_send)
    own_x = pltpu.make_async_copy(x_ref.at[z], land.at[me_k], x_recv.at[me_k])
    sib_x = remote(x_ref.at[z], land.at[me_k], x_send.at[7], x_recv.at[me_k], dev(xl, y, xh, z, 1 - c))

    @pl.when(primary)
    def _():
        own_x.start()

    @pl.when(jnp.logical_not(primary))
    def _():
        sib_x.start()

    def w_at(h_, c_, y_):
        return wg.at[:, pl.ds(pl.multiple_of((h_ * 2 + c_) * 32, 32), 32), pl.ds(pl.multiple_of(y_ * 128, 128), 128)]

    def w_sem(h_, c_, y_):
        return w_recv.at[(h_ * 2 + c_) * 4 + y_]

    w_count = [0]

    def w_push(src, h_, c_, y_, device):
        copy = remote(src, w_at(h_, c_, y_), w_send.at[w_count[0]], w_sem(h_, c_, y_), device)
        w_count[0] += 1
        copy.start()
        ends.append(copy.wait_send)

    w_push(w_ref, xh, c, y, across)
    for dy in (1, 3, 2):
        w_push(w_ref, xh, c, y, dev(xl, plus(y, dy, 4), xh, z, c))
    w_push(w_ref, xh, c, y, sibling)
    pltpu.make_async_copy(w_ref, w_at(xh, c, y), w_sem(xh, c, y)).start()

    for dy in range(4):
        for dc in range(2):
            yd, cd = plus(y, dy, 4), plus(c, dc, 2)
            src, dst, sem = cot_ref.at[cd * 4 + yd], cotl.at[c, y], c_recv.at[c * 4 + y]
            if dy or dc:
                copy = remote(src, dst, c_send.at[dy * 2 + dc], sem, dev(xl, yd, xh, z, cd))
                copy.start()
                ends.append(copy.wait_send)
            else:
                pltpu.make_async_copy(src, dst, sem).start()
    pltpu.make_async_copy(bias_ref, biasl.at[y], b_recv.at[y]).start()
    for dy in range(1, 4):
        copy = remote(bias_ref, biasl.at[y], b_send.at[dy], b_recv.at[y], dev(xl, plus(y, dy, 4), xh, z, c))
        copy.start()
        ends.append(copy.wait_send)

    def spread(j, carry):
        dz = jnp.where(lax.rem(j, 2) == 1, lax.div(j + 1, 2), lax.rem(8 - lax.div(j, 2), 8))
        zs = plus(z, dz, 8)
        for cs in range(2):
            k = 2 * zs + cs
            landed(land.at[k], x_recv.at[k])

            @pl.when(primary)
            def _():
                remote(land.at[k], land.at[k], f_send.at[k], x_recv.at[k], partner).start()

        for cs in range(2):
            k = 2 * zs + cs
            frames = land[k]
            side = jnp.concatenate([frames[i * 96:(i + 1) * 96] for i in range(4)], axis=1)
            taps = jnp.dot(gat_ref[...], side, preferred_element_type=F32)
            for i in range(4):
                piece = taps[:216, i * 128:(i + 1) * 128].reshape(9, 24, 128)
                if i % 2 == 0:
                    im_e[:, 2 * k + i // 2] = piece
                else:
                    im_o[:, 2 * k + 1 + i // 2] = piece
        return carry

    lax.fori_loop(0, 2, spread, 0)
    landed(w_at(1 - xh, c, y), w_sem(1 - xh, c, y))
    for dy in (1, 3, 2):
        w_push(w_at(1 - xh, c, y), 1 - xh, c, y, dev(xl, plus(y, dy, 4), xh, z, c))
    w_push(w_at(1 - xh, c, y), 1 - xh, c, y, sibling)
    lax.fori_loop(2, 8, spread, 0)

    halo_copy = remote(land.at[15, pl.ds(288, 96)], halo, h_sem.at[0], h_sem.at[1], across)
    halo_copy.start()
    ends.append(halo_copy.wait_send)
    for dy in (1, 3, 2):
        for h_ in (xh, 1 - xh):
            yd = plus(y, dy, 4)
            landed(w_at(h_, c, yd), w_sem(h_, c, yd))
            w_push(w_at(h_, c, yd), h_, c, yd, sibling)
    landed(w_at(xh, c, y), w_sem(xh, c, y))
    for dy in range(4):
        for h_ in (xh, 1 - xh):
            yd = plus(y, dy, 4)
            landed(w_at(h_, 1 - c, yd), w_sem(h_, 1 - c, yd))

    def forward(half):
        base = 16 * half

        def step(h, carry):
            lhs, rhs = [], []
            for w in range(3):
                hw = h * 3 + w
                lhs.append(im_o[hw, pl.ds(base, 16)].reshape(384, 128).astype(BF16))
                lhs.append(im_e[hw, pl.ds(base, 16)].reshape(384, 128).astype(BF16))
                lhs.append(im_o[hw, pl.ds(base + 1, 16)].reshape(384, 128).astype(BF16))
                rhs += [wg[hw], wg[9 + hw], wg[18 + hw]]
            pacc[...] += jnp.dot(
                jnp.concatenate(lhs, axis=1), jnp.concatenate(rhs, axis=0), preferred_element_type=F32
            )
            return carry

        pacc[...] = jnp.zeros_like(pacc)
        lax.fori_loop(0, 3, step, 0)
        for q in range(4):
            zt = 4 * half + q
            part[zt] = pacc[q * 96:(q + 1) * 96].astype(BF16)
            copy = remote(part.at[zt], rsl.at[z], rs_send.at[zt], rs_recv.at[z], dev(xl, y, xh, zt, c))

            @pl.when(z != zt)
            def _(copy=copy):
                copy.start()

    forward(1)
    landed(halo, h_sem.at[1])
    rim = jnp.dot(gat_ref[...], halo[...], preferred_element_type=F32)[:216].reshape(9, 24, 128)
    im_o[:, 0] = jnp.where(xh == 1, rim, jnp.zeros_like(rim))
    forward(0)

    for dy in range(4):
        yd = plus(y, dy, 4)
        landed(biasl.at[yd], b_recv.at[yd])
        for cs in range(2):
            landed(cotl.at[cs, yd], c_recv.at[cs * 4 + yd])
    pre = part[z].astype(F32)
    for dz in (1, 7, 2, 6, 3, 5, 4):
        zs = plus(z, dz, 8)
        landed(rsl.at[zs], rs_recv.at[zs])
        pre = pre + rsl[zs].astype(F32)
    pre = pre + jnp.concatenate([biasl[i, 0:1] for i in range(4)], axis=1)
    sig = 1.0 / (1.0 + jnp.exp(-pre))
    samp = (pre * sig).astype(BF16)
    cot = jnp.concatenate(
        [jnp.concatenate([cotl[cs, i] for i in range(4)], axis=1) for cs in range(2)], axis=0
    ).astype(F32)
    slope = cot * sig * (1.0 + pre * (1.0 - sig))
    gbuf[z] = slope.astype(BF16)
    bz[z] = jnp.broadcast_to(jnp.sum(slope, axis=0, keepdims=True), (8, 512))
    for n, dz in enumerate((1, 7, 2, 6, 3, 5, 4)):
        zt = plus(z, dz, 8)
        copy = remote(gbuf.at[z], gbuf.at[z], ag_send.at[n], ag_recv.at[z], dev(xl, y, xh, zt, c))
        copy.start()
        ends.append(copy.wait_send)
        copy = remote(bz.at[z], bz.at[z], bz_send.at[n], bz_recv.at[z], dev(xl, y, xh, zt, c))
        copy.start()
        ends.append(copy.wait_send)
    for cs in range(2):
        for i in range(4):
            sbuf[cs, i] = samp[cs * 48:(cs + 1) * 48, i * 128:(i + 1) * 128]
    for dy in range(4):
        for dc in range(2):
            yd, cd = plus(y, dy, 4), plus(c, dc, 2)
            src, dst, sem = sbuf.at[cd, yd], sland.at[c * 4 + y], s_recv.at[c * 4 + y]
            if dy or dc:
                copy = remote(src, dst, s_send.at[dy * 2 + dc], sem, dev(xl, yd, xh, z, cd))
                copy.start()
                ends.append(copy.wait_send)
            else:
                pltpu.make_async_copy(src, dst, sem).start()
    for dz in (1, 7, 2, 6, 3, 5, 4):
        zs = plus(z, dz, 8)
        landed(gbuf.at[zs], ag_recv.at[zs])
    ghalo_copy = remote(gbuf.at[0, pl.ds(0, 32)], ghalo, gh_sem.at[0], gh_sem.at[1], across)
    ghalo_copy.start()
    ends.append(ghalo_copy.wait_send)

    def back(hw, carry):
        mats = jnp.concatenate([wg[hw], wg[9 + hw], wg[18 + hw]], axis=0)
        r = lax.dot_general(
            gbuf[...].reshape(768, 512), mats, (((1,), (1,)), ((), ())), preferred_element_type=F32
        )
        d_e[hw] = r[:, 128:256].reshape(32, 24, 128)
        d_o[hw, pl.ds(0, 31)] = (r[:744, 256:] + r[24:, :128]).reshape(31, 24, 128)
        d_o[hw, 31] = r[744:, 256:]
        return carry

    lax.fori_loop(0, 9, back, 0)
    landed(ghalo, gh_sem.at[1])

    def back_rim(hw, carry):
        r = lax.dot_general(ghalo[...], wg[hw], (((1,), (1,)), ((), ())), preferred_element_type=F32)
        d_o[hw, 31] += jnp.where(xh == 0, r[:24], jnp.zeros_like(r[:24]))
        return carry

    lax.fori_loop(0, 9, back_rim, 0)

    def gather_back(k, carry):
        cols = []
        for i in range(4):
            held = d_e if i % 2 == 0 else d_o
            cols.append(held[:, 2 * k + i // 2].reshape(216, 128))
        side = jnp.concatenate(cols, axis=1)
        side = jnp.concatenate([side, jnp.zeros((8, 512), F32)], axis=0).astype(BF16)
        r = jnp.dot(sca_ref[...], side, preferred_element_type=F32).astype(BF16)
        for i in range(4):
            dxb[k, pl.ds(i * 96, 96)] = r[:, i * 128:(i + 1) * 128]

        @pl.when(jnp.logical_not(primary))
        def _():
            remote(dxb.at[k], dxp.at[k], dxp_send.at[k], dxp_recv.at[k], partner).start()

        return carry

    lax.fori_loop(0, 16, gather_back, 0)

    def send_back(k, carry):
        landed(dxp.at[k], dxp_recv.at[k])
        dxs[k] = (dxb[k].astype(F32) + dxp[k].astype(F32)).astype(BF16)

        @pl.when(k == me_k)
        def _():
            pltpu.make_async_copy(dxs.at[k], dxl.at[z], dx_recv.at[z]).start()

        @pl.when(k != me_k)
        def _():
            remote(
                dxs.at[k], dxl.at[z], dx_send.at[k], dx_recv.at[z], dev(xl, y, xh, lax.div(k, 2), lax.rem(k, 2))
            ).start()

        return carry

    def some_back(first, last):
        @pl.when(primary)
        def _():
            lax.fori_loop(first, last, send_back, 0)

    for h in range(3):
        def grad_step(w, carry, h=h):
            hw = h * 3 + w
            lhs = jnp.concatenate(
                [
                    im_o[hw, pl.ds(0, 32)].reshape(768, 128).astype(BF16),
                    im_e[hw].reshape(768, 128).astype(BF16),
                    im_o[hw, pl.ds(1, 32)].reshape(768, 128).astype(BF16),
                ],
                axis=1,
            )
            r = lax.dot_general(
                lhs, gbuf[...].reshape(768, 512), (((0,), (0,)), ((), ())), preferred_element_type=F32
            ).astype(BF16)
            for t in range(3):
                for h_ in range(2):
                    for c_ in range(2):
                        at = t * 128 + h_ * 64 + c_ * 32
                        dwb[h, c_, h_, w * 3 + t] = r[at:at + 32]
            return carry

        lax.fori_loop(0, 3, grad_step, 0)
        copy = remote(dwb.at[h, 1 - c], dws.at[h], k1_send.at[h], k1_recv.at[h], sibling)
        copy.start()
        ends.append(copy.wait_send)
        some_back(4 * h, 4 * h + 4)

    for h in range(3):
        landed(dws.at[h], k1_recv.at[h])

        def add_step(n, carry, h=h):
            for h_ in range(2):
                dwr[h, h_, n] = (dwb[h, c, h_, n].astype(F32) + dws[h, h_, n].astype(F32)).astype(BF16)
            return carry

        lax.fori_loop(0, 9, add_step, 0)
        slot = xh * 4 + y
        for dh in range(2):
            for dy in range(4):
                yd, hd = plus(y, dy, 4), plus(xh, dh, 2)
                src = dwr.at[h, hd, :, :, pl.ds(pl.multiple_of(yd * 128, 128), 128)]
                dst, sem = dwl.at[h, slot], k2_recv.at[h * 8 + slot]
                if dh or dy:
                    copy = remote(src, dst, k2_send.at[h * 8 + dh * 4 + dy], sem, dev(xl, yd, hd, z, c))
                    copy.start()
                    ends.append(copy.wait_send)
                else:
                    pltpu.make_async_copy(src, dst, sem).start()
    some_back(12, 16)

    total = bz[z, 0:1]
    for dz in (1, 7, 2, 6, 3, 5, 4):
        zs = plus(z, dz, 8)
        landed(bz.at[zs], bz_recv.at[zs])
        total = total + bz[zs, 0:1]
    for i in range(4):
        bs[i] = jnp.broadcast_to(total[:, i * 128:(i + 1) * 128], (8, 128))
    slot_b = (xh * 2 + c) * 4 + y
    for dy in range(4):
        for dh in range(2):
            for dc in range(2):
                yd, hd, cd = plus(y, dy, 4), plus(xh, dh, 2), plus(c, dc, 2)
                if dy or dh or dc:
                    copy = remote(
                        bs.at[yd], bl.at[slot_b], bs_send.at[(dy * 2 + dh) * 2 + dc], bs_recv.at[slot_b],
                        dev(xl, yd, hd, z, cd),
                    )
                    copy.start()
                    ends.append(copy.wait_send)
                else:
                    pltpu.make_async_copy(bs.at[y], bl.at[slot_b], bs_recv.at[slot_b]).start()

    outs = []
    for i in range(8):
        landed(sland.at[i], s_recv.at[i])
    outs.append(pltpu.make_async_copy(sland, samp_out, o_sem.at[0]))
    outs[-1].start()

    for h in range(3):
        for i in range(8):
            landed(dwl.at[h, i], k2_recv.at[h * 8 + i])

        def sum_step(w, carry, h=h):
            for t in range(3):
                acc = dwl[h, 0, w * 3 + t].astype(F32)
                for i in range(1, 8):
                    acc = acc + dwl[h, i, w * 3 + t].astype(F32)
                kout[t * 9 + h * 3 + w] = acc * inv
            return carry

        lax.fori_loop(0, 3, sum_step, 0)
    outs.append(pltpu.make_async_copy(kout, dw_out, o_sem.at[1]))
    outs[-1].start()

    acc = None
    for i in range(16):
        landed(bl.at[i], bs_recv.at[i])
        acc = bl[i] if acc is None else acc + bl[i]
    dbo[...] = acc * inv
    outs.append(pltpu.make_async_copy(dbo, db_out, o_sem.at[2]))
    outs[-1].start()

    for i in range(8):
        landed(dxl.at[i], dx_recv.at[i])
    outs.append(pltpu.make_async_copy(dxl, dx_out, o_sem.at[3]))
    outs[-1].start()

    for end in ends:
        end()

    @pl.when(jnp.logical_not(primary))
    def _():
        sib_x.wait_send()

        def drain(k, carry):
            remote(dxb.at[k], dxp.at[k], dxp_send.at[k], dxp_recv.at[k], partner).wait_send()
            return carry

        lax.fori_loop(0, 16, drain, 0)

    @pl.when(primary)
    def _():
        def drain(k, carry):
            remote(land.at[k], land.at[k], f_send.at[k], x_recv.at[k], partner).wait_send()

            @pl.when(k != me_k)
            def _():
                remote(
                    dxs.at[k], dxl.at[z], dx_send.at[k], dx_recv.at[z],
                    dev(xl, y, xh, lax.div(k, 2), lax.rem(k, 2)),
                ).wait_send()

            return carry

        lax.fori_loop(0, 16, drain, 0)

    for zt in range(8):
        copy = remote(part.at[zt], rsl.at[z], rs_send.at[zt], rs_recv.at[z], dev(xl, y, xh, zt, c))

        @pl.when(z != zt)
        def _(copy=copy):
            copy.wait_send()

    for out in outs:
        out.wait()


def shards(video_clips, weights, conv_bias, cotangent):
    x = video_clips.reshape(384, 2, 8, 64).transpose(2, 0, 1, 3).reshape(8, 384, 128)
    w = weights.reshape(27, 32, 128)
    cot = cotangent.reshape(8, 48, 128)
    bias = jnp.broadcast_to(conv_bias.reshape(1, 128), (8, 128))
    table = tap_gather()
    gat = jnp.asarray(table, BF16)
    sca = jnp.asarray(table.T, BF16)
    any_spec = pl.BlockSpec(memory_space=pl.ANY)
    vmem_spec = pl.BlockSpec(memory_space=pltpu.VMEM)

    def v(shape, dtype=BF16):
        return pltpu.VMEM(shape, dtype)

    def sems(n):
        return pltpu.SemaphoreType.DMA((n,))

    samp, dx, dw, db = pl.pallas_call(
        kernel,
        out_shape=[
            jax.ShapeDtypeStruct((8, 48, 128), BF16),
            jax.ShapeDtypeStruct((8, 384, 128), BF16),
            jax.ShapeDtypeStruct((27, 32, 128), F32),
            jax.ShapeDtypeStruct((8, 128), F32),
        ],
        in_specs=[any_spec] * 4 + [vmem_spec] * 2,
        out_specs=[any_spec] * 4,
        scratch_shapes=[
            v((16, 384, 128)),
            v((96, 128)),
            v((27, 128, 512)),
            v((2, 4, 48, 128)),
            v((4, 8, 128), F32),
            v((9, 32, 24, 128), F32),
            v((9, 33, 24, 128), F32),
            v((384, 512), F32),
            v((8, 96, 512)),
            v((8, 96, 512)),
            v((2, 4, 48, 128)),
            v((8, 48, 128)),
            v((8, 96, 512)),
            v((32, 512)),
            v((8, 8, 512), F32),
            v((4, 8, 128), F32),
            v((16, 8, 128), F32),
            v((9, 32, 24, 128), F32),
            v((9, 32, 24, 128), F32),
            v((16, 384, 128)),
            v((16, 384, 128)),
            v((16, 384, 128)),
            v((8, 384, 128)),
            v((3, 2, 2, 9, 32, 512)),
            v((3, 2, 9, 32, 512)),
            v((3, 2, 9, 32, 512)),
            v((3, 8, 9, 32, 128)),
            v((27, 32, 128), F32),
            v((8, 128), F32),
            sems(8), sems(16), sems(16), sems(2),
            sems(16), sems(16), sems(8), sems(8), sems(4), sems(4),
            sems(8), sems(8), sems(8), sems(8), sems(8), sems(8), sems(8), sems(8),
            sems(2), sems(16), sems(16), sems(16), sems(16), sems(16), sems(8),
            sems(3), sems(3), sems(24), sems(24), sems(4),
        ],
        compiler_params=pltpu.CompilerParams(
            collective_id=0, has_side_effects=True, vmem_limit_bytes=60 * 1024 * 1024
        ),
        cost_estimate=pl.CostEstimate(flops=10_000_000_000, bytes_accessed=8_000_000, transcendentals=50_000),
    )(x, w, cot, bias, gat, sca)
    sampled = samp.reshape(8, 2, 2, 12, 128)
    clip_grad = dx.reshape(8, 384, 2, 64).transpose(1, 2, 0, 3).reshape(1, 4, 4, 24, 1024)
    return sampled, clip_grad, dw.reshape(3, 3, 3, 32, 128), db[0]


def solution(mesh):
    return jax.shard_map(
        shards,
        mesh=mesh,
        in_specs=(
            P("dp", "tm", None, None, None),
            P(None, None, None, "tm", "dp"),
            P("dp"),
            P(None, "tm", None, None, "dp"),
        ),
        out_specs=(
            P(None, "tm", None, None, "dp"),
            P("dp", "tm", None, None, None),
            P(None, None, None, "tm", "dp"),
            P("dp"),
        ),
        check_vma=False,
    )
```

```python
import math

import jax
import jax.numpy as jnp
import numpy as np
from jax import lax
from jax.experimental import pallas as pl
from jax.experimental.pallas import tpu as pltpu
from jax.sharding import PartitionSpec as P

MESH = pl.DeviceIdType.MESH
F32 = jnp.float32
BF16 = jnp.bfloat16
POSITIONS = 12288


def tap_gather():
    table = np.zeros((224, 96), np.float32)
    for h in range(3):
        for w in range(3):
            for r in range(2):
                for q in range(12):
                    row, col = 2 * r + h - 1, 2 * q + w - 1
                    if 0 <= row < 4 and 0 <= col < 24:
                        table[(h * 3 + w) * 24 + q * 2 + r, row * 24 + col] = 1.0
    return table


def kernel(
    x_ref, w_ref, cot_ref, bias_ref, gat_ref, sca_ref,
    samp_out, dx_out, dw_out, db_out,
    xv, xp, land, halo, wg, cotl, biasb, biasl, im_e, im_o, pacc, part, rsl, sbuf, sland, gbuf, bz, bs, bl,
    dtmp, dxb, dxp, dxs, dxl, dxo, dwb, dws, dwr, dwl, dwo, dwx, dwy, kout, dbo,
    v_sem, x_send, x_recv, f_send, h_sem, w_send, w_recv, c_send, c_recv, b_send, b_recv, rs_send, rs_recv,
    s_send, s_recv, ag_send, ag_recv, bz_send, bz_recv, gh_send, gh_recv, bs_send, bs_recv, dxp_send, dxp_recv,
    dx_send, dx_recv, k1_send, k1_recv, k2_send, k2_recv, k3_send, k3_recv, o_sem,
):
    dp, tm = lax.axis_index("dp"), lax.axis_index("tm")
    xl, y = lax.div(dp, 4), lax.rem(dp, 4)
    xh, z, c = lax.div(tm, 16), lax.rem(lax.div(tm, 2), 8), lax.rem(tm, 2)
    primary = c == xl
    inv = 1.0 / math.sqrt(POSITIONS)

    def dev(xl_, y_, xh_, z_, c_):
        return (xl_ * 4 + y_, (xh_ * 8 + z_) * 2 + c_)

    def remote(src, dst, send, recv, device):
        return pltpu.make_async_remote_copy(
            src_ref=src, dst_ref=dst, send_sem=send, recv_sem=recv, device_id=device, device_id_type=MESH
        )

    def landed(dst, sem):
        pltpu.make_async_copy(dst, dst, sem).wait()

    def plus(a, by, n):
        return lax.rem(a + by, n)

    partner = dev(1 - xl, y, xh, z, c)
    sibling = dev(xl, y, xh, z, 1 - c)
    across = dev(xl, y, 1 - xh, z, c)

    x_in = pltpu.make_async_copy(x_ref, xv, v_sem.at[0])
    x_in.start()

    barrier = pltpu.get_barrier_semaphore()
    peers = [partner]
    for dz in range(8):
        for dc in range(2):
            if dz or dc:
                peers.append(dev(xl, y, xh, plus(z, dz, 8), plus(c, dc, 2)))
    for dy in range(4):
        for dh in range(2):
            for dc in range(2):
                if dy or dh:
                    peers.append(dev(xl, plus(y, dy, 4), plus(xh, dh, 2), z, plus(c, dc, 2)))
    for dz in range(1, 8):
        peers.append(dev(xl, y, 1 - xh, plus(z, dz, 8), c))
    for peer in peers:
        pl.semaphore_signal(barrier, inc=1, device_id=peer, device_id_type=MESH)

    biasb[...] = jnp.broadcast_to(bias_ref[...], (8, 128))
    x_in.wait()
    for zt in range(8):
        at = (zt // 2) * 128 + (zt % 2) * 64
        xp[zt] = jnp.concatenate([xv[:, at:at + 64], xv[:, 512 + at:512 + at + 64]], axis=1)
    pl.semaphore_wait(barrier, len(peers))

    ends = []

    me_k = 2 * z + c
    for n, dz in enumerate((1, 7, 2, 6, 3, 5, 4)):
        zt = plus(z, dz, 8)
        copy = remote(xp.at[zt], land.at[me_k], x_send.at[n], x_recv.at[me_k], dev(xl, y, xh, zt, xl))
        copy.start()
        ends.append(copy.wait_send)
    own_x = pltpu.make_async_copy(xp.at[z], land.at[me_k], x_recv.at[me_k])
    sib_x = remote(xp.at[z], land.at[me_k], x_send.at[7], x_recv.at[me_k], dev(xl, y, xh, z, 1 - c))

    @pl.when(primary)
    def _():
        own_x.start()

    @pl.when(jnp.logical_not(primary))
    def _():
        sib_x.start()

    def w_at(h_, c_, y_):
        return wg.at[:, pl.ds(pl.multiple_of((h_ * 2 + c_) * 32, 32), 32), pl.ds(pl.multiple_of(y_ * 128, 128), 128)]

    def w_sem(h_, c_, y_):
        return w_recv.at[(h_ * 2 + c_) * 4 + y_]

    w_count = [0]

    def w_push(src, h_, c_, y_, device):
        copy = remote(src, w_at(h_, c_, y_), w_send.at[w_count[0]], w_sem(h_, c_, y_), device)
        w_count[0] += 1
        copy.start()
        ends.append(copy.wait_send)

    up, down = plus(y, 1, 4), plus(y, 3, 4)
    dev_up, dev_down = dev(xl, up, xh, z, c), dev(xl, down, xh, z, c)
    w_push(w_ref, xh, c, y, across)
    w_push(w_ref, xh, c, y, dev_up)
    w_push(w_ref, xh, c, y, dev_down)
    w_push(w_ref, xh, c, y, sibling)
    pltpu.make_async_copy(w_ref, w_at(xh, c, y), w_sem(xh, c, y)).start()

    for dy in range(4):
        for dc in range(2):
            yd, cd = plus(y, dy, 4), plus(c, dc, 2)
            src, dst, sem = cot_ref.at[cd * 4 + yd], cotl.at[c, y], c_recv.at[c * 4 + y]
            if dy or dc:
                copy = remote(src, dst, c_send.at[dy * 2 + dc], sem, dev(xl, yd, xh, z, cd))
                copy.start()
                ends.append(copy.wait_send)
            else:
                pltpu.make_async_copy(src, dst, sem).start()
    pltpu.make_async_copy(biasb, biasl.at[y], b_recv.at[y]).start()
    for dy in range(1, 4):
        copy = remote(biasb, biasl.at[y], b_send.at[dy], b_recv.at[y], dev(xl, plus(y, dy, 4), xh, z, c))
        copy.start()
        ends.append(copy.wait_send)

    halo_copy = remote(land.at[15, pl.ds(288, 96)], halo, h_sem.at[0], h_sem.at[1], across)
    ends.append(halo_copy.wait_send)

    def spread(j, carry):
        dz = jnp.where(lax.rem(j, 2) == 1, lax.div(j + 1, 2), lax.rem(8 - lax.div(j, 2), 8))
        zs = plus(z, dz, 8)
        for cs in range(2):
            k = 2 * zs + cs
            landed(land.at[k], x_recv.at[k])

            @pl.when(primary)
            def _():
                remote(land.at[k], land.at[k], f_send.at[k], x_recv.at[k], partner).start()

            if cs == 1:
                @pl.when(k == 15)
                def _():
                    halo_copy.start()

        for cs in range(2):
            k = 2 * zs + cs
            frames = land[k]
            side = jnp.concatenate([frames[i * 96:(i + 1) * 96] for i in range(4)], axis=1)
            taps = jnp.dot(gat_ref[...], side, preferred_element_type=F32)
            for i in range(4):
                piece = taps[:216, i * 128:(i + 1) * 128].reshape(9, 24, 128)
                if i % 2 == 0:
                    im_e[:, 2 * k + i // 2] = piece
                else:
                    im_o[:, 2 * k + 1 + i // 2] = piece
        return carry

    def w_pass(h_, y_, device):
        landed(w_at(h_, c, y_), w_sem(h_, c, y_))
        if device is not None:
            w_push(w_at(h_, c, y_), h_, c, y_, device)
        w_push(w_at(h_, c, y_), h_, c, y_, sibling)

    lax.fori_loop(0, 2, spread, 0)
    w_pass(1 - xh, y, dev_up)
    w_push(w_at(1 - xh, c, y), 1 - xh, c, y, dev_down)
    lax.fori_loop(2, 3, spread, 0)
    w_pass(xh, down, dev_up)
    w_pass(xh, up, None)
    lax.fori_loop(3, 5, spread, 0)
    w_pass(1 - xh, up, dev_down)
    w_pass(1 - xh, down, None)
    lax.fori_loop(5, 8, spread, 0)
    w_pass(xh, plus(y, 2, 4), None)
    w_pass(1 - xh, plus(y, 2, 4), None)
    landed(w_at(xh, c, y), w_sem(xh, c, y))
    for dy in range(4):
        for h_ in (xh, 1 - xh):
            yd = plus(y, dy, 4)
            landed(w_at(h_, 1 - c, yd), w_sem(h_, 1 - c, yd))

    landed(halo, h_sem.at[1])
    rim = jnp.dot(gat_ref[...], halo[...], preferred_element_type=F32)[:216].reshape(9, 24, 128)
    im_o[:, 0] = jnp.where(xh == 1, rim, jnp.zeros_like(rim))

    def forward(dzs):
        zts = [plus(z, dz, 8) for dz in dzs]

        def rows(held, hw, by):
            return jnp.concatenate([held[hw, pl.ds(4 * zt + by, 4)].reshape(96, 128) for zt in zts], axis=0).astype(BF16)

        def step(h, carry):
            lhs, rhs = [], []
            for w in range(3):
                hw = h * 3 + w
                lhs += [rows(im_o, hw, 0), rows(im_e, hw, 0), rows(im_o, hw, 1)]
                rhs += [wg[hw], wg[9 + hw], wg[18 + hw]]
            pacc[...] += jnp.dot(
                jnp.concatenate(lhs, axis=1), jnp.concatenate(rhs, axis=0), preferred_element_type=F32
            )
            return carry

        pacc[...] = jnp.zeros_like(pacc)
        lax.fori_loop(0, 3, step, 0)
        for q in range(4):
            zt = zts[q]
            part[zt] = pacc[q * 96:(q + 1) * 96].astype(BF16)
            if dzs[q]:
                copy = remote(part.at[zt], rsl.at[z], rs_send.at[dzs[q]], rs_recv.at[z], dev(xl, y, xh, zt, c))
                copy.start()
                ends.append(copy.wait_send)

    forward((4, 3, 5, 2))
    forward((6, 1, 7, 0))

    for dy in range(4):
        yd = plus(y, dy, 4)
        landed(biasl.at[yd], b_recv.at[yd])
        for cs in range(2):
            landed(cotl.at[cs, yd], c_recv.at[cs * 4 + yd])
    pre = part[z].astype(F32)
    for dz in (1, 7, 2, 6, 3, 5, 4):
        zs = plus(z, dz, 8)
        landed(rsl.at[zs], rs_recv.at[zs])
        pre = pre + rsl[zs].astype(F32)
    pre = pre + jnp.concatenate([biasl[i, 0:1] for i in range(4)], axis=1)
    sig = 1.0 / (1.0 + jnp.exp(-pre))
    samp = (pre * sig).astype(BF16)
    cot = jnp.concatenate(
        [jnp.concatenate([cotl[cs, i] for i in range(4)], axis=1) for cs in range(2)], axis=0
    ).astype(F32)
    slope = cot * sig * (1.0 + pre * (1.0 - sig))
    gbuf[z] = slope.astype(BF16)
    def g_at(o, half):
        return gbuf.at[o, pl.ds(half * 48, 48)]

    ag_count = [0]

    def ag_push(o, half, device):
        copy = remote(g_at(o, half), g_at(o, half), ag_send.at[ag_count[0]], ag_recv.at[o * 2 + half], device)
        ag_count[0] += 1
        copy.start()
        ends.append(copy.wait_send)

    next_z, last_z = dev(xl, y, xh, plus(z, 1, 8), c), dev(xl, y, xh, plus(z, 7, 8), c)
    for half in range(2):
        ag_push(z, half, next_z)
        ag_push(z, half, last_z)

    def rim_copy(zt):
        return remote(
            gbuf.at[0, pl.ds(0, 32)], gbuf.at[8, pl.ds(0, 32)], gh_send.at[zt], gh_recv.at[0], dev(xl, y, 0, zt, c)
        )

    gives_rim = jnp.logical_and(z == 0, xh == 1)

    @pl.when(gives_rim)
    def _():
        for zt in range(8):
            rim_copy(zt).start()

    @pl.when(xh == 1)
    def _():
        gbuf[8, pl.ds(0, 32)] = jnp.zeros((32, 512), BF16)

    sums = jnp.sum(slope, axis=0, keepdims=True)
    bz[z] = jnp.concatenate([sums[:, i * 128:(i + 1) * 128] for i in range(4)] + [jnp.zeros((4, 128), F32)], axis=0)
    for n, dz in enumerate((1, 7, 2, 6, 3, 5, 4)):
        copy = remote(bz.at[z], bz.at[z], bz_send.at[n], bz_recv.at[z], dev(xl, y, xh, plus(z, dz, 8), c))
        copy.start()
        ends.append(copy.wait_send)
    for cs in range(2):
        for i in range(4):
            sbuf[cs, i] = samp[cs * 48:(cs + 1) * 48, i * 128:(i + 1) * 128]
    for dy in range(4):
        for dc in range(2):
            yd, cd = plus(y, dy, 4), plus(c, dc, 2)
            src, dst, sem = sbuf.at[cd, yd], sland.at[c * 4 + y], s_recv.at[c * 4 + y]
            if dy or dc:
                copy = remote(src, dst, s_send.at[dy * 2 + dc], sem, dev(xl, yd, xh, z, cd))
                copy.start()
                ends.append(copy.wait_send)
            else:
                pltpu.make_async_copy(src, dst, sem).start()

    def chunk_back(zc):
        def back(h, carry):
            hws = [h * 3 + w for w in range(3)]
            mats = jnp.concatenate([wg[t * 9 + hw] for hw in hws for t in range(3)], axis=0)
            rows = jnp.concatenate([gbuf[zc], gbuf[zc + 1, 0:32]], axis=0)
            r = lax.dot_general(rows, mats, (((1,), (1,)), ((), ())), preferred_element_type=F32)
            for w in range(3):
                at = w * 384
                dtmp[h * 3 + w, 0:4] = r[:96, at + 128:at + 256].reshape(4, 24, 128)
                dtmp[h * 3 + w, 4:8] = (r[:96, at + 256:at + 384] + r[24:120, at:at + 128]).reshape(4, 24, 128)
            return carry

        lax.fori_loop(0, 3, back, 0)
        cols = [dtmp[:, i + 4 * odd].reshape(216, 128) for i in range(4) for odd in range(2)]
        side = jnp.concatenate(cols, axis=1)
        side = jnp.concatenate([side, jnp.zeros((8, 1024), F32)], axis=0).astype(BF16)
        r = jnp.dot(sca_ref[...], side, preferred_element_type=F32).astype(BF16)
        for cs in range(2):
            k = 2 * zc + cs
            for i in range(4):
                dxb[k, pl.ds(i * 96, 96)] = r[:, (cs * 4 + i) * 128:(cs * 4 + i + 1) * 128]

            @pl.when(jnp.logical_not(primary))
            def _(k=k):
                remote(dxb.at[k], dxp.at[k], dxp_send.at[k], dxp_recv.at[k], partner).start()

    def back_pair(first, second):
        def one(i, carry):
            chunk_back(jnp.where(i == 0, first, second))
            return carry

        lax.fori_loop(0, 2, one, 0)

    def send_back(k):
        landed(dxp.at[k], dxp_recv.at[k])
        dxs[k] = (dxb[k].astype(F32) + dxp[k].astype(F32)).astype(BF16)

        @pl.when(k == me_k)
        def _():
            pltpu.make_async_copy(dxs.at[k], dxl.at[z], dx_recv.at[z]).start()

        @pl.when(k != me_k)
        def _():
            remote(
                dxs.at[k], dxl.at[z], dx_send.at[k], dx_recv.at[z], dev(xl, y, xh, lax.div(k, 2), lax.rem(k, 2))
            ).start()

    def finish_pair(first, second):
        @pl.when(primary)
        def _():
            def one(i, carry):
                zc = jnp.where(i < 2, first, second)
                send_back(2 * zc + lax.rem(i, 2))
                return carry

            lax.fori_loop(0, 4, one, 0)

    def z_at(dz):
        return plus(z, dz % 8, 8)

    for step in range(1, 4):
        below, above = z_at(-step), z_at(step)
        for half in range(2):
            landed(g_at(below, half), ag_recv.at[below * 2 + half])
            if step < 3 or half == 0:
                ag_push(below, half, next_z)
            landed(g_at(above, half), ag_recv.at[above * 2 + half])
            if step < 3 or half == 1:
                ag_push(above, half, last_z)
        if step == 1:
            @pl.when(xh == 0)
            def _():
                landed(gbuf.at[8, pl.ds(0, 32)], gh_recv.at[0])

        back_pair(z_at(step - 1), z_at(-step))
        if step > 1:
            finish_pair(z_at(step - 2), z_at(1 - step))
    for half in range(2):
        landed(g_at(z_at(4), half), ag_recv.at[z_at(4) * 2 + half])

    def weight_grad(h):
        def grad_step(w, carry):
            hw = h * 3 + w
            lhs = jnp.concatenate(
                [
                    im_o[hw, pl.ds(0, 32)].reshape(768, 128).astype(BF16),
                    im_e[hw].reshape(768, 128).astype(BF16),
                    im_o[hw, pl.ds(1, 32)].reshape(768, 128).astype(BF16),
                ],
                axis=1,
            )
            r = lax.dot_general(
                lhs, gbuf[0:8].reshape(768, 512), (((0,), (0,)), ((), ())), preferred_element_type=F32
            ).astype(BF16)
            for t in range(3):
                for h_ in range(2):
                    for c_ in range(2):
                        at = t * 128 + h_ * 64 + c_ * 32
                        dwb[h, c_, h_, w * 3 + t] = r[at:at + 32]
            return carry

        lax.fori_loop(0, 3, grad_step, 0)
        copy = remote(dwb.at[h, 1 - c], dws.at[h], k1_send.at[h], k1_recv.at[h], sibling)
        copy.start()
        ends.append(copy.wait_send)

    def over_y(h):
        landed(dws.at[h], k1_recv.at[h])

        def add_step(n, carry):
            for h_ in range(2):
                dwr[h, h_, n] = (dwb[h, c, h_, n].astype(F32) + dws[h, h_, n].astype(F32)).astype(BF16)
            return carry

        lax.fori_loop(0, 9, add_step, 0)
        for dy in range(4):
            yd = plus(y, dy, 4)
            src = dwr.at[h, :, :, :, pl.ds(pl.multiple_of(yd * 128, 128), 128)]
            dst, sem = dwl.at[h, y], k2_recv.at[h * 4 + y]
            if dy:
                copy = remote(src, dst, k2_send.at[h * 4 + dy], sem, dev(xl, yd, xh, z, c))
                copy.start()
                ends.append(copy.wait_send)
            else:
                pltpu.make_async_copy(src, dst, sem).start()

    def over_x(h):
        for i in range(4):
            landed(dwl.at[h, i], k2_recv.at[h * 4 + i])

        def add_step(n, carry):
            own, other = dwl[h, 0, xh, n].astype(F32), dwl[h, 0, 1 - xh, n].astype(F32)
            for i in range(1, 4):
                own = own + dwl[h, i, xh, n].astype(F32)
                other = other + dwl[h, i, 1 - xh, n].astype(F32)
            dwo[h, n] = own
            dwx[h, n] = other.astype(BF16)
            return carry

        lax.fori_loop(0, 9, add_step, 0)
        copy = remote(dwx.at[h], dwy.at[h], k3_send.at[h], k3_recv.at[h], across)
        copy.start()
        ends.append(copy.wait_send)

    weight_grad(0)
    back_pair(z_at(3), z_at(4))
    over_y(0)
    finish_pair(z_at(2), z_at(-3))
    weight_grad(1)
    weight_grad(2)
    over_y(1)
    finish_pair(z_at(3), z_at(4))
    over_y(2)

    total = bz[z]
    for dz in (1, 7, 2, 6, 3, 5, 4):
        zs = plus(z, dz, 8)
        landed(bz.at[zs], bz_recv.at[zs])
        total = total + bz[zs]
    for i in range(4):
        bs[i] = jnp.broadcast_to(total[i:i + 1], (8, 128))
    slot_b = (xh * 2 + c) * 4 + y
    for dy in range(4):
        for dh in range(2):
            for dc in range(2):
                yd, hd, cd = plus(y, dy, 4), plus(xh, dh, 2), plus(c, dc, 2)
                if dy or dh or dc:
                    copy = remote(
                        bs.at[yd], bl.at[slot_b], bs_send.at[(dy * 2 + dh) * 2 + dc], bs_recv.at[slot_b],
                        dev(xl, yd, hd, z, cd),
                    )
                    copy.start()
                    ends.append(copy.wait_send)
                else:
                    pltpu.make_async_copy(bs.at[y], bl.at[slot_b], bs_recv.at[slot_b]).start()

    outs = []
    for i in range(8):
        landed(sland.at[i], s_recv.at[i])
    outs.append(pltpu.make_async_copy(sland, samp_out, o_sem.at[0]))
    outs[-1].start()

    for h in range(3):
        over_x(h)
    for h in range(3):
        landed(dwy.at[h], k3_recv.at[h])

        def sum_step(w, carry, h=h):
            for t in range(3):
                kout[t * 9 + h * 3 + w] = (dwo[h, w * 3 + t] + dwy[h, w * 3 + t].astype(F32)) * inv
            return carry

        lax.fori_loop(0, 3, sum_step, 0)
    outs.append(pltpu.make_async_copy(kout, dw_out, o_sem.at[1]))
    outs[-1].start()

    acc = None
    for i in range(16):
        landed(bl.at[i], bs_recv.at[i])
        acc = bl[i] if acc is None else acc + bl[i]
    dbo[...] = acc[0:1] * inv
    outs.append(pltpu.make_async_copy(dbo, db_out, o_sem.at[2]))
    outs[-1].start()

    for m in range(4):
        for i in (2 * m, 2 * m + 1):
            landed(dxl.at[i], dx_recv.at[i])
        a, b = dxl[2 * m], dxl[2 * m + 1]
        dxo[:, m * 128:(m + 1) * 128] = jnp.concatenate([a[:, :64], b[:, :64]], axis=1)
        dxo[:, 512 + m * 128:512 + (m + 1) * 128] = jnp.concatenate([a[:, 64:], b[:, 64:]], axis=1)
    outs.append(pltpu.make_async_copy(dxo, dx_out, o_sem.at[3]))
    outs[-1].start()

    for end in ends:
        end()

    @pl.when(jnp.logical_not(primary))
    def _():
        sib_x.wait_send()

        def drain(k, carry):
            remote(dxb.at[k], dxp.at[k], dxp_send.at[k], dxp_recv.at[k], partner).wait_send()
            return carry

        lax.fori_loop(0, 16, drain, 0)

    @pl.when(primary)
    def _():
        def drain(k, carry):
            remote(land.at[k], land.at[k], f_send.at[k], x_recv.at[k], partner).wait_send()

            @pl.when(k != me_k)
            def _():
                remote(
                    dxs.at[k], dxl.at[z], dx_send.at[k], dx_recv.at[z],
                    dev(xl, y, xh, lax.div(k, 2), lax.rem(k, 2)),
                ).wait_send()

            return carry

        lax.fori_loop(0, 16, drain, 0)

    @pl.when(gives_rim)
    def _():
        for zt in range(8):
            rim_copy(zt).wait_send()

    for out in outs:
        out.wait()


def shards(video_clips, weights, conv_bias, cotangent):
    x = video_clips.reshape(384, 1024)
    w = weights.reshape(27, 32, 128)
    cot = cotangent.transpose(0, 1, 3, 2, 4).reshape(8, 48, 128)
    bias = conv_bias.reshape(1, 128)
    table = tap_gather()
    gat = jnp.asarray(table, BF16)
    sca = jnp.asarray(table.T, BF16)
    any_spec = pl.BlockSpec(memory_space=pl.ANY)
    vmem_spec = pl.BlockSpec(memory_space=pltpu.VMEM)

    def v(shape, dtype=BF16):
        return pltpu.VMEM(shape, dtype)

    def sems(n):
        return pltpu.SemaphoreType.DMA((n,))

    samp, dx, dw, db = pl.pallas_call(
        kernel,
        out_shape=[
            jax.ShapeDtypeStruct((8, 48, 128), BF16),
            jax.ShapeDtypeStruct((384, 1024), BF16),
            jax.ShapeDtypeStruct((27, 32, 128), F32),
            jax.ShapeDtypeStruct((1, 128), F32),
        ],
        in_specs=[any_spec] * 3 + [vmem_spec] * 3,
        out_specs=[any_spec] * 4,
        scratch_shapes=[
            v((384, 1024)),
            v((8, 384, 128)),
            v((16, 384, 128)),
            v((96, 128)),
            v((27, 128, 512)),
            v((2, 4, 48, 128)),
            v((8, 128), F32),
            v((4, 8, 128), F32),
            v((9, 32, 24, 128), F32),
            v((9, 33, 24, 128), F32),
            v((384, 512), F32),
            v((8, 96, 512)),
            v((8, 96, 512)),
            v((2, 4, 48, 128)),
            v((8, 48, 128)),
            v((9, 96, 512)),
            v((8, 8, 128), F32),
            v((4, 8, 128), F32),
            v((16, 8, 128), F32),
            v((9, 8, 24, 128), F32),
            v((16, 384, 128)),
            v((16, 384, 128)),
            v((16, 384, 128)),
            v((8, 384, 128)),
            v((384, 1024)),
            v((3, 2, 2, 9, 32, 512)),
            v((3, 2, 9, 32, 512)),
            v((3, 2, 9, 32, 512)),
            v((3, 4, 2, 9, 32, 128)),
            v((3, 9, 32, 128), F32),
            v((3, 9, 32, 128)),
            v((3, 9, 32, 128)),
            v((27, 32, 128), F32),
            v((1, 128), F32),
            sems(1), sems(8), sems(16), sems(16), sems(2),
            sems(16), sems(16), sems(8), sems(8), sems(4), sems(4),
            sems(8), sems(8), sems(8), sems(8), sems(14), sems(16), sems(8), sems(8),
            sems(8), sems(1), sems(16), sems(16), sems(16), sems(16), sems(16), sems(8),
            sems(3), sems(3), sems(12), sems(12), sems(3), sems(3), sems(4),
        ],
        compiler_params=pltpu.CompilerParams(
            collective_id=0, has_side_effects=True, vmem_limit_bytes=60 * 1024 * 1024
        ),
        cost_estimate=pl.CostEstimate(flops=10_000_000_000, bytes_accessed=8_000_000, transcendentals=50_000),
    )(x, w, cot, bias, gat, sca)
    sampled = samp.reshape(8, 2, 12, 2, 128).transpose(0, 1, 3, 2, 4)
    clip_grad = dx.reshape(1, 4, 4, 24, 1024)
    return sampled, clip_grad, dw.reshape(3, 3, 3, 32, 128), db.reshape(128)


def solution(mesh):
    return jax.shard_map(
        shards,
        mesh=mesh,
        in_specs=(
            P("dp", "tm", None, None, None),
            P(None, None, None, "tm", "dp"),
            P("dp"),
            P(None, "tm", None, None, "dp"),
        ),
        out_specs=(
            P(None, "tm", None, None, "dp"),
            P("dp", "tm", None, None, None),
            P(None, None, None, "tm", "dp"),
            P("dp"),
        ),
        check_vma=False,
    )
```

```python
import math

import jax
import jax.numpy as jnp
import numpy as np
from jax import lax
from jax.experimental import pallas as pl
from jax.experimental.pallas import tpu as pltpu
from jax.sharding import PartitionSpec as P

MESH = pl.DeviceIdType.MESH
F32 = jnp.float32
BF16 = jnp.bfloat16
POSITIONS = 12288


def tap_gather():
    table = np.zeros((224, 96), np.float32)
    for h in range(3):
        for w in range(3):
            for r in range(2):
                for q in range(12):
                    row, col = 2 * r + h - 1, 2 * q + w - 1
                    if 0 <= row < 4 and 0 <= col < 24:
                        table[(h * 3 + w) * 24 + q * 2 + r, row * 24 + col] = 1.0
    return table


def kernel(
    x_ref, w_ref, cot_ref, bias_ref, gat_ref, sca_ref,
    samp_out, dx_out, dw_out, db_out,
    xv, xp, land, halo, wg, cotl, biasb, biasl, im_e, im_o, pacc, part, rsl, rss, sbuf, sland, gbuf, bz, bs, bl,
    dtmp, dxb, dxp, dxs, dxl, dxo, dwb, dws, dwr, dwl, dwo, dwx, dwy, dwm, dwn, kout, dbo,
    v_sem, x_send, x_recv, f_send, h_sem, w_send, w_recv, c_send, c_recv, b_send, b_recv, rs_send, rs_recv,
    s_send, s_recv, ag_send, ag_recv, bz_send, bz_recv, gh_send, gh_recv, bs_send, bs_recv, dxp_send, dxp_recv,
    dx_send, dx_recv, k1_send, k1_recv, k2_send, k2_recv, k3_send, k3_recv, o_sem,
):
    dp, tm = lax.axis_index("dp"), lax.axis_index("tm")
    xl, y = lax.div(dp, 4), lax.rem(dp, 4)
    xh, z, c = lax.div(tm, 16), lax.rem(lax.div(tm, 2), 8), lax.rem(tm, 2)
    primary = c == xl
    inv = 1.0 / math.sqrt(POSITIONS)

    def dev(xl_, y_, xh_, z_, c_):
        return (xl_ * 4 + y_, (xh_ * 8 + z_) * 2 + c_)

    def remote(src, dst, send, recv, device):
        return pltpu.make_async_remote_copy(
            src_ref=src, dst_ref=dst, send_sem=send, recv_sem=recv, device_id=device, device_id_type=MESH
        )

    def landed(dst, sem):
        pltpu.make_async_copy(dst, dst, sem).wait()

    def plus(a, by, n):
        return lax.rem(a + by, n)

    partner = dev(1 - xl, y, xh, z, c)
    sibling = dev(xl, y, xh, z, 1 - c)
    across = dev(xl, y, 1 - xh, z, c)

    x_in = pltpu.make_async_copy(x_ref, xv, v_sem.at[0])
    x_in.start()

    barrier = pltpu.get_barrier_semaphore()
    peers = [partner]
    for dz in range(8):
        for dc in range(2):
            if dz or dc:
                peers.append(dev(xl, y, xh, plus(z, dz, 8), plus(c, dc, 2)))
    for dy in range(4):
        for dh in range(2):
            for dc in range(2):
                if dy or dh:
                    peers.append(dev(xl, plus(y, dy, 4), plus(xh, dh, 2), z, plus(c, dc, 2)))
    for dz in range(1, 8):
        peers.append(dev(xl, y, 1 - xh, plus(z, dz, 8), c))
    for peer in peers:
        pl.semaphore_signal(barrier, inc=1, device_id=peer, device_id_type=MESH)

    biasb[...] = jnp.broadcast_to(bias_ref[...], (8, 128))
    x_in.wait()
    for zt in range(8):
        at = (zt // 2) * 128 + (zt % 2) * 64
        xp[zt] = jnp.concatenate([xv[:, at:at + 64], xv[:, 512 + at:512 + at + 64]], axis=1)
    pl.semaphore_wait(barrier, len(peers))

    ends = []

    me_k = 2 * z + c
    for n, dz in enumerate((4, 3, 5, 2, 6, 1, 7)):
        zt = plus(z, dz, 8)
        copy = remote(xp.at[zt], land.at[me_k], x_send.at[n], x_recv.at[me_k], dev(xl, y, xh, zt, xl))
        copy.start()
        ends.append(copy.wait_send)
    own_x = pltpu.make_async_copy(xp.at[z], land.at[me_k], x_recv.at[me_k])
    sib_x = remote(xp.at[z], land.at[me_k], x_send.at[7], x_recv.at[me_k], dev(xl, y, xh, z, 1 - c))

    @pl.when(primary)
    def _():
        own_x.start()

    @pl.when(jnp.logical_not(primary))
    def _():
        sib_x.start()

    def w_at(h_, c_, y_):
        return wg.at[:, pl.ds(pl.multiple_of((h_ * 2 + c_) * 32, 32), 32), pl.ds(pl.multiple_of(y_ * 128, 128), 128)]

    def w_sem(h_, c_, y_):
        return w_recv.at[(h_ * 2 + c_) * 4 + y_]

    w_count = [0]

    def w_push(src, h_, c_, y_, device):
        copy = remote(src, w_at(h_, c_, y_), w_send.at[w_count[0]], w_sem(h_, c_, y_), device)
        w_count[0] += 1
        copy.start()
        ends.append(copy.wait_send)

    up, down = plus(y, 1, 4), plus(y, 3, 4)
    dev_up, dev_down = dev(xl, up, xh, z, c), dev(xl, down, xh, z, c)
    w_push(w_ref, xh, c, y, across)
    w_push(w_ref, xh, c, y, dev_up)
    w_push(w_ref, xh, c, y, dev_down)
    w_push(w_ref, xh, c, y, sibling)
    pltpu.make_async_copy(w_ref, w_at(xh, c, y), w_sem(xh, c, y)).start()

    for dy in range(4):
        for dc in range(2):
            yd, cd = plus(y, dy, 4), plus(c, dc, 2)
            src, dst, sem = cot_ref.at[cd * 4 + yd], cotl.at[c, y], c_recv.at[c * 4 + y]
            if dy or dc:
                copy = remote(src, dst, c_send.at[dy * 2 + dc], sem, dev(xl, yd, xh, z, cd))
                copy.start()
                ends.append(copy.wait_send)
            else:
                pltpu.make_async_copy(src, dst, sem).start()
    pltpu.make_async_copy(biasb, biasl.at[y], b_recv.at[y]).start()
    for dy in range(1, 4):
        copy = remote(biasb, biasl.at[y], b_send.at[dy], b_recv.at[y], dev(xl, plus(y, dy, 4), xh, z, c))
        copy.start()
        ends.append(copy.wait_send)

    halo_copy = remote(land.at[15, pl.ds(288, 96)], halo, h_sem.at[0], h_sem.at[1], across)
    ends.append(halo_copy.wait_send)

    def place_of(j):
        far = jnp.where(lax.rem(j, 2) == 0, 4 - lax.div(j, 2), 4 + lax.div(j, 2))
        return plus(z, jnp.where(j == 0, 0, far), 8)

    def pass_on(first, last):
        @pl.when(primary)
        def _():
            def one(i, carry):
                k = 2 * place_of(lax.div(i, 2)) + lax.rem(i, 2)
                landed(land.at[k], x_recv.at[k])
                remote(land.at[k], land.at[k], f_send.at[k], x_recv.at[k], partner).start()
                return carry

            lax.fori_loop(2 * first, 2 * last, one, 0)

    def take_in(first, last):
        def one(i, carry):
            k = 2 * place_of(lax.div(i, 2)) + lax.rem(i, 2)

            @pl.when(jnp.logical_not(primary))
            def _():
                landed(land.at[k], x_recv.at[k])

            @pl.when(k == 15)
            def _():
                halo_copy.start()

            frames = land[k]
            side = jnp.concatenate([frames[i * 96:(i + 1) * 96] for i in range(4)], axis=1)
            taps = jnp.dot(gat_ref[...], side, preferred_element_type=F32)
            for f in range(4):
                piece = taps[:216, f * 128:(f + 1) * 128].reshape(9, 24, 128)
                if f % 2 == 0:
                    im_e[:, 2 * k + f // 2] = piece
                else:
                    im_o[:, 2 * k + 1 + f // 2] = piece
            return carry

        lax.fori_loop(2 * first, 2 * last, one, 0)

    def spread(first, last):
        pass_on(first, last)
        take_in(first, last)

    def w_pass(h_, y_, device):
        landed(w_at(h_, c, y_), w_sem(h_, c, y_))
        if device is not None:
            w_push(w_at(h_, c, y_), h_, c, y_, device)
        w_push(w_at(h_, c, y_), h_, c, y_, sibling)

    spread(0, 1)
    w_pass(1 - xh, y, dev_up)
    w_push(w_at(1 - xh, c, y), 1 - xh, c, y, dev_down)
    spread(1, 2)
    w_pass(xh, down, dev_up)
    w_pass(xh, up, None)
    spread(2, 4)
    w_pass(1 - xh, up, dev_down)
    w_pass(1 - xh, down, None)
    spread(4, 6)
    pass_on(6, 8)
    w_pass(xh, plus(y, 2, 4), None)
    w_pass(1 - xh, plus(y, 2, 4), None)
    landed(w_at(xh, c, y), w_sem(xh, c, y))
    for dy in range(4):
        for h_ in (xh, 1 - xh):
            yd = plus(y, dy, 4)
            landed(w_at(h_, 1 - c, yd), w_sem(h_, 1 - c, yd))

    def z_at(dz):
        return plus(z, dz % 8, 8)

    def forward(dzs):
        zts = [z_at(dz) for dz in dzs]
        size = 96 * len(zts)
        for zt in zts:
            @pl.when(zt == 0)
            def _():
                landed(halo, h_sem.at[1])
                rim = jnp.dot(gat_ref[...], halo[...], preferred_element_type=F32)[:216].reshape(9, 24, 128)
                im_o[:, 0] = jnp.where(xh == 1, rim, jnp.zeros_like(rim))

        def rows(held, hw, by):
            return jnp.concatenate([held[hw, pl.ds(4 * zt + by, 4)].reshape(96, 128) for zt in zts], axis=0).astype(BF16)

        def step(h, carry):
            lhs, rhs = [], []
            for w in range(3):
                hw = h * 3 + w
                lhs += [rows(im_o, hw, 0), rows(im_e, hw, 0), rows(im_o, hw, 1)]
                rhs += [wg[hw], wg[9 + hw], wg[18 + hw]]
            pacc[0:size] += jnp.dot(
                jnp.concatenate(lhs, axis=1), jnp.concatenate(rhs, axis=0), preferred_element_type=F32
            )
            return carry

        pacc[0:size] = jnp.zeros((size, 512), F32)
        lax.fori_loop(0, 3, step, 0)
        for q, dz in enumerate(dzs):
            zt = zts[q]
            part[zt] = pacc[q * 96:(q + 1) * 96].astype(BF16)

    next_z, last_z = dev(xl, y, xh, plus(z, 1, 8), c), dev(xl, y, xh, plus(z, 7, 8), c)

    def rs_hop(way, step, half):
        zt = z_at((5 - step) * (1 - 2 * way))
        at = (way * 4 + step - 1) * 2 + half
        own = part[zt, half * 48:(half + 1) * 48]
        if step > 1 and (step > 2 or half == way):
            before = at - 2
            landed(rsl.at[before], rs_recv.at[before])
            own = (own.astype(F32) + rsl[before].astype(F32)).astype(BF16)
        rss[at] = own
        copy = remote(rss.at[at], rsl.at[at], rs_send.at[at], rs_recv.at[at], last_z if way else next_z)
        copy.start()
        ends.append(copy.wait_send)

    def rs_step(step):
        for half in range(2):
            for way in range(2):
                if step > 1 or half == way:
                    rs_hop(way, step, half)

    forward((4, -3))
    rs_step(1)
    forward((3, -2))
    take_in(6, 8)
    rs_step(2)
    forward((2, -1, 1))
    rs_step(3)
    forward((0,))
    rs_step(4)

    for dy in range(4):
        yd = plus(y, dy, 4)
        landed(biasl.at[yd], b_recv.at[yd])
        for cs in range(2):
            landed(cotl.at[cs, yd], c_recv.at[cs * 4 + yd])
    pre = part[z].astype(F32)
    sums_in = []
    for way in range(2):
        for half in range(2):
            at = (way * 4 + 3) * 2 + half
            landed(rsl.at[at], rs_recv.at[at])
        sums_in.append(jnp.concatenate([rsl[way * 8 + 6], rsl[way * 8 + 7]], axis=0).astype(F32))
    pre = pre + sums_in[0] + sums_in[1]
    pre = pre + jnp.concatenate([biasl[i, 0:1] for i in range(4)], axis=1)
    sig = 1.0 / (1.0 + jnp.exp(-pre))
    samp = (pre * sig).astype(BF16)
    cot = jnp.concatenate(
        [jnp.concatenate([cotl[cs, i] for i in range(4)], axis=1) for cs in range(2)], axis=0
    ).astype(F32)
    slope = cot * sig * (1.0 + pre * (1.0 - sig))
    gbuf[z] = slope.astype(BF16)
    def g_at(o, half):
        return gbuf.at[o, pl.ds(half * 48, 48)]

    ag_count = [0]

    def ag_push(o, half, device):
        copy = remote(g_at(o, half), g_at(o, half), ag_send.at[ag_count[0]], ag_recv.at[o * 2 + half], device)
        ag_count[0] += 1
        copy.start()
        ends.append(copy.wait_send)

    for half in range(2):
        ag_push(z, half, next_z)
        ag_push(z, half, last_z)

    def rim_copy(zt):
        return remote(
            gbuf.at[0, pl.ds(0, 32)], gbuf.at[8, pl.ds(0, 32)], gh_send.at[zt], gh_recv.at[0], dev(xl, y, 0, zt, c)
        )

    gives_rim = jnp.logical_and(z == 0, xh == 1)

    @pl.when(gives_rim)
    def _():
        for zt in range(8):
            rim_copy(zt).start()

    @pl.when(xh == 1)
    def _():
        gbuf[8, pl.ds(0, 32)] = jnp.zeros((32, 512), BF16)

    sums = jnp.sum(slope, axis=0, keepdims=True)
    bz[z] = jnp.concatenate([sums[:, i * 128:(i + 1) * 128] for i in range(4)] + [jnp.zeros((4, 128), F32)], axis=0)
    for n, dz in enumerate((1, 7, 2, 6, 3, 5, 4)):
        copy = remote(bz.at[z], bz.at[z], bz_send.at[n], bz_recv.at[z], dev(xl, y, xh, plus(z, dz, 8), c))
        copy.start()
        ends.append(copy.wait_send)
    for cs in range(2):
        for i in range(4):
            sbuf[cs, i] = samp[cs * 48:(cs + 1) * 48, i * 128:(i + 1) * 128]
    for dy in range(4):
        for dc in range(2):
            yd, cd = plus(y, dy, 4), plus(c, dc, 2)
            src, dst, sem = sbuf.at[cd, yd], sland.at[c * 4 + y], s_recv.at[c * 4 + y]
            if dy or dc:
                copy = remote(src, dst, s_send.at[dy * 2 + dc], sem, dev(xl, yd, xh, z, cd))
                copy.start()
                ends.append(copy.wait_send)
            else:
                pltpu.make_async_copy(src, dst, sem).start()

    def back_pair(first, second):
        def back(h, carry):
            hws = [h * 3 + w for w in range(3)]
            mats = jnp.concatenate([wg[t * 9 + hw] for hw in hws for t in range(3)], axis=0)
            rows = jnp.concatenate(
                [gbuf[first], gbuf[first + 1, 0:32], gbuf[second], gbuf[second + 1, 0:32]], axis=0
            )
            r = lax.dot_general(rows, mats, (((1,), (1,)), ((), ())), preferred_element_type=F32)
            for w in range(3):
                at = w * 384
                for i in range(2):
                    p = r[i * 128:i * 128 + 128]
                    dtmp[i, h * 3 + w, 0:4] = p[:96, at + 128:at + 256].reshape(4, 24, 128)
                    dtmp[i, h * 3 + w, 4:8] = (p[:96, at + 256:at + 384] + p[24:120, at:at + 128]).reshape(4, 24, 128)
            return carry

        lax.fori_loop(0, 3, back, 0)

        def place(i, carry):
            zc = jnp.where(i == 0, first, second)
            cols = [dtmp[i, :, f + 4 * odd].reshape(216, 128) for f in range(4) for odd in range(2)]
            side = jnp.concatenate(cols, axis=1)
            side = jnp.concatenate([side, jnp.zeros((8, 1024), F32)], axis=0).astype(BF16)
            r = jnp.dot(sca_ref[...], side, preferred_element_type=F32).astype(BF16)
            for cs in range(2):
                k = 2 * zc + cs
                for f in range(4):
                    dxb[k, pl.ds(f * 96, 96)] = r[:, (cs * 4 + f) * 128:(cs * 4 + f + 1) * 128]

                @pl.when(jnp.logical_not(primary))
                def _(k=k):
                    remote(dxb.at[k], dxp.at[k], dxp_send.at[k], dxp_recv.at[k], partner).start()
            return carry

        lax.fori_loop(0, 2, place, 0)

    def send_back(k):
        landed(dxp.at[k], dxp_recv.at[k])
        dxs[k] = (dxb[k].astype(F32) + dxp[k].astype(F32)).astype(BF16)

        @pl.when(k == me_k)
        def _():
            pltpu.make_async_copy(dxs.at[k], dxl.at[z], dx_recv.at[z]).start()

        @pl.when(k != me_k)
        def _():
            remote(
                dxs.at[k], dxl.at[z], dx_send.at[k], dx_recv.at[z], dev(xl, y, xh, lax.div(k, 2), lax.rem(k, 2))
            ).start()

    def finish_pair(first, second):
        @pl.when(primary)
        def _():
            def one(i, carry):
                zc = jnp.where(i < 2, first, second)
                send_back(2 * zc + lax.rem(i, 2))
                return carry

            lax.fori_loop(0, 4, one, 0)

    for step in range(1, 4):
        below, above = z_at(-step), z_at(step)
        for half in range(2):
            landed(g_at(below, half), ag_recv.at[below * 2 + half])
            if step < 3 or half == 0:
                ag_push(below, half, next_z)
            landed(g_at(above, half), ag_recv.at[above * 2 + half])
            if step < 3 or half == 1:
                ag_push(above, half, last_z)
        if step == 1:
            @pl.when(xh == 0)
            def _():
                landed(gbuf.at[8, pl.ds(0, 32)], gh_recv.at[0])

        back_pair(z_at(step - 1), z_at(-step))
        if step > 1:
            finish_pair(z_at(step - 2), z_at(1 - step))
    for half in range(2):
        landed(g_at(z_at(4), half), ag_recv.at[z_at(4) * 2 + half])

    def weight_grad(h):
        def grad_step(w, carry):
            hw = h * 3 + w
            lhs = jnp.concatenate(
                [
                    im_o[hw, pl.ds(0, 32)].reshape(768, 128).astype(BF16),
                    im_e[hw].reshape(768, 128).astype(BF16),
                    im_o[hw, pl.ds(1, 32)].reshape(768, 128).astype(BF16),
                ],
                axis=1,
            )
            r = lax.dot_general(
                lhs, gbuf[0:8].reshape(768, 512), (((0,), (0,)), ((), ())), preferred_element_type=F32
            ).astype(BF16)
            for t in range(3):
                for h_ in range(2):
                    for c_ in range(2):
                        at = t * 128 + h_ * 64 + c_ * 32
                        dwb[h, c_, h_, w * 3 + t] = r[at:at + 32]
            return carry

        lax.fori_loop(0, 3, grad_step, 0)
        copy = remote(dwb.at[h, 1 - c], dws.at[h], k1_send.at[h], k1_recv.at[h], sibling)
        copy.start()
        ends.append(copy.wait_send)

    def core_sum(h):
        landed(dws.at[h], k1_recv.at[h])

        def add_step(n, carry):
            for h_ in range(2):
                dwr[h, h_, n] = (dwb[h, c, h_, n].astype(F32) + dws[h, h_, n].astype(F32)).astype(BF16)
            return carry

        lax.fori_loop(0, 9, add_step, 0)

    def y_lanes(i):
        return pl.ds(pl.multiple_of(i * 128, 128), 128)

    def to_y(h):
        core_sum(h)
        for dy in range(4):
            yd = plus(y, dy, 4)
            src = dwr.at[h, :, :, :, y_lanes(yd)]
            dst, sem = dwl.at[h, y], k2_recv.at[h * 4 + y]
            if dy:
                copy = remote(src, dst, k2_send.at[h * 4 + dy], sem, dev(xl, yd, xh, z, c))
                copy.start()
                ends.append(copy.wait_send)
            else:
                pltpu.make_async_copy(src, dst, sem).start()

    def y_to_x(h):
        for i in range(4):
            landed(dwl.at[h, i], k2_recv.at[h * 4 + i])

        def add_step(n, carry):
            own, other = dwl[h, 0, xh, n].astype(F32), dwl[h, 0, 1 - xh, n].astype(F32)
            for i in range(1, 4):
                own = own + dwl[h, i, xh, n].astype(F32)
                other = other + dwl[h, i, 1 - xh, n].astype(F32)
            dwo[h, n] = own
            dwx[h, n] = other.astype(BF16)
            return carry

        lax.fori_loop(0, 9, add_step, 0)
        copy = remote(dwx.at[h], dwy.at[h], k3_send.at[h], k3_recv.at[h], across)
        copy.start()
        ends.append(copy.wait_send)

    def to_x(h):
        core_sum(h)
        copy = remote(dwr.at[h, 1 - xh], dwm, k3_send.at[h], k3_recv.at[h], across)
        copy.start()
        ends.append(copy.wait_send)

    def x_to_y(h):
        landed(dwm, k3_recv.at[h])

        def add_step(n, carry):
            dwn[n] = (dwr[h, xh, n].astype(F32) + dwm[n].astype(F32)).astype(BF16)
            return carry

        lax.fori_loop(0, 9, add_step, 0)
        for dy in range(4):
            yd = plus(y, dy, 4)
            src = dwn.at[:, :, y_lanes(yd)]
            dst, sem = dwl.at[h, y, 0], k2_recv.at[h * 4 + y]
            if dy:
                copy = remote(src, dst, k2_send.at[h * 4 + dy], sem, dev(xl, yd, xh, z, c))
                copy.start()
                ends.append(copy.wait_send)
            else:
                pltpu.make_async_copy(src, dst, sem).start()

    weight_grad(0)
    back_pair(z_at(3), z_at(4))
    to_y(0)
    finish_pair(z_at(2), z_at(-3))
    weight_grad(1)
    weight_grad(2)
    finish_pair(z_at(3), z_at(4))
    to_x(1)
    to_y(2)
    x_to_y(1)

    total = bz[z]
    for dz in (1, 7, 2, 6, 3, 5, 4):
        zs = plus(z, dz, 8)
        landed(bz.at[zs], bz_recv.at[zs])
        total = total + bz[zs]
    for i in range(4):
        bs[i] = jnp.broadcast_to(total[i:i + 1], (8, 128))
    slot_b = (xh * 2 + c) * 4 + y
    for dy in range(4):
        for dh in range(2):
            for dc in range(2):
                yd, hd, cd = plus(y, dy, 4), plus(xh, dh, 2), plus(c, dc, 2)
                if dy or dh or dc:
                    copy = remote(
                        bs.at[yd], bl.at[slot_b], bs_send.at[(dy * 2 + dh) * 2 + dc], bs_recv.at[slot_b],
                        dev(xl, yd, hd, z, cd),
                    )
                    copy.start()
                    ends.append(copy.wait_send)
                else:
                    pltpu.make_async_copy(bs.at[y], bl.at[slot_b], bs_recv.at[slot_b]).start()

    outs = []
    for i in range(8):
        landed(sland.at[i], s_recv.at[i])
    outs.append(pltpu.make_async_copy(sland, samp_out, o_sem.at[0]))
    outs[-1].start()

    y_to_x(0)
    y_to_x(2)
    for i in range(4):
        landed(dwl.at[1, i, 0], k2_recv.at[4 + i])

    def sum_middle(w, carry):
        for t in range(3):
            acc = dwl[1, 0, 0, w * 3 + t].astype(F32)
            for i in range(1, 4):
                acc = acc + dwl[1, i, 0, w * 3 + t].astype(F32)
            kout[t * 9 + 3 + w] = acc * inv
        return carry

    lax.fori_loop(0, 3, sum_middle, 0)
    for h in (0, 2):
        landed(dwy.at[h], k3_recv.at[h])

        def sum_step(w, carry, h=h):
            for t in range(3):
                kout[t * 9 + h * 3 + w] = (dwo[h, w * 3 + t] + dwy[h, w * 3 + t].astype(F32)) * inv
            return carry

        lax.fori_loop(0, 3, sum_step, 0)
    outs.append(pltpu.make_async_copy(kout, dw_out, o_sem.at[1]))
    outs[-1].start()

    acc = None
    for i in range(16):
        landed(bl.at[i], bs_recv.at[i])
        acc = bl[i] if acc is None else acc + bl[i]
    dbo[...] = acc[0:1] * inv
    outs.append(pltpu.make_async_copy(dbo, db_out, o_sem.at[2]))
    outs[-1].start()

    for m in range(4):
        for i in (2 * m, 2 * m + 1):
            landed(dxl.at[i], dx_recv.at[i])
        a, b = dxl[2 * m], dxl[2 * m + 1]
        dxo[:, m * 128:(m + 1) * 128] = jnp.concatenate([a[:, :64], b[:, :64]], axis=1)
        dxo[:, 512 + m * 128:512 + (m + 1) * 128] = jnp.concatenate([a[:, 64:], b[:, 64:]], axis=1)
    outs.append(pltpu.make_async_copy(dxo, dx_out, o_sem.at[3]))
    outs[-1].start()

    for end in ends:
        end()

    @pl.when(jnp.logical_not(primary))
    def _():
        sib_x.wait_send()

        def drain(k, carry):
            remote(dxb.at[k], dxp.at[k], dxp_send.at[k], dxp_recv.at[k], partner).wait_send()
            return carry

        lax.fori_loop(0, 16, drain, 0)

    @pl.when(primary)
    def _():
        def drain(k, carry):
            remote(land.at[k], land.at[k], f_send.at[k], x_recv.at[k], partner).wait_send()

            @pl.when(k != me_k)
            def _():
                remote(
                    dxs.at[k], dxl.at[z], dx_send.at[k], dx_recv.at[z],
                    dev(xl, y, xh, lax.div(k, 2), lax.rem(k, 2)),
                ).wait_send()

            return carry

        lax.fori_loop(0, 16, drain, 0)

    @pl.when(gives_rim)
    def _():
        for zt in range(8):
            rim_copy(zt).wait_send()

    for out in outs:
        out.wait()


def shards(video_clips, weights, conv_bias, cotangent):
    x = video_clips.reshape(384, 1024)
    w = weights.reshape(27, 32, 128)
    cot = cotangent.transpose(0, 1, 3, 2, 4).reshape(8, 48, 128)
    bias = conv_bias.reshape(1, 128)
    table = tap_gather()
    gat = jnp.asarray(table, BF16)
    sca = jnp.asarray(table.T, BF16)
    any_spec = pl.BlockSpec(memory_space=pl.ANY)
    vmem_spec = pl.BlockSpec(memory_space=pltpu.VMEM)

    def v(shape, dtype=BF16):
        return pltpu.VMEM(shape, dtype)

    def sems(n):
        return pltpu.SemaphoreType.DMA((n,))

    samp, dx, dw, db = pl.pallas_call(
        kernel,
        out_shape=[
            jax.ShapeDtypeStruct((8, 48, 128), BF16),
            jax.ShapeDtypeStruct((384, 1024), BF16),
            jax.ShapeDtypeStruct((27, 32, 128), F32),
            jax.ShapeDtypeStruct((1, 128), F32),
        ],
        in_specs=[any_spec] * 3 + [vmem_spec] * 3,
        out_specs=[any_spec] * 4,
        scratch_shapes=[
            v((384, 1024)),
            v((8, 384, 128)),
            v((16, 384, 128)),
            v((96, 128)),
            v((27, 128, 512)),
            v((2, 4, 48, 128)),
            v((8, 128), F32),
            v((4, 8, 128), F32),
            v((9, 32, 24, 128), F32),
            v((9, 33, 24, 128), F32),
            v((384, 512), F32),
            v((8, 96, 512)),
            v((16, 48, 512)),
            v((16, 48, 512)),
            v((2, 4, 48, 128)),
            v((8, 48, 128)),
            v((9, 96, 512)),
            v((8, 8, 128), F32),
            v((4, 8, 128), F32),
            v((16, 8, 128), F32),
            v((2, 9, 8, 24, 128), F32),
            v((16, 384, 128)),
            v((16, 384, 128)),
            v((16, 384, 128)),
            v((8, 384, 128)),
            v((384, 1024)),
            v((3, 2, 2, 9, 32, 512)),
            v((3, 2, 9, 32, 512)),
            v((3, 2, 9, 32, 512)),
            v((3, 4, 2, 9, 32, 128)),
            v((3, 9, 32, 128), F32),
            v((3, 9, 32, 128)),
            v((3, 9, 32, 128)),
            v((9, 32, 512)),
            v((9, 32, 512)),
            v((27, 32, 128), F32),
            v((1, 128), F32),
            sems(1), sems(8), sems(16), sems(16), sems(2),
            sems(16), sems(16), sems(8), sems(8), sems(4), sems(4),
            sems(16), sems(16), sems(8), sems(8), sems(14), sems(16), sems(8), sems(8),
            sems(8), sems(1), sems(16), sems(16), sems(16), sems(16), sems(16), sems(8),
            sems(3), sems(3), sems(12), sems(12), sems(3), sems(3), sems(4),
        ],
        compiler_params=pltpu.CompilerParams(
            collective_id=0, has_side_effects=True, vmem_limit_bytes=60 * 1024 * 1024
        ),
        cost_estimate=pl.CostEstimate(flops=10_000_000_000, bytes_accessed=8_000_000, transcendentals=50_000),
    )(x, w, cot, bias, gat, sca)
    sampled = samp.reshape(8, 2, 12, 2, 128).transpose(0, 1, 3, 2, 4)
    clip_grad = dx.reshape(1, 4, 4, 24, 1024)
    return sampled, clip_grad, dw.reshape(3, 3, 3, 32, 128), db.reshape(128)


def solution(mesh):
    return jax.shard_map(
        shards,
        mesh=mesh,
        in_specs=(
            P("dp", "tm", None, None, None),
            P(None, None, None, "tm", "dp"),
            P("dp"),
            P(None, "tm", None, None, "dp"),
        ),
        out_specs=(
            P(None, "tm", None, None, "dp"),
            P("dp", "tm", None, None, None),
            P(None, None, None, "tm", "dp"),
            P("dp"),
        ),
        check_vma=False,
    )
```

```python
import math

import jax
import jax.numpy as jnp
import numpy as np
from jax import lax
from jax.experimental import pallas as pl
from jax.experimental.pallas import tpu as pltpu
from jax.sharding import PartitionSpec as P

MESH = pl.DeviceIdType.MESH
F32 = jnp.float32
BF16 = jnp.bfloat16
POSITIONS = 12288


def tap_gather():
    table = np.zeros((224, 96), np.float32)
    for h in range(3):
        for w in range(3):
            for r in range(2):
                for q in range(12):
                    row, col = 2 * r + h - 1, 2 * q + w - 1
                    if 0 <= row < 4 and 0 <= col < 24:
                        table[(h * 3 + w) * 24 + q * 2 + r, row * 24 + col] = 1.0
    return table


def kernel(
    x_ref, w_ref, cot_ref, bias_ref, gat_ref, sca_ref,
    samp_out, dx_out, dw_out, db_out,
    xv, xp, land, halo, wg, cotl, biasb, biasl, im_e, im_o, pacc, part, rsl, rss, sbuf, sland, gbuf, bz, bs, bl,
    dtmp, dxb, dxp, dxs, dwb, dws, dwr, dwl, dwo, dwx, dwy, dwm, dwn, kout, dbo,
    v_sem, x_send, x_recv, f_send, h_sem, w_send, w_recv, c_send, c_recv, b_send, b_recv, rs_send, rs_recv,
    s_send, s_recv, ag_send, ag_recv, bz_send, bz_recv, gh_send, gh_recv, bs_send, bs_recv, dxp_send, dxp_recv,
    dx_send, dx_recv, k1_send, k1_recv, k2_send, k2_recv, k3_send, k3_recv, o_sem,
):
    dp, tm = lax.axis_index("dp"), lax.axis_index("tm")
    xl, y = lax.div(dp, 4), lax.rem(dp, 4)
    xh, z, c = lax.div(tm, 16), lax.rem(lax.div(tm, 2), 8), lax.rem(tm, 2)
    primary = c == xl
    inv = 1.0 / math.sqrt(POSITIONS)

    def dev(xl_, y_, xh_, z_, c_):
        return (xl_ * 4 + y_, (xh_ * 8 + z_) * 2 + c_)

    def remote(src, dst, send, recv, device):
        return pltpu.make_async_remote_copy(
            src_ref=src, dst_ref=dst, send_sem=send, recv_sem=recv, device_id=device, device_id_type=MESH
        )

    def landed(dst, sem):
        pltpu.make_async_copy(dst, dst, sem).wait()

    def plus(a, by, n):
        return lax.rem(a + by, n)

    partner = dev(1 - xl, y, xh, z, c)
    sibling = dev(xl, y, xh, z, 1 - c)
    across = dev(xl, y, 1 - xh, z, c)

    x_in = pltpu.make_async_copy(x_ref, xv, v_sem.at[0])
    x_in.start()

    barrier = pltpu.get_barrier_semaphore()
    peers = [partner]
    for dz in range(8):
        for dc in range(2):
            if dz or dc:
                peers.append(dev(xl, y, xh, plus(z, dz, 8), plus(c, dc, 2)))
    for dy in range(4):
        for dh in range(2):
            for dc in range(2):
                if dy or dh:
                    peers.append(dev(xl, plus(y, dy, 4), plus(xh, dh, 2), z, plus(c, dc, 2)))
    for dz in range(1, 8):
        peers.append(dev(xl, y, 1 - xh, plus(z, dz, 8), c))
    for peer in peers:
        pl.semaphore_signal(barrier, inc=1, device_id=peer, device_id_type=MESH)

    biasb[...] = jnp.broadcast_to(bias_ref[...], (8, 128))
    x_in.wait()
    for zt in range(8):
        at = (zt // 2) * 128 + (zt % 2) * 64
        xp[zt] = jnp.concatenate([xv[:, at:at + 64], xv[:, 512 + at:512 + at + 64]], axis=1)
    pl.semaphore_wait(barrier, len(peers))

    ends = []

    me_k = 2 * z + c
    for n, dz in enumerate((4, 3, 5, 2, 6, 1, 7)):
        zt = plus(z, dz, 8)
        copy = remote(xp.at[zt], land.at[me_k], x_send.at[n], x_recv.at[me_k], dev(xl, y, xh, zt, xl))
        copy.start()
        ends.append(copy.wait_send)
    own_x = pltpu.make_async_copy(xp.at[z], land.at[me_k], x_recv.at[me_k])
    sib_x = remote(xp.at[z], land.at[me_k], x_send.at[7], x_recv.at[me_k], dev(xl, y, xh, z, 1 - c))

    @pl.when(primary)
    def _():
        own_x.start()

    @pl.when(jnp.logical_not(primary))
    def _():
        sib_x.start()

    def w_at(h_, c_, y_):
        return wg.at[:, pl.ds(pl.multiple_of((h_ * 2 + c_) * 32, 32), 32), pl.ds(pl.multiple_of(y_ * 128, 128), 128)]

    def w_sem(h_, c_, y_):
        return w_recv.at[(h_ * 2 + c_) * 4 + y_]

    w_count = [0]

    def w_push(src, h_, c_, y_, device):
        copy = remote(src, w_at(h_, c_, y_), w_send.at[w_count[0]], w_sem(h_, c_, y_), device)
        w_count[0] += 1
        copy.start()
        ends.append(copy.wait_send)

    up, down = plus(y, 1, 4), plus(y, 3, 4)
    dev_up, dev_down = dev(xl, up, xh, z, c), dev(xl, down, xh, z, c)
    w_push(w_ref, xh, c, y, across)
    w_push(w_ref, xh, c, y, dev_up)
    w_push(w_ref, xh, c, y, dev_down)
    w_push(w_ref, xh, c, y, sibling)
    pltpu.make_async_copy(w_ref, w_at(xh, c, y), w_sem(xh, c, y)).start()

    for dy in range(4):
        for dc in range(2):
            yd, cd = plus(y, dy, 4), plus(c, dc, 2)
            src, dst, sem = cot_ref.at[cd * 4 + yd], cotl.at[c, y], c_recv.at[c * 4 + y]
            if dy or dc:
                copy = remote(src, dst, c_send.at[dy * 2 + dc], sem, dev(xl, yd, xh, z, cd))
                copy.start()
                ends.append(copy.wait_send)
            else:
                pltpu.make_async_copy(src, dst, sem).start()
    pltpu.make_async_copy(biasb, biasl.at[y], b_recv.at[y]).start()
    for dy in range(1, 4):
        copy = remote(biasb, biasl.at[y], b_send.at[dy], b_recv.at[y], dev(xl, plus(y, dy, 4), xh, z, c))
        copy.start()
        ends.append(copy.wait_send)

    halo_copy = remote(land.at[15, pl.ds(288, 96)], halo, h_sem.at[0], h_sem.at[1], across)
    ends.append(halo_copy.wait_send)

    def place_of(j):
        far = jnp.where(lax.rem(j, 2) == 0, 4 - lax.div(j, 2), 4 + lax.div(j, 2))
        return plus(z, jnp.where(j == 0, 0, far), 8)

    def pass_on(first, last):
        @pl.when(primary)
        def _():
            def one(i, carry):
                k = 2 * place_of(lax.div(i, 2)) + lax.rem(i, 2)
                landed(land.at[k], x_recv.at[k])
                remote(land.at[k], land.at[k], f_send.at[k], x_recv.at[k], partner).start()
                return carry

            lax.fori_loop(2 * first, 2 * last, one, 0)

    def take_in(first, last):
        def one(i, carry):
            k = 2 * place_of(lax.div(i, 2)) + lax.rem(i, 2)

            @pl.when(jnp.logical_not(primary))
            def _():
                landed(land.at[k], x_recv.at[k])

            @pl.when(k == 15)
            def _():
                halo_copy.start()

            frames = land[k]
            side = jnp.concatenate([frames[i * 96:(i + 1) * 96] for i in range(4)], axis=1)
            taps = jnp.dot(gat_ref[...], side, preferred_element_type=F32)
            for f in range(4):
                piece = taps[:216, f * 128:(f + 1) * 128].reshape(9, 24, 128)
                if f % 2 == 0:
                    im_e[:, 2 * k + f // 2] = piece
                else:
                    im_o[:, 2 * k + 1 + f // 2] = piece
            return carry

        lax.fori_loop(2 * first, 2 * last, one, 0)

    def spread(first, last):
        pass_on(first, last)
        take_in(first, last)

    def w_pass(h_, y_, device):
        landed(w_at(h_, c, y_), w_sem(h_, c, y_))
        if device is not None:
            w_push(w_at(h_, c, y_), h_, c, y_, device)
        w_push(w_at(h_, c, y_), h_, c, y_, sibling)

    spread(0, 1)
    w_pass(1 - xh, y, dev_up)
    w_push(w_at(1 - xh, c, y), 1 - xh, c, y, dev_down)
    spread(1, 2)
    w_pass(xh, down, dev_up)
    w_pass(xh, up, None)
    spread(2, 4)
    w_pass(1 - xh, up, dev_down)
    w_pass(1 - xh, down, None)
    spread(4, 6)
    pass_on(6, 8)
    w_pass(xh, plus(y, 2, 4), None)
    w_pass(1 - xh, plus(y, 2, 4), None)
    landed(w_at(xh, c, y), w_sem(xh, c, y))
    for dy in range(4):
        for h_ in (xh, 1 - xh):
            yd = plus(y, dy, 4)
            landed(w_at(h_, 1 - c, yd), w_sem(h_, 1 - c, yd))

    def z_at(dz):
        return plus(z, dz % 8, 8)

    def forward(dzs):
        zts = [z_at(dz) for dz in dzs]
        size = 96 * len(zts)
        for zt in zts:
            @pl.when(zt == 0)
            def _():
                landed(halo, h_sem.at[1])
                rim = jnp.dot(gat_ref[...], halo[...], preferred_element_type=F32)[:216].reshape(9, 24, 128)
                im_o[:, 0] = jnp.where(xh == 1, rim, jnp.zeros_like(rim))

        def rows(held, hw, by):
            return jnp.concatenate([held[hw, pl.ds(4 * zt + by, 4)].reshape(96, 128) for zt in zts], axis=0).astype(BF16)

        def step(h, carry):
            lhs, rhs = [], []
            for w in range(3):
                hw = h * 3 + w
                lhs += [rows(im_o, hw, 0), rows(im_e, hw, 0), rows(im_o, hw, 1)]
                rhs += [wg[hw], wg[9 + hw], wg[18 + hw]]
            pacc[0:size] += jnp.dot(
                jnp.concatenate(lhs, axis=1), jnp.concatenate(rhs, axis=0), preferred_element_type=F32
            )
            return carry

        pacc[0:size] = jnp.zeros((size, 512), F32)
        lax.fori_loop(0, 3, step, 0)
        for q, dz in enumerate(dzs):
            zt = zts[q]
            part[zt] = pacc[q * 96:(q + 1) * 96].astype(BF16)

    next_z, last_z = dev(xl, y, xh, plus(z, 1, 8), c), dev(xl, y, xh, plus(z, 7, 8), c)

    def rs_hop(way, step, half):
        zt = z_at((5 - step) * (1 - 2 * way))
        at = (way * 4 + step - 1) * 2 + half
        own = part[zt, half * 48:(half + 1) * 48]
        if step > 1 and (step > 2 or half == way):
            before = at - 2
            landed(rsl.at[before], rs_recv.at[before])
            own = (own.astype(F32) + rsl[before].astype(F32)).astype(BF16)
        rss[at] = own
        copy = remote(rss.at[at], rsl.at[at], rs_send.at[at], rs_recv.at[at], last_z if way else next_z)
        copy.start()
        ends.append(copy.wait_send)

    def rs_step(step):
        for half in range(2):
            for way in range(2):
                if step > 1 or half == way:
                    rs_hop(way, step, half)

    forward((4, -3))
    rs_step(1)
    forward((3, -2))
    take_in(6, 8)
    rs_step(2)
    forward((2, -1, 1))
    rs_step(3)
    forward((0,))
    rs_step(4)

    for dy in range(4):
        yd = plus(y, dy, 4)
        landed(biasl.at[yd], b_recv.at[yd])
        for cs in range(2):
            landed(cotl.at[cs, yd], c_recv.at[cs * 4 + yd])
    pre = part[z].astype(F32)
    sums_in = []
    for way in range(2):
        for half in range(2):
            at = (way * 4 + 3) * 2 + half
            landed(rsl.at[at], rs_recv.at[at])
        sums_in.append(jnp.concatenate([rsl[way * 8 + 6], rsl[way * 8 + 7]], axis=0).astype(F32))
    pre = pre + sums_in[0] + sums_in[1]
    pre = pre + jnp.concatenate([biasl[i, 0:1] for i in range(4)], axis=1)
    sig = 1.0 / (1.0 + jnp.exp(-pre))
    samp = (pre * sig).astype(BF16)
    cot = jnp.concatenate(
        [jnp.concatenate([cotl[cs, i] for i in range(4)], axis=1) for cs in range(2)], axis=0
    ).astype(F32)
    slope = cot * sig * (1.0 + pre * (1.0 - sig))
    gbuf[z] = slope.astype(BF16)
    def g_at(o, half):
        return gbuf.at[o, pl.ds(half * 48, 48)]

    ag_count = [0]

    def ag_push(o, half, device):
        copy = remote(g_at(o, half), g_at(o, half), ag_send.at[ag_count[0]], ag_recv.at[o * 2 + half], device)
        ag_count[0] += 1
        copy.start()
        ends.append(copy.wait_send)

    for half in range(2):
        ag_push(z, half, next_z)
        ag_push(z, half, last_z)

    def rim_copy(zt):
        return remote(
            gbuf.at[0, pl.ds(0, 32)], gbuf.at[8, pl.ds(0, 32)], gh_send.at[zt], gh_recv.at[0], dev(xl, y, 0, zt, c)
        )

    gives_rim = jnp.logical_and(z == 0, xh == 1)

    @pl.when(gives_rim)
    def _():
        for zt in range(8):
            rim_copy(zt).start()

    @pl.when(xh == 1)
    def _():
        gbuf[8, pl.ds(0, 32)] = jnp.zeros((32, 512), BF16)

    sums = jnp.sum(slope, axis=0, keepdims=True)
    bz[z] = jnp.concatenate([sums[:, i * 128:(i + 1) * 128] for i in range(4)] + [jnp.zeros((4, 128), F32)], axis=0)
    for n, dz in enumerate((1, 7, 2, 6, 3, 5, 4)):
        copy = remote(bz.at[z], bz.at[z], bz_send.at[n], bz_recv.at[z], dev(xl, y, xh, plus(z, dz, 8), c))
        copy.start()
        ends.append(copy.wait_send)
    for cs in range(2):
        for i in range(4):
            sbuf[cs, i] = samp[cs * 48:(cs + 1) * 48, i * 128:(i + 1) * 128]
    for dy in range(4):
        for dc in range(2):
            yd, cd = plus(y, dy, 4), plus(c, dc, 2)
            src, dst, sem = sbuf.at[cd, yd], sland.at[c * 4 + y], s_recv.at[c * 4 + y]
            if dy or dc:
                copy = remote(src, dst, s_send.at[dy * 2 + dc], sem, dev(xl, yd, xh, z, cd))
                copy.start()
                ends.append(copy.wait_send)
            else:
                pltpu.make_async_copy(src, dst, sem).start()

    def back_pair(first, second):
        def back(h, carry):
            hws = [h * 3 + w for w in range(3)]
            mats = jnp.concatenate([wg[t * 9 + hw] for hw in hws for t in range(3)], axis=0)
            rows = jnp.concatenate(
                [gbuf[first], gbuf[first + 1, 0:32], gbuf[second], gbuf[second + 1, 0:32]], axis=0
            )
            r = lax.dot_general(rows, mats, (((1,), (1,)), ((), ())), preferred_element_type=F32)
            for w in range(3):
                at = w * 384
                for i in range(2):
                    p = r[i * 128:i * 128 + 128]
                    dtmp[i, h * 3 + w, 0:4] = p[:96, at + 128:at + 256].reshape(4, 24, 128)
                    dtmp[i, h * 3 + w, 4:8] = (p[:96, at + 256:at + 384] + p[24:120, at:at + 128]).reshape(4, 24, 128)
            return carry

        lax.fori_loop(0, 3, back, 0)

        def place(i, carry):
            zc = jnp.where(i == 0, first, second)
            cols = [dtmp[i, :, f + 4 * odd].reshape(216, 128) for f in range(4) for odd in range(2)]
            side = jnp.concatenate(cols, axis=1)
            side = jnp.concatenate([side, jnp.zeros((8, 1024), F32)], axis=0).astype(BF16)
            r = jnp.dot(sca_ref[...], side, preferred_element_type=F32).astype(BF16)
            for cs in range(2):
                k = 2 * zc + cs
                for f in range(4):
                    dxb[k, pl.ds(f * 96, 96)] = r[:, (cs * 4 + f) * 128:(cs * 4 + f + 1) * 128]

                @pl.when(jnp.logical_not(primary))
                def _(k=k):
                    remote(dxb.at[k], dxp.at[k], dxp_send.at[k], dxp_recv.at[k], partner).start()
            return carry

        lax.fori_loop(0, 2, place, 0)

    def send_back(k):
        landed(dxp.at[k], dxp_recv.at[k])
        dxs[k] = (dxb[k].astype(F32) + dxp[k].astype(F32)).astype(BF16)

        @pl.when(k == me_k)
        def _():
            pltpu.make_async_copy(dxs.at[k], dx_out.at[z], dx_recv.at[z]).start()

        @pl.when(k != me_k)
        def _():
            remote(
                dxs.at[k], dx_out.at[z], dx_send.at[k], dx_recv.at[z], dev(xl, y, xh, lax.div(k, 2), lax.rem(k, 2))
            ).start()

    def finish_pair(first, second):
        @pl.when(primary)
        def _():
            def one(i, carry):
                zc = jnp.where(i < 2, first, second)
                send_back(2 * zc + lax.rem(i, 2))
                return carry

            lax.fori_loop(0, 4, one, 0)

    for step in range(1, 4):
        below, above = z_at(-step), z_at(step)
        for half in range(2):
            landed(g_at(below, half), ag_recv.at[below * 2 + half])
            if step < 3 or half == 0:
                ag_push(below, half, next_z)
            landed(g_at(above, half), ag_recv.at[above * 2 + half])
            if step < 3 or half == 1:
                ag_push(above, half, last_z)
        if step == 1:
            @pl.when(xh == 0)
            def _():
                landed(gbuf.at[8, pl.ds(0, 32)], gh_recv.at[0])

        back_pair(z_at(step - 1), z_at(-step))
        if step > 1:
            finish_pair(z_at(step - 2), z_at(1 - step))
    for half in range(2):
        landed(g_at(z_at(4), half), ag_recv.at[z_at(4) * 2 + half])

    def weight_grad(h):
        def grad_step(w, carry):
            hw = h * 3 + w
            lhs = jnp.concatenate(
                [
                    im_o[hw, pl.ds(0, 32)].reshape(768, 128).astype(BF16),
                    im_e[hw].reshape(768, 128).astype(BF16),
                    im_o[hw, pl.ds(1, 32)].reshape(768, 128).astype(BF16),
                ],
                axis=1,
            )
            r = lax.dot_general(
                lhs, gbuf[0:8].reshape(768, 512), (((0,), (0,)), ((), ())), preferred_element_type=F32
            ).astype(BF16)
            for t in range(3):
                for h_ in range(2):
                    for c_ in range(2):
                        at = t * 128 + h_ * 64 + c_ * 32
                        dwb[h, c_, h_, w * 3 + t] = r[at:at + 32]
            return carry

        lax.fori_loop(0, 3, grad_step, 0)
        copy = remote(dwb.at[h, 1 - c], dws.at[h], k1_send.at[h], k1_recv.at[h], sibling)
        copy.start()
        ends.append(copy.wait_send)

    def core_sum(h):
        landed(dws.at[h], k1_recv.at[h])

        def add_step(n, carry):
            for h_ in range(2):
                dwr[h, h_, n] = (dwb[h, c, h_, n].astype(F32) + dws[h, h_, n].astype(F32)).astype(BF16)
            return carry

        lax.fori_loop(0, 9, add_step, 0)

    def y_lanes(i):
        return pl.ds(pl.multiple_of(i * 128, 128), 128)

    def to_y(h):
        core_sum(h)
        for dy in range(4):
            yd = plus(y, dy, 4)
            src = dwr.at[h, :, :, :, y_lanes(yd)]
            dst, sem = dwl.at[h, y], k2_recv.at[h * 4 + y]
            if dy:
                copy = remote(src, dst, k2_send.at[h * 4 + dy], sem, dev(xl, yd, xh, z, c))
                copy.start()
                ends.append(copy.wait_send)
            else:
                pltpu.make_async_copy(src, dst, sem).start()

    def y_to_x(h):
        for i in range(4):
            landed(dwl.at[h, i], k2_recv.at[h * 4 + i])

        def add_step(n, carry):
            own, other = dwl[h, 0, xh, n].astype(F32), dwl[h, 0, 1 - xh, n].astype(F32)
            for i in range(1, 4):
                own = own + dwl[h, i, xh, n].astype(F32)
                other = other + dwl[h, i, 1 - xh, n].astype(F32)
            dwo[h, n] = own
            dwx[h, n] = other.astype(BF16)
            return carry

        lax.fori_loop(0, 9, add_step, 0)
        copy = remote(dwx.at[h], dwy.at[h], k3_send.at[h], k3_recv.at[h], across)
        copy.start()
        ends.append(copy.wait_send)

    def to_x(h):
        core_sum(h)
        copy = remote(dwr.at[h, 1 - xh], dwm, k3_send.at[h], k3_recv.at[h], across)
        copy.start()
        ends.append(copy.wait_send)

    def x_to_y(h):
        landed(dwm, k3_recv.at[h])

        def add_step(n, carry):
            dwn[n] = (dwr[h, xh, n].astype(F32) + dwm[n].astype(F32)).astype(BF16)
            return carry

        lax.fori_loop(0, 9, add_step, 0)
        for dy in range(4):
            yd = plus(y, dy, 4)
            src = dwn.at[:, :, y_lanes(yd)]
            dst, sem = dwl.at[h, y, 0], k2_recv.at[h * 4 + y]
            if dy:
                copy = remote(src, dst, k2_send.at[h * 4 + dy], sem, dev(xl, yd, xh, z, c))
                copy.start()
                ends.append(copy.wait_send)
            else:
                pltpu.make_async_copy(src, dst, sem).start()

    weight_grad(0)
    back_pair(z_at(3), z_at(4))
    to_y(0)
    finish_pair(z_at(2), z_at(-3))
    weight_grad(1)
    weight_grad(2)
    finish_pair(z_at(3), z_at(4))
    to_x(1)
    to_y(2)
    y_to_x(0)
    x_to_y(1)

    total = bz[z]
    for dz in (1, 7, 2, 6, 3, 5, 4):
        zs = plus(z, dz, 8)
        landed(bz.at[zs], bz_recv.at[zs])
        total = total + bz[zs]
    for i in range(4):
        bs[i] = jnp.broadcast_to(total[i:i + 1], (8, 128))
    slot_b = (xh * 2 + c) * 4 + y
    for dy in range(4):
        for dh in range(2):
            for dc in range(2):
                yd, hd, cd = plus(y, dy, 4), plus(xh, dh, 2), plus(c, dc, 2)
                if dy or dh or dc:
                    copy = remote(
                        bs.at[yd], bl.at[slot_b], bs_send.at[(dy * 2 + dh) * 2 + dc], bs_recv.at[slot_b],
                        dev(xl, yd, hd, z, cd),
                    )
                    copy.start()
                    ends.append(copy.wait_send)
                else:
                    pltpu.make_async_copy(bs.at[y], bl.at[slot_b], bs_recv.at[slot_b]).start()

    outs = []
    for i in range(8):
        landed(sland.at[i], s_recv.at[i])
    outs.append(pltpu.make_async_copy(sland, samp_out, o_sem.at[0]))
    outs[-1].start()

    y_to_x(2)
    for i in range(4):
        landed(dwl.at[1, i, 0], k2_recv.at[4 + i])

    def sum_middle(w, carry):
        for t in range(3):
            acc = dwl[1, 0, 0, w * 3 + t].astype(F32)
            for i in range(1, 4):
                acc = acc + dwl[1, i, 0, w * 3 + t].astype(F32)
            kout[t * 9 + 3 + w] = acc * inv
        return carry

    lax.fori_loop(0, 3, sum_middle, 0)
    for h in (0, 2):
        landed(dwy.at[h], k3_recv.at[h])

        def sum_step(w, carry, h=h):
            for t in range(3):
                kout[t * 9 + h * 3 + w] = (dwo[h, w * 3 + t] + dwy[h, w * 3 + t].astype(F32)) * inv
            return carry

        lax.fori_loop(0, 3, sum_step, 0)
    outs.append(pltpu.make_async_copy(kout, dw_out, o_sem.at[1]))
    outs[-1].start()

    acc = None
    for i in range(16):
        landed(bl.at[i], bs_recv.at[i])
        acc = bl[i] if acc is None else acc + bl[i]
    dbo[...] = acc[0:1] * inv
    outs.append(pltpu.make_async_copy(dbo, db_out, o_sem.at[2]))
    outs[-1].start()

    for i in range(8):
        landed(dx_out.at[i], dx_recv.at[i])

    for end in ends:
        end()

    @pl.when(jnp.logical_not(primary))
    def _():
        sib_x.wait_send()

        def drain(k, carry):
            remote(dxb.at[k], dxp.at[k], dxp_send.at[k], dxp_recv.at[k], partner).wait_send()
            return carry

        lax.fori_loop(0, 16, drain, 0)

    @pl.when(primary)
    def _():
        def drain(k, carry):
            remote(land.at[k], land.at[k], f_send.at[k], x_recv.at[k], partner).wait_send()

            @pl.when(k != me_k)
            def _():
                remote(
                    dxs.at[k], dx_out.at[z], dx_send.at[k], dx_recv.at[z],
                    dev(xl, y, xh, lax.div(k, 2), lax.rem(k, 2)),
                ).wait_send()

            return carry

        lax.fori_loop(0, 16, drain, 0)

    @pl.when(gives_rim)
    def _():
        for zt in range(8):
            rim_copy(zt).wait_send()

    for out in outs:
        out.wait()


def finisher(samp_in, dx_in, dw_in, db_in, samp_out, dx_out, dw_out, db_out, held, made, in_sem, out_sem):
    loads = [pltpu.make_async_copy(dx_in.at[i], held.at[i], in_sem.at[i]) for i in range(8)]
    for copy in loads:
        copy.start()
    samp_out[...] = samp_in[...]
    dw_out[...] = dw_in[...]
    db_out[...] = db_in[...]
    stores = []
    for m in range(4):
        loads[2 * m].wait()
        loads[2 * m + 1].wait()
        a, b = held[2 * m], held[2 * m + 1]
        for half in range(2):
            cols = pl.ds(half * 512 + m * 128, 128)
            made[:, cols] = jnp.concatenate(
                [a[:, half * 64:half * 64 + 64], b[:, half * 64:half * 64 + 64]], axis=1
            )
            copy = pltpu.make_async_copy(made.at[:, cols], dx_out.at[:, cols], out_sem.at[2 * m + half])
            copy.start()
            stores.append(copy)
    for copy in stores:
        copy.wait()


def shards(video_clips, weights, conv_bias, cotangent):
    x = video_clips.reshape(384, 1024)
    w = weights.reshape(27, 32, 128)
    cot = cotangent.transpose(0, 1, 3, 2, 4).reshape(8, 48, 128)
    bias = conv_bias.reshape(1, 128)
    table = tap_gather()
    gat = jnp.asarray(table, BF16)
    sca = jnp.asarray(table.T, BF16)
    any_spec = pl.BlockSpec(memory_space=pl.ANY)
    vmem_spec = pl.BlockSpec(memory_space=pltpu.VMEM)

    def v(shape, dtype=BF16):
        return pltpu.VMEM(shape, dtype)

    def sems(n):
        return pltpu.SemaphoreType.DMA((n,))

    samp, dx, dw, db = pl.pallas_call(
        kernel,
        out_shape=[
            jax.ShapeDtypeStruct((8, 48, 128), BF16),
            jax.ShapeDtypeStruct((8, 384, 128), BF16),
            jax.ShapeDtypeStruct((27, 32, 128), F32),
            jax.ShapeDtypeStruct((1, 128), F32),
        ],
        in_specs=[any_spec] * 3 + [vmem_spec] * 3,
        out_specs=[any_spec] * 4,
        scratch_shapes=[
            v((384, 1024)),
            v((8, 384, 128)),
            v((16, 384, 128)),
            v((96, 128)),
            v((27, 128, 512)),
            v((2, 4, 48, 128)),
            v((8, 128), F32),
            v((4, 8, 128), F32),
            v((9, 32, 24, 128), F32),
            v((9, 33, 24, 128), F32),
            v((384, 512), F32),
            v((8, 96, 512)),
            v((16, 48, 512)),
            v((16, 48, 512)),
            v((2, 4, 48, 128)),
            v((8, 48, 128)),
            v((9, 96, 512)),
            v((8, 8, 128), F32),
            v((4, 8, 128), F32),
            v((16, 8, 128), F32),
            v((2, 9, 8, 24, 128), F32),
            v((16, 384, 128)),
            v((16, 384, 128)),
            v((16, 384, 128)),
            v((3, 2, 2, 9, 32, 512)),
            v((3, 2, 9, 32, 512)),
            v((3, 2, 9, 32, 512)),
            v((3, 4, 2, 9, 32, 128)),
            v((3, 9, 32, 128), F32),
            v((3, 9, 32, 128)),
            v((3, 9, 32, 128)),
            v((9, 32, 512)),
            v((9, 32, 512)),
            v((27, 32, 128), F32),
            v((1, 128), F32),
            sems(1), sems(8), sems(16), sems(16), sems(2),
            sems(16), sems(16), sems(8), sems(8), sems(4), sems(4),
            sems(16), sems(16), sems(8), sems(8), sems(14), sems(16), sems(8), sems(8),
            sems(8), sems(1), sems(16), sems(16), sems(16), sems(16), sems(16), sems(8),
            sems(3), sems(3), sems(12), sems(12), sems(3), sems(3), sems(4),
        ],
        compiler_params=pltpu.CompilerParams(
            collective_id=0, has_side_effects=True, vmem_limit_bytes=60 * 1024 * 1024
        ),
        cost_estimate=pl.CostEstimate(flops=10_000_000_000, bytes_accessed=8_000_000, transcendentals=50_000),
    )(x, w, cot, bias, gat, sca)
    samp, dx, dw, db = pl.pallas_call(
        finisher,
        out_shape=[
            jax.ShapeDtypeStruct((8, 48, 128), BF16),
            jax.ShapeDtypeStruct((384, 1024), BF16),
            jax.ShapeDtypeStruct((27, 32, 128), F32),
            jax.ShapeDtypeStruct((1, 128), F32),
        ],
        in_specs=[vmem_spec, any_spec, vmem_spec, vmem_spec],
        out_specs=[vmem_spec, any_spec, vmem_spec, vmem_spec],
        scratch_shapes=[v((8, 384, 128)), v((384, 1024)), sems(8), sems(8)],
        cost_estimate=pl.CostEstimate(flops=0, bytes_accessed=3_000_000, transcendentals=0),
    )(samp, dx, dw, db)
    sampled = samp.reshape(8, 2, 12, 2, 128).transpose(0, 1, 3, 2, 4)
    clip_grad = dx.reshape(1, 4, 4, 24, 1024)
    return sampled, clip_grad, dw.reshape(3, 3, 3, 32, 128), db.reshape(128)


def solution(mesh):
    return jax.shard_map(
        shards,
        mesh=mesh,
        in_specs=(
            P("dp", "tm", None, None, None),
            P(None, None, None, "tm", "dp"),
            P("dp"),
            P(None, "tm", None, None, "dp"),
        ),
        out_specs=(
            P(None, "tm", None, None, "dp"),
            P("dp", "tm", None, None, None),
            P(None, None, None, "tm", "dp"),
            P("dp"),
        ),
        check_vma=False,
    )
```

```python
import math

import jax
import jax.numpy as jnp
import numpy as np
from jax import lax
from jax.experimental import pallas as pl
from jax.experimental.pallas import tpu as pltpu
from jax.sharding import PartitionSpec as P

MESH = pl.DeviceIdType.MESH
F32 = jnp.float32
BF16 = jnp.bfloat16
POSITIONS = 12288


def tap_gather():
    table = np.zeros((224, 96), np.float32)
    for h in range(3):
        for w in range(3):
            for r in range(2):
                for q in range(12):
                    row, col = 2 * r + h - 1, 2 * q + w - 1
                    if 0 <= row < 4 and 0 <= col < 24:
                        table[(h * 3 + w) * 24 + q * 2 + r, row * 24 + col] = 1.0
    return table


def kernel(
    x_ref, w_ref, cot_ref, bias_ref, gat_ref, sca_ref,
    samp_out, dx_out, dw_out, db_out,
    xv, xp, land, halo, wg, cotl, biasb, biasl, im_e, im_o, pacc, part, rsl, rss, sbuf, sland, gbuf, bz, bs, bl,
    dtmp, dxb, dxp, dxs, dwb, dws, dwr, dwl, dwo, dwx, dwy, dwm, dwn, kout, dbo,
    v_sem, x_send, x_recv, f_send, h_sem, w_send, w_recv, c_send, c_recv, b_send, b_recv, rs_send, rs_recv,
    s_send, s_recv, ag_send, ag_recv, bz_send, bz_recv, gh_send, gh_recv, bs_send, bs_recv, dxp_send, dxp_recv,
    dx_send, dx_recv, k1_send, k1_recv, k2_send, k2_recv, k3_send, k3_recv, o_sem,
):
    dp, tm = lax.axis_index("dp"), lax.axis_index("tm")
    xl, y = lax.div(dp, 4), lax.rem(dp, 4)
    xh, z, c = lax.div(tm, 16), lax.rem(lax.div(tm, 2), 8), lax.rem(tm, 2)
    primary = c == xl
    inv = 1.0 / math.sqrt(POSITIONS)

    def dev(xl_, y_, xh_, z_, c_):
        return (xl_ * 4 + y_, (xh_ * 8 + z_) * 2 + c_)

    def remote(src, dst, send, recv, device):
        return pltpu.make_async_remote_copy(
            src_ref=src, dst_ref=dst, send_sem=send, recv_sem=recv, device_id=device, device_id_type=MESH
        )

    def landed(dst, sem):
        pltpu.make_async_copy(dst, dst, sem).wait()

    def plus(a, by, n):
        return lax.rem(a + by, n)

    partner = dev(1 - xl, y, xh, z, c)
    sibling = dev(xl, y, xh, z, 1 - c)
    across = dev(xl, y, 1 - xh, z, c)

    x_in = pltpu.make_async_copy(x_ref, xv, v_sem.at[0])
    x_in.start()

    barrier = pltpu.get_barrier_semaphore()
    peers = [partner]
    for dz in range(8):
        for dc in range(2):
            if dz or dc:
                peers.append(dev(xl, y, xh, plus(z, dz, 8), plus(c, dc, 2)))
    for dy in range(4):
        for dh in range(2):
            for dc in range(2):
                if dy or dh:
                    peers.append(dev(xl, plus(y, dy, 4), plus(xh, dh, 2), z, plus(c, dc, 2)))
    for dz in range(1, 8):
        peers.append(dev(xl, y, 1 - xh, plus(z, dz, 8), c))
    for peer in peers:
        pl.semaphore_signal(barrier, inc=1, device_id=peer, device_id_type=MESH)

    biasb[...] = jnp.broadcast_to(bias_ref[...], (8, 128))
    x_in.wait()
    for zt in range(8):
        at = (zt // 2) * 128 + (zt % 2) * 64
        xp[zt] = jnp.concatenate([xv[:, at:at + 64], xv[:, 512 + at:512 + at + 64]], axis=1)
    pl.semaphore_wait(barrier, len(peers))

    ends = []

    me_k = 2 * z + c
    for n, dz in enumerate((1, 7, 4, 3, 5, 2, 6)):
        zt = plus(z, dz, 8)
        copy = remote(xp.at[zt], land.at[me_k], x_send.at[n], x_recv.at[me_k], dev(xl, y, xh, zt, xl))
        copy.start()
        ends.append(copy.wait_send)
    own_x = pltpu.make_async_copy(xp.at[z], land.at[me_k], x_recv.at[me_k])
    sib_x = remote(xp.at[z], land.at[me_k], x_send.at[7], x_recv.at[me_k], dev(xl, y, xh, z, 1 - c))

    @pl.when(primary)
    def _():
        own_x.start()

    @pl.when(jnp.logical_not(primary))
    def _():
        sib_x.start()

    def w_at(h_, c_, y_):
        return wg.at[:, pl.ds(pl.multiple_of((h_ * 2 + c_) * 32, 32), 32), pl.ds(pl.multiple_of(y_ * 128, 128), 128)]

    def w_sem(h_, c_, y_):
        return w_recv.at[(h_ * 2 + c_) * 4 + y_]

    w_count = [0]

    def w_push(src, h_, c_, y_, device):
        copy = remote(src, w_at(h_, c_, y_), w_send.at[w_count[0]], w_sem(h_, c_, y_), device)
        w_count[0] += 1
        copy.start()
        ends.append(copy.wait_send)

    up, down = plus(y, 1, 4), plus(y, 3, 4)
    dev_up, dev_down = dev(xl, up, xh, z, c), dev(xl, down, xh, z, c)
    w_push(w_ref, xh, c, y, across)
    w_push(w_ref, xh, c, y, dev_up)
    w_push(w_ref, xh, c, y, dev_down)
    w_push(w_ref, xh, c, y, sibling)
    pltpu.make_async_copy(w_ref, w_at(xh, c, y), w_sem(xh, c, y)).start()

    for dy in range(4):
        for dc in range(2):
            yd, cd = plus(y, dy, 4), plus(c, dc, 2)
            src, dst, sem = cot_ref.at[cd * 4 + yd], cotl.at[c, y], c_recv.at[c * 4 + y]
            if dy or dc:
                copy = remote(src, dst, c_send.at[dy * 2 + dc], sem, dev(xl, yd, xh, z, cd))
                copy.start()
                ends.append(copy.wait_send)
            else:
                pltpu.make_async_copy(src, dst, sem).start()
    pltpu.make_async_copy(biasb, biasl.at[y], b_recv.at[y]).start()
    for dy in range(1, 4):
        copy = remote(biasb, biasl.at[y], b_send.at[dy], b_recv.at[y], dev(xl, plus(y, dy, 4), xh, z, c))
        copy.start()
        ends.append(copy.wait_send)

    halo_copy = remote(land.at[15, pl.ds(288, 96)], halo, h_sem.at[0], h_sem.at[1], across)
    ends.append(halo_copy.wait_send)

    def place_of(j):
        dz = 0
        dz = jnp.where(j == 1, 1, dz)
        dz = jnp.where(j == 2, 7, dz)
        dz = jnp.where(j == 3, 4, dz)
        dz = jnp.where(j == 4, 3, dz)
        dz = jnp.where(j == 5, 5, dz)
        dz = jnp.where(j == 6, 2, dz)
        dz = jnp.where(j == 7, 6, dz)
        return plus(z, dz, 8)

    def pass_on(first, last):
        @pl.when(primary)
        def _():
            def one(i, carry):
                k = 2 * place_of(lax.div(i, 2)) + lax.rem(i, 2)
                landed(land.at[k], x_recv.at[k])
                remote(land.at[k], land.at[k], f_send.at[k], x_recv.at[k], partner).start()
                return carry

            lax.fori_loop(2 * first, 2 * last, one, 0)

    def take_in(first, last):
        def one(i, carry):
            k = 2 * place_of(lax.div(i, 2)) + lax.rem(i, 2)

            @pl.when(jnp.logical_not(primary))
            def _():
                landed(land.at[k], x_recv.at[k])

            @pl.when(k == 15)
            def _():
                halo_copy.start()

            frames = land[k]
            side = jnp.concatenate([frames[i * 96:(i + 1) * 96] for i in range(4)], axis=1)
            taps = jnp.dot(gat_ref[...], side, preferred_element_type=F32)
            for f in range(4):
                piece = taps[:216, f * 128:(f + 1) * 128].reshape(9, 24, 128)
                if f % 2 == 0:
                    im_e[:, 2 * k + f // 2] = piece
                else:
                    im_o[:, 2 * k + 1 + f // 2] = piece
            return carry

        lax.fori_loop(2 * first, 2 * last, one, 0)

    def spread(first, last):
        pass_on(first, last)
        take_in(first, last)

    def w_pass(h_, y_, device):
        landed(w_at(h_, c, y_), w_sem(h_, c, y_))
        if device is not None:
            w_push(w_at(h_, c, y_), h_, c, y_, device)
        w_push(w_at(h_, c, y_), h_, c, y_, sibling)

    spread(0, 1)
    w_pass(1 - xh, y, dev_up)
    w_push(w_at(1 - xh, c, y), 1 - xh, c, y, dev_down)
    spread(1, 2)
    w_pass(xh, down, dev_up)
    w_pass(xh, up, None)
    spread(2, 4)
    w_pass(1 - xh, up, dev_down)
    w_pass(1 - xh, down, None)
    spread(4, 6)
    pass_on(6, 8)
    w_pass(xh, plus(y, 2, 4), None)
    w_pass(1 - xh, plus(y, 2, 4), None)
    landed(w_at(xh, c, y), w_sem(xh, c, y))
    for dy in range(4):
        for h_ in (xh, 1 - xh):
            yd = plus(y, dy, 4)
            landed(w_at(h_, 1 - c, yd), w_sem(h_, 1 - c, yd))

    def z_at(dz):
        return plus(z, dz % 8, 8)

    def forward(dzs):
        zts = [z_at(dz) for dz in dzs]
        size = 96 * len(zts)
        for zt in zts:
            @pl.when(zt == 0)
            def _():
                landed(halo, h_sem.at[1])
                rim = jnp.dot(gat_ref[...], halo[...], preferred_element_type=F32)[:216].reshape(9, 24, 128)
                im_o[:, 0] = jnp.where(xh == 1, rim, jnp.zeros_like(rim))

        def rows(held, hw, by):
            return jnp.concatenate([held[hw, pl.ds(4 * zt + by, 4)].reshape(96, 128) for zt in zts], axis=0).astype(BF16)

        def step(h, carry):
            lhs, rhs = [], []
            for w in range(3):
                hw = h * 3 + w
                lhs += [rows(im_o, hw, 0), rows(im_e, hw, 0), rows(im_o, hw, 1)]
                rhs += [wg[hw], wg[9 + hw], wg[18 + hw]]
            pacc[0:size] += jnp.dot(
                jnp.concatenate(lhs, axis=1), jnp.concatenate(rhs, axis=0), preferred_element_type=F32
            )
            return carry

        pacc[0:size] = jnp.zeros((size, 512), F32)
        lax.fori_loop(0, 3, step, 0)
        for q, dz in enumerate(dzs):
            zt = zts[q]
            part[zt] = pacc[q * 96:(q + 1) * 96].astype(BF16)

    next_z, last_z = dev(xl, y, xh, plus(z, 1, 8), c), dev(xl, y, xh, plus(z, 7, 8), c)

    def rs_hop(way, step, half):
        zt = z_at((5 - step) * (1 - 2 * way))
        at = (way * 4 + step - 1) * 2 + half
        own = part[zt, half * 48:(half + 1) * 48]
        if step > 1 and (step > 2 or half == way):
            before = at - 2
            landed(rsl.at[before], rs_recv.at[before])
            own = (own.astype(F32) + rsl[before].astype(F32)).astype(BF16)
        rss[at] = own
        copy = remote(rss.at[at], rsl.at[at], rs_send.at[at], rs_recv.at[at], last_z if way else next_z)
        copy.start()
        ends.append(copy.wait_send)

    def rs_step(step):
        for half in range(2):
            for way in range(2):
                if step > 1 or half == way:
                    rs_hop(way, step, half)

    forward((4, -3))
    rs_step(1)
    take_in(6, 8)
    forward((3, -2))
    rs_step(2)
    forward((2, -1, 1))
    rs_step(3)
    forward((0,))
    rs_step(4)

    for dy in range(4):
        yd = plus(y, dy, 4)
        landed(biasl.at[yd], b_recv.at[yd])
        for cs in range(2):
            landed(cotl.at[cs, yd], c_recv.at[cs * 4 + yd])
    pre = part[z].astype(F32)
    sums_in = []
    for way in range(2):
        for half in range(2):
            at = (way * 4 + 3) * 2 + half
            landed(rsl.at[at], rs_recv.at[at])
        sums_in.append(jnp.concatenate([rsl[way * 8 + 6], rsl[way * 8 + 7]], axis=0).astype(F32))
    pre = pre + sums_in[0] + sums_in[1]
    pre = pre + jnp.concatenate([biasl[i, 0:1] for i in range(4)], axis=1)
    sig = 1.0 / (1.0 + jnp.exp(-pre))
    samp = (pre * sig).astype(BF16)
    cot = jnp.concatenate(
        [jnp.concatenate([cotl[cs, i] for i in range(4)], axis=1) for cs in range(2)], axis=0
    ).astype(F32)
    slope = cot * sig * (1.0 + pre * (1.0 - sig))
    gbuf[z] = slope.astype(BF16)
    def g_at(o, half):
        return gbuf.at[o, pl.ds(half * 48, 48)]

    ag_count = [0]

    def ag_push(o, half, device):
        copy = remote(g_at(o, half), g_at(o, half), ag_send.at[ag_count[0]], ag_recv.at[o * 2 + half], device)
        ag_count[0] += 1
        copy.start()
        ends.append(copy.wait_send)

    for half in range(2):
        ag_push(z, half, next_z)
        ag_push(z, half, last_z)

    def rim_copy(zt):
        return remote(
            gbuf.at[0, pl.ds(0, 32)], gbuf.at[8, pl.ds(0, 32)], gh_send.at[zt], gh_recv.at[0], dev(xl, y, 0, zt, c)
        )

    gives_rim = jnp.logical_and(z == 0, xh == 1)

    @pl.when(gives_rim)
    def _():
        for zt in range(8):
            rim_copy(zt).start()

    @pl.when(xh == 1)
    def _():
        gbuf[8, pl.ds(0, 32)] = jnp.zeros((32, 512), BF16)

    sums = jnp.sum(slope, axis=0, keepdims=True)
    bz[z] = jnp.concatenate([sums[:, i * 128:(i + 1) * 128] for i in range(4)] + [jnp.zeros((4, 128), F32)], axis=0)
    for cs in range(2):
        for i in range(4):
            sbuf[cs, i] = samp[cs * 48:(cs + 1) * 48, i * 128:(i + 1) * 128]

    def late_sends():
        for n, dz in enumerate((1, 7, 2, 6, 3, 5, 4)):
            copy = remote(bz.at[z], bz.at[z], bz_send.at[n], bz_recv.at[z], dev(xl, y, xh, plus(z, dz, 8), c))
            copy.start()
            ends.append(copy.wait_send)
        for dy in range(4):
            for dc in range(2):
                yd, cd = plus(y, dy, 4), plus(c, dc, 2)
                src, dst, sem = sbuf.at[cd, yd], sland.at[c * 4 + y], s_recv.at[c * 4 + y]
                if dy or dc:
                    copy = remote(src, dst, s_send.at[dy * 2 + dc], sem, dev(xl, yd, xh, z, cd))
                    copy.start()
                    ends.append(copy.wait_send)
                else:
                    pltpu.make_async_copy(src, dst, sem).start()

    def back_pair(first, second):
        def back(h, carry):
            hws = [h * 3 + w for w in range(3)]
            mats = jnp.concatenate([wg[t * 9 + hw] for hw in hws for t in range(3)], axis=0)
            rows = jnp.concatenate(
                [gbuf[first], gbuf[first + 1, 0:32], gbuf[second], gbuf[second + 1, 0:32]], axis=0
            )
            r = lax.dot_general(rows, mats, (((1,), (1,)), ((), ())), preferred_element_type=F32)
            for w in range(3):
                at = w * 384
                for i in range(2):
                    p = r[i * 128:i * 128 + 128]
                    dtmp[i, h * 3 + w, 0:4] = p[:96, at + 128:at + 256].reshape(4, 24, 128)
                    dtmp[i, h * 3 + w, 4:8] = (p[:96, at + 256:at + 384] + p[24:120, at:at + 128]).reshape(4, 24, 128)
            return carry

        lax.fori_loop(0, 3, back, 0)

        def place(i, carry):
            zc = jnp.where(i == 0, first, second)
            cols = [dtmp[i, :, f + 4 * odd].reshape(216, 128) for f in range(4) for odd in range(2)]
            side = jnp.concatenate(cols, axis=1)
            side = jnp.concatenate([side, jnp.zeros((8, 1024), F32)], axis=0).astype(BF16)
            r = jnp.dot(sca_ref[...], side, preferred_element_type=F32).astype(BF16)
            for cs in range(2):
                k = 2 * zc + cs
                for f in range(4):
                    dxb[k, pl.ds(f * 96, 96)] = r[:, (cs * 4 + f) * 128:(cs * 4 + f + 1) * 128]

                @pl.when(jnp.logical_not(primary))
                def _(k=k):
                    remote(dxb.at[k], dxp.at[k], dxp_send.at[k], dxp_recv.at[k], partner).start()
            return carry

        lax.fori_loop(0, 2, place, 0)

    def send_back(k):
        landed(dxp.at[k], dxp_recv.at[k])
        dxs[k] = (dxb[k].astype(F32) + dxp[k].astype(F32)).astype(BF16)

        @pl.when(k == me_k)
        def _():
            pltpu.make_async_copy(dxs.at[k], dx_out.at[z], dx_recv.at[z]).start()

        @pl.when(k != me_k)
        def _():
            remote(
                dxs.at[k], dx_out.at[z], dx_send.at[k], dx_recv.at[z], dev(xl, y, xh, lax.div(k, 2), lax.rem(k, 2))
            ).start()

    def finish_pair(first, second):
        @pl.when(primary)
        def _():
            def one(i, carry):
                zc = jnp.where(i < 2, first, second)
                send_back(2 * zc + lax.rem(i, 2))
                return carry

            lax.fori_loop(0, 4, one, 0)

    for step in range(1, 4):
        below, above = z_at(-step), z_at(step)
        for half in range(2):
            landed(g_at(below, half), ag_recv.at[below * 2 + half])
            if step < 3 or half == 0:
                ag_push(below, half, next_z)
            landed(g_at(above, half), ag_recv.at[above * 2 + half])
            if step < 3 or half == 1:
                ag_push(above, half, last_z)
        if step == 1:
            @pl.when(xh == 0)
            def _():
                landed(gbuf.at[8, pl.ds(0, 32)], gh_recv.at[0])

        back_pair(z_at(step - 1), z_at(-step))
        if step == 1:
            late_sends()
        if step > 1:
            finish_pair(z_at(step - 2), z_at(1 - step))
    for half in range(2):
        landed(g_at(z_at(4), half), ag_recv.at[z_at(4) * 2 + half])

    def weight_grad(h):
        def grad_step(w, carry):
            hw = h * 3 + w
            lhs = jnp.concatenate(
                [
                    im_o[hw, pl.ds(0, 32)].reshape(768, 128).astype(BF16),
                    im_e[hw].reshape(768, 128).astype(BF16),
                    im_o[hw, pl.ds(1, 32)].reshape(768, 128).astype(BF16),
                ],
                axis=1,
            )
            r = lax.dot_general(
                lhs, gbuf[0:8].reshape(768, 512), (((0,), (0,)), ((), ())), preferred_element_type=F32
            ).astype(BF16)
            for t in range(3):
                for h_ in range(2):
                    for c_ in range(2):
                        at = t * 128 + h_ * 64 + c_ * 32
                        dwb[h, c_, h_, w * 3 + t] = r[at:at + 32]
            return carry

        lax.fori_loop(0, 3, grad_step, 0)
        copy = remote(dwb.at[h, 1 - c], dws.at[h], k1_send.at[h], k1_recv.at[h], sibling)
        copy.start()
        ends.append(copy.wait_send)

    def core_sum(h):
        landed(dws.at[h], k1_recv.at[h])

        def add_step(n, carry):
            for h_ in range(2):
                dwr[h, h_, n] = (dwb[h, c, h_, n].astype(F32) + dws[h, h_, n].astype(F32)).astype(BF16)
            return carry

        lax.fori_loop(0, 9, add_step, 0)

    def y_lanes(i):
        return pl.ds(pl.multiple_of(i * 128, 128), 128)

    def to_y(h):
        core_sum(h)
        for dy in range(4):
            yd = plus(y, dy, 4)
            src = dwr.at[h, :, :, :, y_lanes(yd)]
            dst, sem = dwl.at[h, y], k2_recv.at[h * 4 + y]
            if dy:
                copy = remote(src, dst, k2_send.at[h * 4 + dy], sem, dev(xl, yd, xh, z, c))
                copy.start()
                ends.append(copy.wait_send)
            else:
                pltpu.make_async_copy(src, dst, sem).start()

    def y_to_x(h):
        for i in range(4):
            landed(dwl.at[h, i], k2_recv.at[h * 4 + i])

        def add_step(n, carry):
            own, other = dwl[h, 0, xh, n].astype(F32), dwl[h, 0, 1 - xh, n].astype(F32)
            for i in range(1, 4):
                own = own + dwl[h, i, xh, n].astype(F32)
                other = other + dwl[h, i, 1 - xh, n].astype(F32)
            dwo[h, n] = own
            dwx[h, n] = other.astype(BF16)
            return carry

        lax.fori_loop(0, 9, add_step, 0)
        copy = remote(dwx.at[h], dwy.at[h], k3_send.at[h], k3_recv.at[h], across)
        copy.start()
        ends.append(copy.wait_send)

    def to_x(h):
        core_sum(h)
        copy = remote(dwr.at[h, 1 - xh], dwm, k3_send.at[h], k3_recv.at[h], across)
        copy.start()
        ends.append(copy.wait_send)

    def x_to_y(h):
        landed(dwm, k3_recv.at[h])

        def add_step(n, carry):
            dwn[n] = (dwr[h, xh, n].astype(F32) + dwm[n].astype(F32)).astype(BF16)
            return carry

        lax.fori_loop(0, 9, add_step, 0)
        for dy in range(4):
            yd = plus(y, dy, 4)
            src = dwn.at[:, :, y_lanes(yd)]
            dst, sem = dwl.at[h, y, 0], k2_recv.at[h * 4 + y]
            if dy:
                copy = remote(src, dst, k2_send.at[h * 4 + dy], sem, dev(xl, yd, xh, z, c))
                copy.start()
                ends.append(copy.wait_send)
            else:
                pltpu.make_async_copy(src, dst, sem).start()

    weight_grad(0)
    back_pair(z_at(3), z_at(4))
    to_y(0)
    finish_pair(z_at(2), z_at(-3))
    weight_grad(1)
    weight_grad(2)
    finish_pair(z_at(3), z_at(4))
    to_x(1)
    to_y(2)
    y_to_x(0)
    x_to_y(1)

    total = bz[z]
    for dz in (1, 7, 2, 6, 3, 5, 4):
        zs = plus(z, dz, 8)
        landed(bz.at[zs], bz_recv.at[zs])
        total = total + bz[zs]
    for i in range(4):
        bs[i] = jnp.broadcast_to(total[i:i + 1], (8, 128))
    slot_b = (xh * 2 + c) * 4 + y
    for dy in range(4):
        for dh in range(2):
            for dc in range(2):
                yd, hd, cd = plus(y, dy, 4), plus(xh, dh, 2), plus(c, dc, 2)
                if dy or dh or dc:
                    copy = remote(
                        bs.at[yd], bl.at[slot_b], bs_send.at[(dy * 2 + dh) * 2 + dc], bs_recv.at[slot_b],
                        dev(xl, yd, hd, z, cd),
                    )
                    copy.start()
                    ends.append(copy.wait_send)
                else:
                    pltpu.make_async_copy(bs.at[y], bl.at[slot_b], bs_recv.at[slot_b]).start()

    outs = []
    for i in range(8):
        landed(sland.at[i], s_recv.at[i])
    outs.append(pltpu.make_async_copy(sland, samp_out, o_sem.at[0]))
    outs[-1].start()

    y_to_x(2)
    for i in range(4):
        landed(dwl.at[1, i, 0], k2_recv.at[4 + i])

    def sum_middle(w, carry):
        for t in range(3):
            acc = dwl[1, 0, 0, w * 3 + t].astype(F32)
            for i in range(1, 4):
                acc = acc + dwl[1, i, 0, w * 3 + t].astype(F32)
            kout[t * 9 + 3 + w] = acc * inv
        return carry

    lax.fori_loop(0, 3, sum_middle, 0)
    for h in (0, 2):
        landed(dwy.at[h], k3_recv.at[h])

        def sum_step(w, carry, h=h):
            for t in range(3):
                kout[t * 9 + h * 3 + w] = (dwo[h, w * 3 + t] + dwy[h, w * 3 + t].astype(F32)) * inv
            return carry

        lax.fori_loop(0, 3, sum_step, 0)
    outs.append(pltpu.make_async_copy(kout, dw_out, o_sem.at[1]))
    outs[-1].start()

    acc = None
    for i in range(16):
        landed(bl.at[i], bs_recv.at[i])
        acc = bl[i] if acc is None else acc + bl[i]
    dbo[...] = acc[0:1] * inv
    outs.append(pltpu.make_async_copy(dbo, db_out, o_sem.at[2]))
    outs[-1].start()

    for i in range(8):
        landed(dx_out.at[i], dx_recv.at[i])

    for end in ends:
        end()

    @pl.when(jnp.logical_not(primary))
    def _():
        sib_x.wait_send()

        def drain(k, carry):
            remote(dxb.at[k], dxp.at[k], dxp_send.at[k], dxp_recv.at[k], partner).wait_send()
            return carry

        lax.fori_loop(0, 16, drain, 0)

    @pl.when(primary)
    def _():
        def drain(k, carry):
            remote(land.at[k], land.at[k], f_send.at[k], x_recv.at[k], partner).wait_send()

            @pl.when(k != me_k)
            def _():
                remote(
                    dxs.at[k], dx_out.at[z], dx_send.at[k], dx_recv.at[z],
                    dev(xl, y, xh, lax.div(k, 2), lax.rem(k, 2)),
                ).wait_send()

            return carry

        lax.fori_loop(0, 16, drain, 0)

    @pl.when(gives_rim)
    def _():
        for zt in range(8):
            rim_copy(zt).wait_send()

    for out in outs:
        out.wait()


def finisher(samp_in, dx_in, dw_in, db_in, samp_out, dx_out, dw_out, db_out, held, made, in_sem, out_sem):
    loads = [pltpu.make_async_copy(dx_in.at[i], held.at[i], in_sem.at[i]) for i in range(8)]
    for copy in loads:
        copy.start()
    samp_out[...] = samp_in[...]
    dw_out[...] = dw_in[...]
    db_out[...] = db_in[...]
    stores = []
    for m in range(4):
        loads[2 * m].wait()
        loads[2 * m + 1].wait()
        a, b = held[2 * m], held[2 * m + 1]
        for half in range(2):
            cols = pl.ds(half * 512 + m * 128, 128)
            made[:, cols] = jnp.concatenate(
                [a[:, half * 64:half * 64 + 64], b[:, half * 64:half * 64 + 64]], axis=1
            )
            copy = pltpu.make_async_copy(made.at[:, cols], dx_out.at[:, cols], out_sem.at[2 * m + half])
            copy.start()
            stores.append(copy)
    for copy in stores:
        copy.wait()


def shards(video_clips, weights, conv_bias, cotangent):
    x = video_clips.reshape(384, 1024)
    w = weights.reshape(27, 32, 128)
    cot = cotangent.transpose(0, 1, 3, 2, 4).reshape(8, 48, 128)
    bias = conv_bias.reshape(1, 128)
    table = tap_gather()
    gat = jnp.asarray(table, BF16)
    sca = jnp.asarray(table.T, BF16)
    any_spec = pl.BlockSpec(memory_space=pl.ANY)
    vmem_spec = pl.BlockSpec(memory_space=pltpu.VMEM)

    def v(shape, dtype=BF16):
        return pltpu.VMEM(shape, dtype)

    def sems(n):
        return pltpu.SemaphoreType.DMA((n,))

    samp, dx, dw, db = pl.pallas_call(
        kernel,
        out_shape=[
            jax.ShapeDtypeStruct((8, 48, 128), BF16),
            jax.ShapeDtypeStruct((8, 384, 128), BF16),
            jax.ShapeDtypeStruct((27, 32, 128), F32),
            jax.ShapeDtypeStruct((1, 128), F32),
        ],
        in_specs=[any_spec] * 3 + [vmem_spec] * 3,
        out_specs=[any_spec] * 4,
        scratch_shapes=[
            v((384, 1024)),
            v((8, 384, 128)),
            v((16, 384, 128)),
            v((96, 128)),
            v((27, 128, 512)),
            v((2, 4, 48, 128)),
            v((8, 128), F32),
            v((4, 8, 128), F32),
            v((9, 32, 24, 128), F32),
            v((9, 33, 24, 128), F32),
            v((384, 512), F32),
            v((8, 96, 512)),
            v((16, 48, 512)),
            v((16, 48, 512)),
            v((2, 4, 48, 128)),
            v((8, 48, 128)),
            v((9, 96, 512)),
            v((8, 8, 128), F32),
            v((4, 8, 128), F32),
            v((16, 8, 128), F32),
            v((2, 9, 8, 24, 128), F32),
            v((16, 384, 128)),
            v((16, 384, 128)),
            v((16, 384, 128)),
            v((3, 2, 2, 9, 32, 512)),
            v((3, 2, 9, 32, 512)),
            v((3, 2, 9, 32, 512)),
            v((3, 4, 2, 9, 32, 128)),
            v((3, 9, 32, 128), F32),
            v((3, 9, 32, 128)),
            v((3, 9, 32, 128)),
            v((9, 32, 512)),
            v((9, 32, 512)),
            v((27, 32, 128), F32),
            v((1, 128), F32),
            sems(1), sems(8), sems(16), sems(16), sems(2),
            sems(16), sems(16), sems(8), sems(8), sems(4), sems(4),
            sems(16), sems(16), sems(8), sems(8), sems(14), sems(16), sems(8), sems(8),
            sems(8), sems(1), sems(16), sems(16), sems(16), sems(16), sems(16), sems(8),
            sems(3), sems(3), sems(12), sems(12), sems(3), sems(3), sems(4),
        ],
        compiler_params=pltpu.CompilerParams(
            collective_id=0, has_side_effects=True, vmem_limit_bytes=60 * 1024 * 1024
        ),
        cost_estimate=pl.CostEstimate(flops=10_000_000_000, bytes_accessed=8_000_000, transcendentals=50_000),
    )(x, w, cot, bias, gat, sca)
    samp, dx, dw, db = pl.pallas_call(
        finisher,
        out_shape=[
            jax.ShapeDtypeStruct((8, 48, 128), BF16),
            jax.ShapeDtypeStruct((384, 1024), BF16),
            jax.ShapeDtypeStruct((27, 32, 128), F32),
            jax.ShapeDtypeStruct((1, 128), F32),
        ],
        in_specs=[vmem_spec, any_spec, vmem_spec, vmem_spec],
        out_specs=[vmem_spec, any_spec, vmem_spec, vmem_spec],
        scratch_shapes=[v((8, 384, 128)), v((384, 1024)), sems(8), sems(8)],
        cost_estimate=pl.CostEstimate(flops=0, bytes_accessed=3_000_000, transcendentals=0),
    )(samp, dx, dw, db)
    sampled = samp.reshape(8, 2, 12, 2, 128).transpose(0, 1, 3, 2, 4)
    clip_grad = dx.reshape(1, 4, 4, 24, 1024)
    return sampled, clip_grad, dw.reshape(3, 3, 3, 32, 128), db.reshape(128)


def solution(mesh):
    return jax.shard_map(
        shards,
        mesh=mesh,
        in_specs=(
            P("dp", "tm", None, None, None),
            P(None, None, None, "tm", "dp"),
            P("dp"),
            P(None, "tm", None, None, "dp"),
        ),
        out_specs=(
            P(None, "tm", None, None, "dp"),
            P("dp", "tm", None, None, None),
            P(None, None, None, "tm", "dp"),
            P("dp"),
        ),
        check_vma=False,
    )
```

```python
import math

import jax
import jax.numpy as jnp
import numpy as np
from jax import lax
from jax.experimental import pallas as pl
from jax.experimental.pallas import tpu as pltpu
from jax.sharding import PartitionSpec as P

MESH = pl.DeviceIdType.MESH
F32 = jnp.float32
BF16 = jnp.bfloat16
POSITIONS = 12288


def tap_gather():
    table = np.zeros((224, 96), np.float32)
    for h in range(3):
        for w in range(3):
            for r in range(2):
                for q in range(12):
                    row, col = 2 * r + h - 1, 2 * q + w - 1
                    if 0 <= row < 4 and 0 <= col < 24:
                        table[(h * 3 + w) * 24 + q * 2 + r, row * 24 + col] = 1.0
    return table


def kernel(
    x_ref, w_ref, cot_ref, bias_ref, gat_ref, sca_ref,
    samp_out, dx_out, dw_out, db_out,
    xv, xp, land, halo, wg, cotl, biasb, biasl, im_e, im_o, pacc, part, rsl, rss, sbuf, sland, gbuf, bz, bs, bl,
    dtmp, dxb, dxp, dxs, dwb, dws, dwr, dwl, dwo, dwx, dwy, dwm, dwn, kout, dbo,
    v_sem, x_send, x_recv, f_send, h_sem, w_send, w_recv, c_send, c_recv, b_send, b_recv, rs_send, rs_recv,
    s_send, s_recv, ag_send, ag_recv, bz_send, bz_recv, gh_send, gh_recv, bs_send, bs_recv, dxp_send, dxp_recv,
    dx_send, dx_recv, k1_send, k1_recv, k2_send, k2_recv, k3_send, k3_recv, o_sem,
):
    dp, tm = lax.axis_index("dp"), lax.axis_index("tm")
    xl, y = lax.div(dp, 4), lax.rem(dp, 4)
    xh, z, c = lax.div(tm, 16), lax.rem(lax.div(tm, 2), 8), lax.rem(tm, 2)
    primary = c == xl
    inv = 1.0 / math.sqrt(POSITIONS)

    def dev(xl_, y_, xh_, z_, c_):
        return (xl_ * 4 + y_, (xh_ * 8 + z_) * 2 + c_)

    def remote(src, dst, send, recv, device):
        return pltpu.make_async_remote_copy(
            src_ref=src, dst_ref=dst, send_sem=send, recv_sem=recv, device_id=device, device_id_type=MESH
        )

    def landed(dst, sem):
        pltpu.make_async_copy(dst, dst, sem).wait()

    def plus(a, by, n):
        return lax.rem(a + by, n)

    partner = dev(1 - xl, y, xh, z, c)
    sibling = dev(xl, y, xh, z, 1 - c)
    across = dev(xl, y, 1 - xh, z, c)

    x_in = pltpu.make_async_copy(x_ref, xv, v_sem.at[0])
    x_in.start()

    barrier = pltpu.get_barrier_semaphore()
    peers = [partner]
    for dz in range(8):
        for dc in range(2):
            if dz or dc:
                peers.append(dev(xl, y, xh, plus(z, dz, 8), plus(c, dc, 2)))
    for dy in range(4):
        for dh in range(2):
            for dc in range(2):
                if dy or dh:
                    peers.append(dev(xl, plus(y, dy, 4), plus(xh, dh, 2), z, plus(c, dc, 2)))
    for dz in range(1, 8):
        peers.append(dev(xl, y, 1 - xh, plus(z, dz, 8), c))
    for peer in peers:
        pl.semaphore_signal(barrier, inc=1, device_id=peer, device_id_type=MESH)

    biasb[...] = jnp.broadcast_to(bias_ref[...], (8, 128))
    x_in.wait()
    for zt in range(8):
        at = (zt // 2) * 128 + (zt % 2) * 64
        xp[zt] = jnp.concatenate([xv[:, at:at + 64], xv[:, 512 + at:512 + at + 64]], axis=1)
    pl.semaphore_wait(barrier, len(peers))

    ends = []

    me_k = 2 * z + c
    for n, dz in enumerate((4, 1, 7, 3, 5, 2, 6)):
        zt = plus(z, dz, 8)
        copy = remote(xp.at[zt], land.at[me_k], x_send.at[n], x_recv.at[me_k], dev(xl, y, xh, zt, xl))
        copy.start()
        ends.append(copy.wait_send)
    own_x = pltpu.make_async_copy(xp.at[z], land.at[me_k], x_recv.at[me_k])
    sib_x = remote(xp.at[z], land.at[me_k], x_send.at[7], x_recv.at[me_k], dev(xl, y, xh, z, 1 - c))

    @pl.when(primary)
    def _():
        own_x.start()

    @pl.when(jnp.logical_not(primary))
    def _():
        sib_x.start()

    def w_at(h_, c_, y_):
        return wg.at[:, pl.ds(pl.multiple_of((h_ * 2 + c_) * 32, 32), 32), pl.ds(pl.multiple_of(y_ * 128, 128), 128)]

    def w_sem(h_, c_, y_):
        return w_recv.at[(h_ * 2 + c_) * 4 + y_]

    w_count = [0]

    def w_push(src, h_, c_, y_, device):
        copy = remote(src, w_at(h_, c_, y_), w_send.at[w_count[0]], w_sem(h_, c_, y_), device)
        w_count[0] += 1
        copy.start()
        ends.append(copy.wait_send)

    up, down = plus(y, 1, 4), plus(y, 3, 4)
    dev_up, dev_down = dev(xl, up, xh, z, c), dev(xl, down, xh, z, c)
    w_push(w_ref, xh, c, y, across)
    w_push(w_ref, xh, c, y, dev_up)
    w_push(w_ref, xh, c, y, dev_down)
    w_push(w_ref, xh, c, y, sibling)
    pltpu.make_async_copy(w_ref, w_at(xh, c, y), w_sem(xh, c, y)).start()

    for dy in range(4):
        for dc in range(2):
            yd, cd = plus(y, dy, 4), plus(c, dc, 2)
            src, dst, sem = cot_ref.at[cd * 4 + yd], cotl.at[c, y], c_recv.at[c * 4 + y]
            if dy or dc:
                copy = remote(src, dst, c_send.at[dy * 2 + dc], sem, dev(xl, yd, xh, z, cd))
                copy.start()
                ends.append(copy.wait_send)
            else:
                pltpu.make_async_copy(src, dst, sem).start()
    pltpu.make_async_copy(biasb, biasl.at[y], b_recv.at[y]).start()
    for dy in range(1, 4):
        copy = remote(biasb, biasl.at[y], b_send.at[dy], b_recv.at[y], dev(xl, plus(y, dy, 4), xh, z, c))
        copy.start()
        ends.append(copy.wait_send)

    halo_copy = remote(land.at[15, pl.ds(288, 96)], halo, h_sem.at[0], h_sem.at[1], across)
    ends.append(halo_copy.wait_send)

    def place_of(j):
        dz = 0
        dz = jnp.where(j == 1, 4, dz)
        dz = jnp.where(j == 2, 1, dz)
        dz = jnp.where(j == 3, 7, dz)
        dz = jnp.where(j == 4, 3, dz)
        dz = jnp.where(j == 5, 5, dz)
        dz = jnp.where(j == 6, 2, dz)
        dz = jnp.where(j == 7, 6, dz)
        return plus(z, dz, 8)

    def pass_on(first, last):
        @pl.when(primary)
        def _():
            def one(i, carry):
                k = 2 * place_of(lax.div(i, 2)) + lax.rem(i, 2)
                landed(land.at[k], x_recv.at[k])
                remote(land.at[k], land.at[k], f_send.at[k], x_recv.at[k], partner).start()
                return carry

            lax.fori_loop(2 * first, 2 * last, one, 0)

    def take_in(first, last):
        def one(i, carry):
            k = 2 * place_of(lax.div(i, 2)) + lax.rem(i, 2)

            @pl.when(jnp.logical_not(primary))
            def _():
                landed(land.at[k], x_recv.at[k])

            @pl.when(k == 15)
            def _():
                halo_copy.start()

            frames = land[k]
            side = jnp.concatenate([frames[i * 96:(i + 1) * 96] for i in range(4)], axis=1)
            taps = jnp.dot(gat_ref[...], side, preferred_element_type=F32)
            for f in range(4):
                piece = taps[:216, f * 128:(f + 1) * 128].reshape(9, 24, 128)
                if f % 2 == 0:
                    im_e[:, 2 * k + f // 2] = piece
                else:
                    im_o[:, 2 * k + 1 + f // 2] = piece
            return carry

        lax.fori_loop(2 * first, 2 * last, one, 0)

    def spread(first, last):
        pass_on(first, last)
        take_in(first, last)

    def w_pass(h_, y_, device):
        landed(w_at(h_, c, y_), w_sem(h_, c, y_))
        if device is not None:
            w_push(w_at(h_, c, y_), h_, c, y_, device)
        w_push(w_at(h_, c, y_), h_, c, y_, sibling)

    spread(0, 1)
    w_pass(1 - xh, y, dev_up)
    w_push(w_at(1 - xh, c, y), 1 - xh, c, y, dev_down)
    spread(1, 2)
    w_pass(xh, down, dev_up)
    w_pass(xh, up, None)
    spread(2, 4)
    w_pass(1 - xh, up, dev_down)
    w_pass(1 - xh, down, None)
    spread(4, 6)
    pass_on(6, 8)
    w_pass(xh, plus(y, 2, 4), None)
    w_pass(1 - xh, plus(y, 2, 4), None)
    landed(w_at(xh, c, y), w_sem(xh, c, y))
    for dy in range(4):
        for h_ in (xh, 1 - xh):
            yd = plus(y, dy, 4)
            landed(w_at(h_, 1 - c, yd), w_sem(h_, 1 - c, yd))

    def z_at(dz):
        return plus(z, dz % 8, 8)

    def forward(dzs):
        zts = [z_at(dz) for dz in dzs]
        size = 96 * len(zts)
        for zt in zts:
            @pl.when(zt == 0)
            def _():
                landed(halo, h_sem.at[1])
                rim = jnp.dot(gat_ref[...], halo[...], preferred_element_type=F32)[:216].reshape(9, 24, 128)
                im_o[:, 0] = jnp.where(xh == 1, rim, jnp.zeros_like(rim))

        def rows(held, hw, by):
            return jnp.concatenate([held[hw, pl.ds(4 * zt + by, 4)].reshape(96, 128) for zt in zts], axis=0).astype(BF16)

        def step(h, carry):
            lhs, rhs = [], []
            for w in range(3):
                hw = h * 3 + w
                lhs += [rows(im_o, hw, 0), rows(im_e, hw, 0), rows(im_o, hw, 1)]
                rhs += [wg[hw], wg[9 + hw], wg[18 + hw]]
            pacc[0:size] += jnp.dot(
                jnp.concatenate(lhs, axis=1), jnp.concatenate(rhs, axis=0), preferred_element_type=F32
            )
            return carry

        pacc[0:size] = jnp.zeros((size, 512), F32)
        lax.fori_loop(0, 3, step, 0)
        for q, dz in enumerate(dzs):
            zt = zts[q]
            part[zt] = pacc[q * 96:(q + 1) * 96].astype(BF16)

    next_z, last_z = dev(xl, y, xh, plus(z, 1, 8), c), dev(xl, y, xh, plus(z, 7, 8), c)

    def rs_hop(way, step, half):
        zt = z_at((5 - step) * (1 - 2 * way))
        at = (way * 4 + step - 1) * 2 + half
        own = part[zt, half * 48:(half + 1) * 48]
        if step > 1 and (step > 2 or half == way):
            before = at - 2
            landed(rsl.at[before], rs_recv.at[before])
            own = (own.astype(F32) + rsl[before].astype(F32)).astype(BF16)
        rss[at] = own
        copy = remote(rss.at[at], rsl.at[at], rs_send.at[at], rs_recv.at[at], last_z if way else next_z)
        copy.start()
        ends.append(copy.wait_send)

    def rs_step(step):
        for half in range(2):
            for way in range(2):
                if step > 1 or half == way:
                    rs_hop(way, step, half)

    forward((4, -3))
    rs_step(1)
    take_in(6, 8)
    forward((3, -2))
    rs_step(2)
    forward((2, -1, 1))
    rs_step(3)
    forward((0,))
    rs_step(4)

    for dy in range(4):
        yd = plus(y, dy, 4)
        landed(biasl.at[yd], b_recv.at[yd])
        for cs in range(2):
            landed(cotl.at[cs, yd], c_recv.at[cs * 4 + yd])
    pre = part[z].astype(F32)
    sums_in = []
    for way in range(2):
        for half in range(2):
            at = (way * 4 + 3) * 2 + half
            landed(rsl.at[at], rs_recv.at[at])
        sums_in.append(jnp.concatenate([rsl[way * 8 + 6], rsl[way * 8 + 7]], axis=0).astype(F32))
    pre = pre + sums_in[0] + sums_in[1]
    pre = pre + jnp.concatenate([biasl[i, 0:1] for i in range(4)], axis=1)
    sig = 1.0 / (1.0 + jnp.exp(-pre))
    samp = (pre * sig).astype(BF16)
    cot = jnp.concatenate(
        [jnp.concatenate([cotl[cs, i] for i in range(4)], axis=1) for cs in range(2)], axis=0
    ).astype(F32)
    slope = cot * sig * (1.0 + pre * (1.0 - sig))
    gbuf[z] = slope.astype(BF16)
    def g_at(o, half):
        return gbuf.at[o, pl.ds(half * 48, 48)]

    ag_count = [0]

    def ag_push(o, half, device):
        copy = remote(g_at(o, half), g_at(o, half), ag_send.at[ag_count[0]], ag_recv.at[o * 2 + half], device)
        ag_count[0] += 1
        copy.start()
        ends.append(copy.wait_send)

    for half in range(2):
        ag_push(z, half, next_z)
        ag_push(z, half, last_z)

    def rim_copy(zt):
        return remote(
            gbuf.at[0, pl.ds(0, 32)], gbuf.at[8, pl.ds(0, 32)], gh_send.at[zt], gh_recv.at[0], dev(xl, y, 0, zt, c)
        )

    gives_rim = jnp.logical_and(z == 0, xh == 1)

    @pl.when(gives_rim)
    def _():
        for zt in range(8):
            rim_copy(zt).start()

    @pl.when(xh == 1)
    def _():
        gbuf[8, pl.ds(0, 32)] = jnp.zeros((32, 512), BF16)

    sums = jnp.sum(slope, axis=0, keepdims=True)
    bz[z] = jnp.concatenate([sums[:, i * 128:(i + 1) * 128] for i in range(4)] + [jnp.zeros((4, 128), F32)], axis=0)
    for cs in range(2):
        for i in range(4):
            sbuf[cs, i] = samp[cs * 48:(cs + 1) * 48, i * 128:(i + 1) * 128]

    def late_sends():
        for n, dz in enumerate((1, 7, 2, 6, 3, 5, 4)):
            copy = remote(bz.at[z], bz.at[z], bz_send.at[n], bz_recv.at[z], dev(xl, y, xh, plus(z, dz, 8), c))
            copy.start()
            ends.append(copy.wait_send)
        for dy in range(4):
            for dc in range(2):
                yd, cd = plus(y, dy, 4), plus(c, dc, 2)
                src, dst, sem = sbuf.at[cd, yd], sland.at[c * 4 + y], s_recv.at[c * 4 + y]
                if dy or dc:
                    copy = remote(src, dst, s_send.at[dy * 2 + dc], sem, dev(xl, yd, xh, z, cd))
                    copy.start()
                    ends.append(copy.wait_send)
                else:
                    pltpu.make_async_copy(src, dst, sem).start()

    def back_pair(first, second):
        def back(h, carry):
            hws = [h * 3 + w for w in range(3)]
            mats = jnp.concatenate([wg[t * 9 + hw] for hw in hws for t in range(3)], axis=0)
            rows = jnp.concatenate(
                [gbuf[first], gbuf[first + 1, 0:32], gbuf[second], gbuf[second + 1, 0:32]], axis=0
            )
            r = lax.dot_general(rows, mats, (((1,), (1,)), ((), ())), preferred_element_type=F32)
            for w in range(3):
                at = w * 384
                for i in range(2):
                    p = r[i * 128:i * 128 + 128]
                    dtmp[i, h * 3 + w, 0:4] = p[:96, at + 128:at + 256].reshape(4, 24, 128)
                    dtmp[i, h * 3 + w, 4:8] = (p[:96, at + 256:at + 384] + p[24:120, at:at + 128]).reshape(4, 24, 128)
            return carry

        lax.fori_loop(0, 3, back, 0)

        def place(i, carry):
            zc = jnp.where(i == 0, first, second)
            cols = [dtmp[i, :, f + 4 * odd].reshape(216, 128) for f in range(4) for odd in range(2)]
            side = jnp.concatenate(cols, axis=1)
            side = jnp.concatenate([side, jnp.zeros((8, 1024), F32)], axis=0).astype(BF16)
            r = jnp.dot(sca_ref[...], side, preferred_element_type=F32).astype(BF16)
            for cs in range(2):
                k = 2 * zc + cs
                for f in range(4):
                    dxb[k, pl.ds(f * 96, 96)] = r[:, (cs * 4 + f) * 128:(cs * 4 + f + 1) * 128]

                @pl.when(jnp.logical_not(primary))
                def _(k=k):
                    remote(dxb.at[k], dxp.at[k], dxp_send.at[k], dxp_recv.at[k], partner).start()
            return carry

        lax.fori_loop(0, 2, place, 0)

    def send_back(k):
        landed(dxp.at[k], dxp_recv.at[k])
        dxs[k] = (dxb[k].astype(F32) + dxp[k].astype(F32)).astype(BF16)

        @pl.when(k == me_k)
        def _():
            pltpu.make_async_copy(dxs.at[k], dx_out.at[z], dx_recv.at[z]).start()

        @pl.when(k != me_k)
        def _():
            remote(
                dxs.at[k], dx_out.at[z], dx_send.at[k], dx_recv.at[z], dev(xl, y, xh, lax.div(k, 2), lax.rem(k, 2))
            ).start()

    def finish_pair(first, second):
        @pl.when(primary)
        def _():
            def one(i, carry):
                zc = jnp.where(i < 2, first, second)
                send_back(2 * zc + lax.rem(i, 2))
                return carry

            lax.fori_loop(0, 4, one, 0)

    for step in range(1, 4):
        below, above = z_at(-step), z_at(step)
        for half in range(2):
            landed(g_at(below, half), ag_recv.at[below * 2 + half])
            if step < 3 or half == 0:
                ag_push(below, half, next_z)
            landed(g_at(above, half), ag_recv.at[above * 2 + half])
            if step < 3 or half == 1:
                ag_push(above, half, last_z)
        if step == 1:
            @pl.when(xh == 0)
            def _():
                landed(gbuf.at[8, pl.ds(0, 32)], gh_recv.at[0])

        back_pair(z_at(step - 1), z_at(-step))
        if step == 1:
            late_sends()
        if step > 1:
            finish_pair(z_at(step - 2), z_at(1 - step))
    for half in range(2):
        landed(g_at(z_at(4), half), ag_recv.at[z_at(4) * 2 + half])

    def weight_grad(h):
        def grad_step(w, carry):
            hw = h * 3 + w
            lhs = jnp.concatenate(
                [
                    im_o[hw, pl.ds(0, 32)].reshape(768, 128).astype(BF16),
                    im_e[hw].reshape(768, 128).astype(BF16),
                    im_o[hw, pl.ds(1, 32)].reshape(768, 128).astype(BF16),
                ],
                axis=1,
            )
            r = lax.dot_general(
                lhs, gbuf[0:8].reshape(768, 512), (((0,), (0,)), ((), ())), preferred_element_type=F32
            ).astype(BF16)
            for t in range(3):
                for h_ in range(2):
                    for c_ in range(2):
                        at = t * 128 + h_ * 64 + c_ * 32
                        dwb[h, c_, h_, w * 3 + t] = r[at:at + 32]
            return carry

        lax.fori_loop(0, 3, grad_step, 0)
        copy = remote(dwb.at[h, 1 - c], dws.at[h], k1_send.at[h], k1_recv.at[h], sibling)
        copy.start()
        ends.append(copy.wait_send)

    def core_sum(h):
        landed(dws.at[h], k1_recv.at[h])

        def add_step(n, carry):
            for h_ in range(2):
                dwr[h, h_, n] = (dwb[h, c, h_, n].astype(F32) + dws[h, h_, n].astype(F32)).astype(BF16)
            return carry

        lax.fori_loop(0, 9, add_step, 0)

    def y_lanes(i):
        return pl.ds(pl.multiple_of(i * 128, 128), 128)

    def to_y(h):
        core_sum(h)
        for dy in range(4):
            yd = plus(y, dy, 4)
            src = dwr.at[h, :, :, :, y_lanes(yd)]
            dst, sem = dwl.at[h, y], k2_recv.at[h * 4 + y]
            if dy:
                copy = remote(src, dst, k2_send.at[h * 4 + dy], sem, dev(xl, yd, xh, z, c))
                copy.start()
                ends.append(copy.wait_send)
            else:
                pltpu.make_async_copy(src, dst, sem).start()

    def y_to_x(h):
        for i in range(4):
            landed(dwl.at[h, i], k2_recv.at[h * 4 + i])

        def add_step(n, carry):
            own, other = dwl[h, 0, xh, n].astype(F32), dwl[h, 0, 1 - xh, n].astype(F32)
            for i in range(1, 4):
                own = own + dwl[h, i, xh, n].astype(F32)
                other = other + dwl[h, i, 1 - xh, n].astype(F32)
            dwo[h, n] = own
            dwx[h, n] = other.astype(BF16)
            return carry

        lax.fori_loop(0, 9, add_step, 0)
        copy = remote(dwx.at[h], dwy.at[h], k3_send.at[h], k3_recv.at[h], across)
        copy.start()
        ends.append(copy.wait_send)

    def to_x(h):
        core_sum(h)
        copy = remote(dwr.at[h, 1 - xh], dwm, k3_send.at[h], k3_recv.at[h], across)
        copy.start()
        ends.append(copy.wait_send)

    def x_to_y(h):
        landed(dwm, k3_recv.at[h])

        def add_step(n, carry):
            dwn[n] = (dwr[h, xh, n].astype(F32) + dwm[n].astype(F32)).astype(BF16)
            return carry

        lax.fori_loop(0, 9, add_step, 0)
        for dy in range(4):
            yd = plus(y, dy, 4)
            src = dwn.at[:, :, y_lanes(yd)]
            dst, sem = dwl.at[h, y, 0], k2_recv.at[h * 4 + y]
            if dy:
                copy = remote(src, dst, k2_send.at[h * 4 + dy], sem, dev(xl, yd, xh, z, c))
                copy.start()
                ends.append(copy.wait_send)
            else:
                pltpu.make_async_copy(src, dst, sem).start()

    weight_grad(0)
    back_pair(z_at(3), z_at(4))
    to_y(0)
    finish_pair(z_at(2), z_at(-3))
    weight_grad(1)
    weight_grad(2)
    finish_pair(z_at(3), z_at(4))
    to_x(1)
    to_y(2)
    y_to_x(0)
    x_to_y(1)

    total = bz[z]
    for dz in (1, 7, 2, 6, 3, 5, 4):
        zs = plus(z, dz, 8)
        landed(bz.at[zs], bz_recv.at[zs])
        total = total + bz[zs]
    for i in range(4):
        bs[i] = jnp.broadcast_to(total[i:i + 1], (8, 128))
    slot_b = (xh * 2 + c) * 4 + y
    for dy in range(4):
        for dh in range(2):
            for dc in range(2):
                yd, hd, cd = plus(y, dy, 4), plus(xh, dh, 2), plus(c, dc, 2)
                if dy or dh or dc:
                    copy = remote(
                        bs.at[yd], bl.at[slot_b], bs_send.at[(dy * 2 + dh) * 2 + dc], bs_recv.at[slot_b],
                        dev(xl, yd, hd, z, cd),
                    )
                    copy.start()
                    ends.append(copy.wait_send)
                else:
                    pltpu.make_async_copy(bs.at[y], bl.at[slot_b], bs_recv.at[slot_b]).start()

    outs = []
    for i in range(8):
        landed(sland.at[i], s_recv.at[i])
    outs.append(pltpu.make_async_copy(sland, samp_out, o_sem.at[0]))
    outs[-1].start()

    y_to_x(2)
    for i in range(4):
        landed(dwl.at[1, i, 0], k2_recv.at[4 + i])

    def sum_middle(w, carry):
        for t in range(3):
            acc = dwl[1, 0, 0, w * 3 + t].astype(F32)
            for i in range(1, 4):
                acc = acc + dwl[1, i, 0, w * 3 + t].astype(F32)
            kout[t * 9 + 3 + w] = acc * inv
        return carry

    lax.fori_loop(0, 3, sum_middle, 0)
    for h in (0, 2):
        landed(dwy.at[h], k3_recv.at[h])

        def sum_step(w, carry, h=h):
            for t in range(3):
                kout[t * 9 + h * 3 + w] = (dwo[h, w * 3 + t] + dwy[h, w * 3 + t].astype(F32)) * inv
            return carry

        lax.fori_loop(0, 3, sum_step, 0)
    outs.append(pltpu.make_async_copy(kout, dw_out, o_sem.at[1]))
    outs[-1].start()

    acc = None
    for i in range(16):
        landed(bl.at[i], bs_recv.at[i])
        acc = bl[i] if acc is None else acc + bl[i]
    dbo[...] = acc[0:1] * inv
    outs.append(pltpu.make_async_copy(dbo, db_out, o_sem.at[2]))
    outs[-1].start()

    for i in range(8):
        landed(dx_out.at[i], dx_recv.at[i])

    for end in ends:
        end()

    @pl.when(jnp.logical_not(primary))
    def _():
        sib_x.wait_send()

        def drain(k, carry):
            remote(dxb.at[k], dxp.at[k], dxp_send.at[k], dxp_recv.at[k], partner).wait_send()
            return carry

        lax.fori_loop(0, 16, drain, 0)

    @pl.when(primary)
    def _():
        def drain(k, carry):
            remote(land.at[k], land.at[k], f_send.at[k], x_recv.at[k], partner).wait_send()

            @pl.when(k != me_k)
            def _():
                remote(
                    dxs.at[k], dx_out.at[z], dx_send.at[k], dx_recv.at[z],
                    dev(xl, y, xh, lax.div(k, 2), lax.rem(k, 2)),
                ).wait_send()

            return carry

        lax.fori_loop(0, 16, drain, 0)

    @pl.when(gives_rim)
    def _():
        for zt in range(8):
            rim_copy(zt).wait_send()

    for out in outs:
        out.wait()


def finisher(samp_in, dx_in, dw_in, db_in, samp_out, dx_out, dw_out, db_out, held, made, in_sem, out_sem):
    loads = [pltpu.make_async_copy(dx_in.at[i], held.at[i], in_sem.at[i]) for i in range(8)]
    for copy in loads:
        copy.start()
    samp_out[...] = samp_in[...]
    dw_out[...] = dw_in[...]
    db_out[...] = db_in[...]
    stores = []
    for m in range(4):
        loads[2 * m].wait()
        loads[2 * m + 1].wait()
        a, b = held[2 * m], held[2 * m + 1]
        for half in range(2):
            cols = pl.ds(half * 512 + m * 128, 128)
            made[:, cols] = jnp.concatenate(
                [a[:, half * 64:half * 64 + 64], b[:, half * 64:half * 64 + 64]], axis=1
            )
            copy = pltpu.make_async_copy(made.at[:, cols], dx_out.at[:, cols], out_sem.at[2 * m + half])
            copy.start()
            stores.append(copy)
    for copy in stores:
        copy.wait()


def shards(video_clips, weights, conv_bias, cotangent):
    x = video_clips.reshape(384, 1024)
    w = weights.reshape(27, 32, 128)
    cot = cotangent.transpose(0, 1, 3, 2, 4).reshape(8, 48, 128)
    bias = conv_bias.reshape(1, 128)
    table = tap_gather()
    gat = jnp.asarray(table, BF16)
    sca = jnp.asarray(table.T, BF16)
    any_spec = pl.BlockSpec(memory_space=pl.ANY)
    vmem_spec = pl.BlockSpec(memory_space=pltpu.VMEM)

    def v(shape, dtype=BF16):
        return pltpu.VMEM(shape, dtype)

    def sems(n):
        return pltpu.SemaphoreType.DMA((n,))

    samp, dx, dw, db = pl.pallas_call(
        kernel,
        out_shape=[
            jax.ShapeDtypeStruct((8, 48, 128), BF16),
            jax.ShapeDtypeStruct((8, 384, 128), BF16),
            jax.ShapeDtypeStruct((27, 32, 128), F32),
            jax.ShapeDtypeStruct((1, 128), F32),
        ],
        in_specs=[any_spec] * 3 + [vmem_spec] * 3,
        out_specs=[any_spec] * 4,
        scratch_shapes=[
            v((384, 1024)),
            v((8, 384, 128)),
            v((16, 384, 128)),
            v((96, 128)),
            v((27, 128, 512)),
            v((2, 4, 48, 128)),
            v((8, 128), F32),
            v((4, 8, 128), F32),
            v((9, 32, 24, 128), F32),
            v((9, 33, 24, 128), F32),
            v((384, 512), F32),
            v((8, 96, 512)),
            v((16, 48, 512)),
            v((16, 48, 512)),
            v((2, 4, 48, 128)),
            v((8, 48, 128)),
            v((9, 96, 512)),
            v((8, 8, 128), F32),
            v((4, 8, 128), F32),
            v((16, 8, 128), F32),
            v((2, 9, 8, 24, 128), F32),
            v((16, 384, 128)),
            v((16, 384, 128)),
            v((16, 384, 128)),
            v((3, 2, 2, 9, 32, 512)),
            v((3, 2, 9, 32, 512)),
            v((3, 2, 9, 32, 512)),
            v((3, 4, 2, 9, 32, 128)),
            v((3, 9, 32, 128), F32),
            v((3, 9, 32, 128)),
            v((3, 9, 32, 128)),
            v((9, 32, 512)),
            v((9, 32, 512)),
            v((27, 32, 128), F32),
            v((1, 128), F32),
            sems(1), sems(8), sems(16), sems(16), sems(2),
            sems(16), sems(16), sems(8), sems(8), sems(4), sems(4),
            sems(16), sems(16), sems(8), sems(8), sems(14), sems(16), sems(8), sems(8),
            sems(8), sems(1), sems(16), sems(16), sems(16), sems(16), sems(16), sems(8),
            sems(3), sems(3), sems(12), sems(12), sems(3), sems(3), sems(4),
        ],
        compiler_params=pltpu.CompilerParams(
            collective_id=0, has_side_effects=True, vmem_limit_bytes=60 * 1024 * 1024
        ),
        cost_estimate=pl.CostEstimate(flops=10_000_000_000, bytes_accessed=8_000_000, transcendentals=50_000),
    )(x, w, cot, bias, gat, sca)
    samp, dx, dw, db = pl.pallas_call(
        finisher,
        out_shape=[
            jax.ShapeDtypeStruct((8, 48, 128), BF16),
            jax.ShapeDtypeStruct((384, 1024), BF16),
            jax.ShapeDtypeStruct((27, 32, 128), F32),
            jax.ShapeDtypeStruct((1, 128), F32),
        ],
        in_specs=[vmem_spec, any_spec, vmem_spec, vmem_spec],
        out_specs=[vmem_spec, any_spec, vmem_spec, vmem_spec],
        scratch_shapes=[v((8, 384, 128)), v((384, 1024)), sems(8), sems(8)],
        cost_estimate=pl.CostEstimate(flops=0, bytes_accessed=3_000_000, transcendentals=0),
    )(samp, dx, dw, db)
    sampled = samp.reshape(8, 2, 12, 2, 128).transpose(0, 1, 3, 2, 4)
    clip_grad = dx.reshape(1, 4, 4, 24, 1024)
    return sampled, clip_grad, dw.reshape(3, 3, 3, 32, 128), db.reshape(128)


def solution(mesh):
    return jax.shard_map(
        shards,
        mesh=mesh,
        in_specs=(
            P("dp", "tm", None, None, None),
            P(None, None, None, "tm", "dp"),
            P("dp"),
            P(None, "tm", None, None, "dp"),
        ),
        out_specs=(
            P(None, "tm", None, None, "dp"),
            P("dp", "tm", None, None, None),
            P(None, None, None, "tm", "dp"),
            P("dp"),
        ),
        check_vma=False,
    )
```

```python
import math

import jax
import jax.numpy as jnp
import numpy as np
from jax import lax
from jax.experimental import pallas as pl
from jax.experimental.pallas import tpu as pltpu
from jax.sharding import PartitionSpec as P

MESH = pl.DeviceIdType.MESH
F32 = jnp.float32
BF16 = jnp.bfloat16
POSITIONS = 12288


def tap_gather():
    table = np.zeros((224, 96), np.float32)
    for h in range(3):
        for w in range(3):
            for r in range(2):
                for q in range(12):
                    row, col = 2 * r + h - 1, 2 * q + w - 1
                    if 0 <= row < 4 and 0 <= col < 24:
                        table[(h * 3 + w) * 24 + q * 2 + r, row * 24 + col] = 1.0
    return table


def kernel(
    x_ref, w_ref, cot_ref, bias_ref, gat_ref, sca_ref,
    samp_out, dx_out, dw_out, db_out,
    xv, xp, land, halo, wg, cotl, biasb, biasl, im_e, im_o, pacc, part, rsl, rss, sbuf, sland, gbuf, bz, bs, bl,
    dtmp, dxb, dxp, dxs, dwb, dws, dwr, dwl, dwo, dwx, dwy, dwm, dwn, kout, dbo,
    v_sem, x_send, x_recv, f_send, h_sem, w_send, w_recv, c_send, c_recv, b_send, b_recv, rs_send, rs_recv,
    s_send, s_recv, ag_send, ag_recv, bz_send, bz_recv, gh_send, gh_recv, bs_send, bs_recv, dxp_send, dxp_recv,
    dx_send, dx_recv, k1_send, k1_recv, k2_send, k2_recv, k3_send, k3_recv, o_sem,
):
    dp, tm = lax.axis_index("dp"), lax.axis_index("tm")
    xl, y = lax.div(dp, 4), lax.rem(dp, 4)
    xh, z, c = lax.div(tm, 16), lax.rem(lax.div(tm, 2), 8), lax.rem(tm, 2)
    primary = c == xl
    inv = 1.0 / math.sqrt(POSITIONS)

    def dev(xl_, y_, xh_, z_, c_):
        return (xl_ * 4 + y_, (xh_ * 8 + z_) * 2 + c_)

    def remote(src, dst, send, recv, device):
        return pltpu.make_async_remote_copy(
            src_ref=src, dst_ref=dst, send_sem=send, recv_sem=recv, device_id=device, device_id_type=MESH
        )

    def landed(dst, sem):
        pltpu.make_async_copy(dst, dst, sem).wait()

    def plus(a, by, n):
        return lax.rem(a + by, n)

    partner = dev(1 - xl, y, xh, z, c)
    sibling = dev(xl, y, xh, z, 1 - c)
    across = dev(xl, y, 1 - xh, z, c)

    x_in = pltpu.make_async_copy(x_ref, xv, v_sem.at[0])
    x_in.start()

    barrier = pltpu.get_barrier_semaphore()
    peers = [partner]
    for dz in range(8):
        for dc in range(2):
            if dz or dc:
                peers.append(dev(xl, y, xh, plus(z, dz, 8), plus(c, dc, 2)))
    for dy in range(4):
        for dh in range(2):
            for dc in range(2):
                if dy or dh:
                    peers.append(dev(xl, plus(y, dy, 4), plus(xh, dh, 2), z, plus(c, dc, 2)))
    for dz in range(1, 8):
        peers.append(dev(xl, y, 1 - xh, plus(z, dz, 8), c))
    for peer in peers:
        pl.semaphore_signal(barrier, inc=1, device_id=peer, device_id_type=MESH)

    biasb[...] = jnp.broadcast_to(bias_ref[...], (8, 128))
    x_in.wait()
    for zt in range(8):
        at = (zt // 2) * 128 + (zt % 2) * 64
        xp[zt] = jnp.concatenate([xv[:, at:at + 64], xv[:, 512 + at:512 + at + 64]], axis=1)
    pl.semaphore_wait(barrier, len(peers))

    ends = []

    def w_at(h_, c_, y_):
        return wg.at[:, pl.ds(pl.multiple_of((h_ * 2 + c_) * 32, 32), 32), pl.ds(pl.multiple_of(y_ * 128, 128), 128)]

    def w_sem(h_, c_, y_):
        return w_recv.at[(h_ * 2 + c_) * 4 + y_]

    w_count = [0]

    def w_push(src, h_, c_, y_, device):
        copy = remote(src, w_at(h_, c_, y_), w_send.at[w_count[0]], w_sem(h_, c_, y_), device)
        w_count[0] += 1
        copy.start()
        ends.append(copy.wait_send)

    up, down = plus(y, 1, 4), plus(y, 3, 4)
    dev_up, dev_down = dev(xl, up, xh, z, c), dev(xl, down, xh, z, c)
    w_push(w_ref, xh, c, y, across)
    w_push(w_ref, xh, c, y, dev_up)
    w_push(w_ref, xh, c, y, dev_down)
    w_push(w_ref, xh, c, y, sibling)
    pltpu.make_async_copy(w_ref, w_at(xh, c, y), w_sem(xh, c, y)).start()

    me_k = 2 * z + c
    for n, dz in enumerate((4, 1, 7, 3, 5, 2, 6)):
        zt = plus(z, dz, 8)
        copy = remote(xp.at[zt], land.at[me_k], x_send.at[n], x_recv.at[me_k], dev(xl, y, xh, zt, xl))
        copy.start()
        ends.append(copy.wait_send)
    own_x = pltpu.make_async_copy(xp.at[z], land.at[me_k], x_recv.at[me_k])
    sib_x = remote(xp.at[z], land.at[me_k], x_send.at[7], x_recv.at[me_k], dev(xl, y, xh, z, 1 - c))

    @pl.when(primary)
    def _():
        own_x.start()

    @pl.when(jnp.logical_not(primary))
    def _():
        sib_x.start()

    for dy in range(4):
        for dc in range(2):
            yd, cd = plus(y, dy, 4), plus(c, dc, 2)
            src, dst, sem = cot_ref.at[cd * 4 + yd], cotl.at[c, y], c_recv.at[c * 4 + y]
            if dy or dc:
                copy = remote(src, dst, c_send.at[dy * 2 + dc], sem, dev(xl, yd, xh, z, cd))
                copy.start()
                ends.append(copy.wait_send)
            else:
                pltpu.make_async_copy(src, dst, sem).start()
    pltpu.make_async_copy(biasb, biasl.at[y], b_recv.at[y]).start()
    for dy in range(1, 4):
        copy = remote(biasb, biasl.at[y], b_send.at[dy], b_recv.at[y], dev(xl, plus(y, dy, 4), xh, z, c))
        copy.start()
        ends.append(copy.wait_send)

    halo_copy = remote(land.at[15, pl.ds(288, 96)], halo, h_sem.at[0], h_sem.at[1], across)
    ends.append(halo_copy.wait_send)

    def place_of(j):
        dz = 0
        dz = jnp.where(j == 1, 4, dz)
        dz = jnp.where(j == 2, 1, dz)
        dz = jnp.where(j == 3, 7, dz)
        dz = jnp.where(j == 4, 3, dz)
        dz = jnp.where(j == 5, 5, dz)
        dz = jnp.where(j == 6, 2, dz)
        dz = jnp.where(j == 7, 6, dz)
        return plus(z, dz, 8)

    def pass_on(first, last):
        @pl.when(primary)
        def _():
            def one(i, carry):
                k = 2 * place_of(lax.div(i, 2)) + lax.rem(i, 2)
                landed(land.at[k], x_recv.at[k])
                remote(land.at[k], land.at[k], f_send.at[k], x_recv.at[k], partner).start()
                return carry

            lax.fori_loop(2 * first, 2 * last, one, 0)

    def take_in(first, last):
        def one(i, carry):
            k = 2 * place_of(lax.div(i, 2)) + lax.rem(i, 2)

            @pl.when(jnp.logical_not(primary))
            def _():
                landed(land.at[k], x_recv.at[k])

            @pl.when(k == 15)
            def _():
                halo_copy.start()

            frames = land[k]
            side = jnp.concatenate([frames[i * 96:(i + 1) * 96] for i in range(4)], axis=1)
            taps = jnp.dot(gat_ref[...], side, preferred_element_type=F32)
            for f in range(4):
                piece = taps[:216, f * 128:(f + 1) * 128].reshape(9, 24, 128)
                if f % 2 == 0:
                    im_e[:, 2 * k + f // 2] = piece
                else:
                    im_o[:, 2 * k + 1 + f // 2] = piece
            return carry

        lax.fori_loop(2 * first, 2 * last, one, 0)

    def spread(first, last):
        pass_on(first, last)
        take_in(first, last)

    def w_pass(h_, y_, device):
        landed(w_at(h_, c, y_), w_sem(h_, c, y_))
        if device is not None:
            w_push(w_at(h_, c, y_), h_, c, y_, device)
        w_push(w_at(h_, c, y_), h_, c, y_, sibling)

    spread(0, 1)
    w_pass(1 - xh, y, dev_up)
    w_push(w_at(1 - xh, c, y), 1 - xh, c, y, dev_down)
    spread(1, 2)
    w_pass(xh, down, dev_up)
    w_pass(xh, up, None)
    spread(2, 4)
    w_pass(1 - xh, up, dev_down)
    w_pass(1 - xh, down, None)
    spread(4, 6)
    pass_on(6, 8)
    w_pass(xh, plus(y, 2, 4), None)
    w_pass(1 - xh, plus(y, 2, 4), None)
    landed(w_at(xh, c, y), w_sem(xh, c, y))
    for dy in range(4):
        for h_ in (xh, 1 - xh):
            yd = plus(y, dy, 4)
            landed(w_at(h_, 1 - c, yd), w_sem(h_, 1 - c, yd))

    def z_at(dz):
        return plus(z, dz % 8, 8)

    def forward(dzs):
        zts = [z_at(dz) for dz in dzs]
        size = 96 * len(zts)
        for zt in zts:
            @pl.when(zt == 0)
            def _():
                landed(halo, h_sem.at[1])
                rim = jnp.dot(gat_ref[...], halo[...], preferred_element_type=F32)[:216].reshape(9, 24, 128)
                im_o[:, 0] = jnp.where(xh == 1, rim, jnp.zeros_like(rim))

        def rows(held, hw, by):
            return jnp.concatenate([held[hw, pl.ds(4 * zt + by, 4)].reshape(96, 128) for zt in zts], axis=0).astype(BF16)

        def step(h, carry):
            lhs, rhs = [], []
            for w in range(3):
                hw = h * 3 + w
                lhs += [rows(im_o, hw, 0), rows(im_e, hw, 0), rows(im_o, hw, 1)]
                rhs += [wg[hw], wg[9 + hw], wg[18 + hw]]
            pacc[0:size] += jnp.dot(
                jnp.concatenate(lhs, axis=1), jnp.concatenate(rhs, axis=0), preferred_element_type=F32
            )
            return carry

        pacc[0:size] = jnp.zeros((size, 512), F32)
        lax.fori_loop(0, 3, step, 0)
        for q, dz in enumerate(dzs):
            zt = zts[q]
            part[zt] = pacc[q * 96:(q + 1) * 96].astype(BF16)

    next_z, last_z = dev(xl, y, xh, plus(z, 1, 8), c), dev(xl, y, xh, plus(z, 7, 8), c)

    def rs_hop(way, step, half):
        zt = z_at((5 - step) * (1 - 2 * way))
        at = (way * 4 + step - 1) * 2 + half
        own = part[zt, half * 48:(half + 1) * 48]
        if step > 1 and (step > 2 or half == way):
            before = at - 2
            landed(rsl.at[before], rs_recv.at[before])
            own = (own.astype(F32) + rsl[before].astype(F32)).astype(BF16)
        rss[at] = own
        copy = remote(rss.at[at], rsl.at[at], rs_send.at[at], rs_recv.at[at], last_z if way else next_z)
        copy.start()
        ends.append(copy.wait_send)

    def rs_step(step):
        for half in range(2):
            for way in range(2):
                if step > 1 or half == way:
                    rs_hop(way, step, half)

    forward((4, -3))
    rs_step(1)
    take_in(6, 8)
    forward((3, -2))
    rs_step(2)
    forward((2, -1, 1))
    rs_step(3)
    forward((0,))
    rs_step(4)

    for dy in range(4):
        yd = plus(y, dy, 4)
        landed(biasl.at[yd], b_recv.at[yd])
        for cs in range(2):
            landed(cotl.at[cs, yd], c_recv.at[cs * 4 + yd])
    pre = part[z].astype(F32)
    sums_in = []
    for way in range(2):
        for half in range(2):
            at = (way * 4 + 3) * 2 + half
            landed(rsl.at[at], rs_recv.at[at])
        sums_in.append(jnp.concatenate([rsl[way * 8 + 6], rsl[way * 8 + 7]], axis=0).astype(F32))
    pre = pre + sums_in[0] + sums_in[1]
    pre = pre + jnp.concatenate([biasl[i, 0:1] for i in range(4)], axis=1)
    sig = 1.0 / (1.0 + jnp.exp(-pre))
    samp = (pre * sig).astype(BF16)
    cot = jnp.concatenate(
        [jnp.concatenate([cotl[cs, i] for i in range(4)], axis=1) for cs in range(2)], axis=0
    ).astype(F32)
    slope = cot * sig * (1.0 + pre * (1.0 - sig))
    gbuf[z] = slope.astype(BF16)
    def g_at(o, half):
        return gbuf.at[o, pl.ds(half * 48, 48)]

    ag_count = [0]

    def ag_push(o, half, device):
        copy = remote(g_at(o, half), g_at(o, half), ag_send.at[ag_count[0]], ag_recv.at[o * 2 + half], device)
        ag_count[0] += 1
        copy.start()
        ends.append(copy.wait_send)

    for half in range(2):
        ag_push(z, half, next_z)
        ag_push(z, half, last_z)

    def rim_copy(zt):
        return remote(
            gbuf.at[0, pl.ds(0, 32)], gbuf.at[8, pl.ds(0, 32)], gh_send.at[zt], gh_recv.at[0], dev(xl, y, 0, zt, c)
        )

    gives_rim = jnp.logical_and(z == 0, xh == 1)

    @pl.when(gives_rim)
    def _():
        for zt in range(8):
            rim_copy(zt).start()

    @pl.when(xh == 1)
    def _():
        gbuf[8, pl.ds(0, 32)] = jnp.zeros((32, 512), BF16)

    sums = jnp.sum(slope, axis=0, keepdims=True)
    bz[z] = jnp.concatenate([sums[:, i * 128:(i + 1) * 128] for i in range(4)] + [jnp.zeros((4, 128), F32)], axis=0)
    for cs in range(2):
        for i in range(4):
            sbuf[cs, i] = samp[cs * 48:(cs + 1) * 48, i * 128:(i + 1) * 128]

    def late_sends():
        for n, dz in enumerate((1, 7, 2, 6, 3, 5, 4)):
            copy = remote(bz.at[z], bz.at[z], bz_send.at[n], bz_recv.at[z], dev(xl, y, xh, plus(z, dz, 8), c))
            copy.start()
            ends.append(copy.wait_send)
        for dy in range(4):
            for dc in range(2):
                yd, cd = plus(y, dy, 4), plus(c, dc, 2)
                src, dst, sem = sbuf.at[cd, yd], sland.at[c * 4 + y], s_recv.at[c * 4 + y]
                if dy or dc:
                    copy = remote(src, dst, s_send.at[dy * 2 + dc], sem, dev(xl, yd, xh, z, cd))
                    copy.start()
                    ends.append(copy.wait_send)
                else:
                    pltpu.make_async_copy(src, dst, sem).start()

    def back_pair(first, second):
        def back(h, carry):
            hws = [h * 3 + w for w in range(3)]
            mats = jnp.concatenate([wg[t * 9 + hw] for hw in hws for t in range(3)], axis=0)
            rows = jnp.concatenate(
                [gbuf[first], gbuf[first + 1, 0:32], gbuf[second], gbuf[second + 1, 0:32]], axis=0
            )
            r = lax.dot_general(rows, mats, (((1,), (1,)), ((), ())), preferred_element_type=F32)
            for w in range(3):
                at = w * 384
                for i in range(2):
                    p = r[i * 128:i * 128 + 128]
                    dtmp[i, h * 3 + w, 0:4] = p[:96, at + 128:at + 256].reshape(4, 24, 128)
                    dtmp[i, h * 3 + w, 4:8] = (p[:96, at + 256:at + 384] + p[24:120, at:at + 128]).reshape(4, 24, 128)
            return carry

        lax.fori_loop(0, 3, back, 0)

        def place(i, carry):
            zc = jnp.where(i == 0, first, second)
            cols = [dtmp[i, :, f + 4 * odd].reshape(216, 128) for f in range(4) for odd in range(2)]
            side = jnp.concatenate(cols, axis=1)
            side = jnp.concatenate([side, jnp.zeros((8, 1024), F32)], axis=0).astype(BF16)
            r = jnp.dot(sca_ref[...], side, preferred_element_type=F32).astype(BF16)
            for cs in range(2):
                k = 2 * zc + cs
                for f in range(4):
                    dxb[k, pl.ds(f * 96, 96)] = r[:, (cs * 4 + f) * 128:(cs * 4 + f + 1) * 128]

                @pl.when(jnp.logical_not(primary))
                def _(k=k):
                    remote(dxb.at[k], dxp.at[k], dxp_send.at[k], dxp_recv.at[k], partner).start()
            return carry

        lax.fori_loop(0, 2, place, 0)

    def send_back(k):
        landed(dxp.at[k], dxp_recv.at[k])
        dxs[k] = (dxb[k].astype(F32) + dxp[k].astype(F32)).astype(BF16)

        @pl.when(k == me_k)
        def _():
            pltpu.make_async_copy(dxs.at[k], dx_out.at[z], dx_recv.at[z]).start()

        @pl.when(k != me_k)
        def _():
            remote(
                dxs.at[k], dx_out.at[z], dx_send.at[k], dx_recv.at[z], dev(xl, y, xh, lax.div(k, 2), lax.rem(k, 2))
            ).start()

    def finish_pair(first, second):
        @pl.when(primary)
        def _():
            def one(i, carry):
                zc = jnp.where(i < 2, first, second)
                send_back(2 * zc + lax.rem(i, 2))
                return carry

            lax.fori_loop(0, 4, one, 0)

    for step in range(1, 4):
        below, above = z_at(-step), z_at(step)
        for half in range(2):
            landed(g_at(below, half), ag_recv.at[below * 2 + half])
            if step < 3 or half == 0:
                ag_push(below, half, next_z)
            landed(g_at(above, half), ag_recv.at[above * 2 + half])
            if step < 3 or half == 1:
                ag_push(above, half, last_z)
        if step == 1:
            @pl.when(xh == 0)
            def _():
                landed(gbuf.at[8, pl.ds(0, 32)], gh_recv.at[0])

        back_pair(z_at(step - 1), z_at(-step))
        if step == 1:
            late_sends()
        if step > 1:
            finish_pair(z_at(step - 2), z_at(1 - step))
    for half in range(2):
        landed(g_at(z_at(4), half), ag_recv.at[z_at(4) * 2 + half])

    def weight_grad(h):
        def grad_step(w, carry):
            hw = h * 3 + w
            lhs = jnp.concatenate(
                [
                    im_o[hw, pl.ds(0, 32)].reshape(768, 128).astype(BF16),
                    im_e[hw].reshape(768, 128).astype(BF16),
                    im_o[hw, pl.ds(1, 32)].reshape(768, 128).astype(BF16),
                ],
                axis=1,
            )
            r = lax.dot_general(
                lhs, gbuf[0:8].reshape(768, 512), (((0,), (0,)), ((), ())), preferred_element_type=F32
            ).astype(BF16)
            for t in range(3):
                for h_ in range(2):
                    for c_ in range(2):
                        at = t * 128 + h_ * 64 + c_ * 32
                        dwb[h, c_, h_, w * 3 + t] = r[at:at + 32]
            return carry

        lax.fori_loop(0, 3, grad_step, 0)
        copy = remote(dwb.at[h, 1 - c], dws.at[h], k1_send.at[h], k1_recv.at[h], sibling)
        copy.start()
        ends.append(copy.wait_send)

    def core_sum(h):
        landed(dws.at[h], k1_recv.at[h])

        def add_step(n, carry):
            for h_ in range(2):
                dwr[h, h_, n] = (dwb[h, c, h_, n].astype(F32) + dws[h, h_, n].astype(F32)).astype(BF16)
            return carry

        lax.fori_loop(0, 9, add_step, 0)

    def y_lanes(i):
        return pl.ds(pl.multiple_of(i * 128, 128), 128)

    def to_y(h):
        core_sum(h)
        for dy in range(4):
            yd = plus(y, dy, 4)
            src = dwr.at[h, :, :, :, y_lanes(yd)]
            dst, sem = dwl.at[h, y], k2_recv.at[h * 4 + y]
            if dy:
                copy = remote(src, dst, k2_send.at[h * 4 + dy], sem, dev(xl, yd, xh, z, c))
                copy.start()
                ends.append(copy.wait_send)
            else:
                pltpu.make_async_copy(src, dst, sem).start()

    def y_to_x(h):
        for i in range(4):
            landed(dwl.at[h, i], k2_recv.at[h * 4 + i])

        def add_step(n, carry):
            own, other = dwl[h, 0, xh, n].astype(F32), dwl[h, 0, 1 - xh, n].astype(F32)
            for i in range(1, 4):
                own = own + dwl[h, i, xh, n].astype(F32)
                other = other + dwl[h, i, 1 - xh, n].astype(F32)
            dwo[h, n] = own
            dwx[h, n] = other.astype(BF16)
            return carry

        lax.fori_loop(0, 9, add_step, 0)
        copy = remote(dwx.at[h], dwy.at[h], k3_send.at[h], k3_recv.at[h], across)
        copy.start()
        ends.append(copy.wait_send)

    def to_x(h):
        core_sum(h)
        copy = remote(dwr.at[h, 1 - xh], dwm, k3_send.at[h], k3_recv.at[h], across)
        copy.start()
        ends.append(copy.wait_send)

    def x_to_y(h):
        landed(dwm, k3_recv.at[h])

        def add_step(n, carry):
            dwn[n] = (dwr[h, xh, n].astype(F32) + dwm[n].astype(F32)).astype(BF16)
            return carry

        lax.fori_loop(0, 9, add_step, 0)
        for dy in range(4):
            yd = plus(y, dy, 4)
            src = dwn.at[:, :, y_lanes(yd)]
            dst, sem = dwl.at[h, y, 0], k2_recv.at[h * 4 + y]
            if dy:
                copy = remote(src, dst, k2_send.at[h * 4 + dy], sem, dev(xl, yd, xh, z, c))
                copy.start()
                ends.append(copy.wait_send)
            else:
                pltpu.make_async_copy(src, dst, sem).start()

    weight_grad(0)
    back_pair(z_at(3), z_at(4))
    to_y(0)
    finish_pair(z_at(2), z_at(-3))
    weight_grad(1)
    weight_grad(2)
    finish_pair(z_at(3), z_at(4))
    to_x(1)
    to_y(2)
    y_to_x(0)
    x_to_y(1)

    total = bz[z]
    for dz in (1, 7, 2, 6, 3, 5, 4):
        zs = plus(z, dz, 8)
        landed(bz.at[zs], bz_recv.at[zs])
        total = total + bz[zs]
    for i in range(4):
        bs[i] = jnp.broadcast_to(total[i:i + 1], (8, 128))
    slot_b = (xh * 2 + c) * 4 + y
    for dy in range(4):
        for dh in range(2):
            for dc in range(2):
                yd, hd, cd = plus(y, dy, 4), plus(xh, dh, 2), plus(c, dc, 2)
                if dy or dh or dc:
                    copy = remote(
                        bs.at[yd], bl.at[slot_b], bs_send.at[(dy * 2 + dh) * 2 + dc], bs_recv.at[slot_b],
                        dev(xl, yd, hd, z, cd),
                    )
                    copy.start()
                    ends.append(copy.wait_send)
                else:
                    pltpu.make_async_copy(bs.at[y], bl.at[slot_b], bs_recv.at[slot_b]).start()

    outs = []
    for i in range(8):
        landed(sland.at[i], s_recv.at[i])
    outs.append(pltpu.make_async_copy(sland, samp_out, o_sem.at[0]))
    outs[-1].start()

    y_to_x(2)
    for i in range(4):
        landed(dwl.at[1, i, 0], k2_recv.at[4 + i])

    def sum_middle(w, carry):
        for t in range(3):
            acc = dwl[1, 0, 0, w * 3 + t].astype(F32)
            for i in range(1, 4):
                acc = acc + dwl[1, i, 0, w * 3 + t].astype(F32)
            kout[t * 9 + 3 + w] = acc * inv
        return carry

    lax.fori_loop(0, 3, sum_middle, 0)
    for h in (0, 2):
        landed(dwy.at[h], k3_recv.at[h])

        def sum_step(w, carry, h=h):
            for t in range(3):
                kout[t * 9 + h * 3 + w] = (dwo[h, w * 3 + t] + dwy[h, w * 3 + t].astype(F32)) * inv
            return carry

        lax.fori_loop(0, 3, sum_step, 0)
    outs.append(pltpu.make_async_copy(kout, dw_out, o_sem.at[1]))
    outs[-1].start()

    acc = None
    for i in range(16):
        landed(bl.at[i], bs_recv.at[i])
        acc = bl[i] if acc is None else acc + bl[i]
    dbo[...] = acc[0:1] * inv
    outs.append(pltpu.make_async_copy(dbo, db_out, o_sem.at[2]))
    outs[-1].start()

    for i in range(8):
        landed(dx_out.at[i], dx_recv.at[i])

    for end in ends:
        end()

    @pl.when(jnp.logical_not(primary))
    def _():
        sib_x.wait_send()

        def drain(k, carry):
            remote(dxb.at[k], dxp.at[k], dxp_send.at[k], dxp_recv.at[k], partner).wait_send()
            return carry

        lax.fori_loop(0, 16, drain, 0)

    @pl.when(primary)
    def _():
        def drain(k, carry):
            remote(land.at[k], land.at[k], f_send.at[k], x_recv.at[k], partner).wait_send()

            @pl.when(k != me_k)
            def _():
                remote(
                    dxs.at[k], dx_out.at[z], dx_send.at[k], dx_recv.at[z],
                    dev(xl, y, xh, lax.div(k, 2), lax.rem(k, 2)),
                ).wait_send()

            return carry

        lax.fori_loop(0, 16, drain, 0)

    @pl.when(gives_rim)
    def _():
        for zt in range(8):
            rim_copy(zt).wait_send()

    for out in outs:
        out.wait()


def finisher(samp_in, dx_in, dw_in, db_in, samp_out, dx_out, dw_out, db_out, held, made, in_sem, out_sem):
    loads = [pltpu.make_async_copy(dx_in.at[i], held.at[i], in_sem.at[i]) for i in range(8)]
    for copy in loads:
        copy.start()
    samp_out[...] = samp_in[...]
    dw_out[...] = dw_in[...]
    db_out[...] = db_in[...]
    stores = []
    for m in range(4):
        loads[2 * m].wait()
        loads[2 * m + 1].wait()
        a, b = held[2 * m], held[2 * m + 1]
        for half in range(2):
            cols = pl.ds(half * 512 + m * 128, 128)
            made[:, cols] = jnp.concatenate(
                [a[:, half * 64:half * 64 + 64], b[:, half * 64:half * 64 + 64]], axis=1
            )
            copy = pltpu.make_async_copy(made.at[:, cols], dx_out.at[:, cols], out_sem.at[2 * m + half])
            copy.start()
            stores.append(copy)
    for copy in stores:
        copy.wait()


def shards(video_clips, weights, conv_bias, cotangent):
    x = video_clips.reshape(384, 1024)
    w = weights.reshape(27, 32, 128)
    cot = cotangent.transpose(0, 1, 3, 2, 4).reshape(8, 48, 128)
    bias = conv_bias.reshape(1, 128)
    table = tap_gather()
    gat = jnp.asarray(table, BF16)
    sca = jnp.asarray(table.T, BF16)
    any_spec = pl.BlockSpec(memory_space=pl.ANY)
    vmem_spec = pl.BlockSpec(memory_space=pltpu.VMEM)

    def v(shape, dtype=BF16):
        return pltpu.VMEM(shape, dtype)

    def sems(n):
        return pltpu.SemaphoreType.DMA((n,))

    samp, dx, dw, db = pl.pallas_call(
        kernel,
        out_shape=[
            jax.ShapeDtypeStruct((8, 48, 128), BF16),
            jax.ShapeDtypeStruct((8, 384, 128), BF16),
            jax.ShapeDtypeStruct((27, 32, 128), F32),
            jax.ShapeDtypeStruct((1, 128), F32),
        ],
        in_specs=[any_spec] * 3 + [vmem_spec] * 3,
        out_specs=[any_spec] * 4,
        scratch_shapes=[
            v((384, 1024)),
            v((8, 384, 128)),
            v((16, 384, 128)),
            v((96, 128)),
            v((27, 128, 512)),
            v((2, 4, 48, 128)),
            v((8, 128), F32),
            v((4, 8, 128), F32),
            v((9, 32, 24, 128), F32),
            v((9, 33, 24, 128), F32),
            v((384, 512), F32),
            v((8, 96, 512)),
            v((16, 48, 512)),
            v((16, 48, 512)),
            v((2, 4, 48, 128)),
            v((8, 48, 128)),
            v((9, 96, 512)),
            v((8, 8, 128), F32),
            v((4, 8, 128), F32),
            v((16, 8, 128), F32),
            v((2, 9, 8, 24, 128), F32),
            v((16, 384, 128)),
            v((16, 384, 128)),
            v((16, 384, 128)),
            v((3, 2, 2, 9, 32, 512)),
            v((3, 2, 9, 32, 512)),
            v((3, 2, 9, 32, 512)),
            v((3, 4, 2, 9, 32, 128)),
            v((3, 9, 32, 128), F32),
            v((3, 9, 32, 128)),
            v((3, 9, 32, 128)),
            v((9, 32, 512)),
            v((9, 32, 512)),
            v((27, 32, 128), F32),
            v((1, 128), F32),
            sems(1), sems(8), sems(16), sems(16), sems(2),
            sems(16), sems(16), sems(8), sems(8), sems(4), sems(4),
            sems(16), sems(16), sems(8), sems(8), sems(14), sems(16), sems(8), sems(8),
            sems(8), sems(1), sems(16), sems(16), sems(16), sems(16), sems(16), sems(8),
            sems(3), sems(3), sems(12), sems(12), sems(3), sems(3), sems(4),
        ],
        compiler_params=pltpu.CompilerParams(
            collective_id=0, has_side_effects=True, vmem_limit_bytes=60 * 1024 * 1024
        ),
        cost_estimate=pl.CostEstimate(flops=10_000_000_000, bytes_accessed=8_000_000, transcendentals=50_000),
    )(x, w, cot, bias, gat, sca)
    samp, dx, dw, db = pl.pallas_call(
        finisher,
        out_shape=[
            jax.ShapeDtypeStruct((8, 48, 128), BF16),
            jax.ShapeDtypeStruct((384, 1024), BF16),
            jax.ShapeDtypeStruct((27, 32, 128), F32),
            jax.ShapeDtypeStruct((1, 128), F32),
        ],
        in_specs=[vmem_spec, any_spec, vmem_spec, vmem_spec],
        out_specs=[vmem_spec, any_spec, vmem_spec, vmem_spec],
        scratch_shapes=[v((8, 384, 128)), v((384, 1024)), sems(8), sems(8)],
        cost_estimate=pl.CostEstimate(flops=0, bytes_accessed=3_000_000, transcendentals=0),
    )(samp, dx, dw, db)
    sampled = samp.reshape(8, 2, 12, 2, 128).transpose(0, 1, 3, 2, 4)
    clip_grad = dx.reshape(1, 4, 4, 24, 1024)
    return sampled, clip_grad, dw.reshape(3, 3, 3, 32, 128), db.reshape(128)


def solution(mesh):
    return jax.shard_map(
        shards,
        mesh=mesh,
        in_specs=(
            P("dp", "tm", None, None, None),
            P(None, None, None, "tm", "dp"),
            P("dp"),
            P(None, "tm", None, None, "dp"),
        ),
        out_specs=(
            P(None, "tm", None, None, "dp"),
            P("dp", "tm", None, None, None),
            P(None, None, None, "tm", "dp"),
            P("dp"),
        ),
        check_vma=False,
    )
```
